128 devices in a mesh: gx: 16 (over y, x), gy: 8 (over z, core).
Axes of the slice: x: 4, y: 4, z: 4, core: 2. Of those that a mesh axis runs over, the one named last changes fastest.
Arguments:
- right_side: float32 [256, 128, 512], P('gx', 'gy'), may hold values from -12 to 12
- coefficient: float32 [256, 128, 512], P('gx', 'gy'), may hold values from 0.25 to 4
Outputs:
- solution: float32 [256, 128, 512], P('gx', 'gy')
- residual: float32 [256, 128, 512], P('gx', 'gy')
The draws below stay inside these ranges and needn't reach their ends.
All inputs are finite; a program needn't handle non-finite values.
Results may differ from the reference program's by a relative error of at most 0.0003.
Values sent between devices are 32-bit elements; how exact they have to be, the bound alone decides.
No kernel may reach another device: no remote copies, remote signals or barrier semaphores. Data moves between devices by JAX's collectives and lax.ppermute only.
A program may use at most 128 MiB of HBM per device.

```python
import math
import jax
import jax.numpy as jnp

LEVELS = 5
NU = 2
BOTTOM = 16
NX = 256
NY = 128
NZ = 512


def draw_right_side(key, part):
    key = jax.random.fold_in(key, 11)
    key_rough = jax.random.fold_in(key, 0)
    rough_part = jax.random.normal(key_rough, (NX, NY, NZ), jnp.float32)
    return jnp.clip(rough_part, -4.0, 4.0)


def block_scale(own_key, dims, cuts, low, largest):
    gain = 1.0
    for position, blocks in cuts:
        steps = jax.random.uniform(jax.random.fold_in(jax.random.fold_in(own_key, 6), position), (blocks,), jnp.float32, low / len(cuts), largest / len(cuts))
        gain = gain * jnp.repeat(jnp.exp(steps), dims[position] // blocks).reshape((-1,) + (1,) * (len(dims) - 1 - position))
    return gain


def setup_inputs(seed: int = 0) -> dict:
    key_of = jax.random.split(jax.random.key(seed), 3)
    right_side = draw_right_side(jax.random.fold_in(key_of[2], 71), 0)
    coefficient = jnp.clip(jnp.exp(math.log(4.0) - 2.7725887 * jax.random.uniform(key_of[1], (NX, NY, NZ), jnp.float32) ** block_scale(key_of[1], (NX, NY, NZ), ((0, 16), (1, 8)), -0.2, 0.2)), 0.25, 4.0)
    return {"right_side": right_side, "coefficient": coefficient}


OMEGA = 0.8


def face_weights(padded):
    centre = padded[1:-1, 1:-1, 1:-1]
    return (0.5 * (centre + padded[:-2, 1:-1, 1:-1]), 0.5 * (centre + padded[2:, 1:-1, 1:-1]),
            0.5 * (centre + padded[1:-1, :-2, 1:-1]), 0.5 * (centre + padded[1:-1, 2:, 1:-1]),
            0.5 * (centre + padded[1:-1, 1:-1, :-2]), 0.5 * (centre + padded[1:-1, 1:-1, 2:]))


def stencil(padded, weights, inv_h2):
    centre = padded[1:-1, 1:-1, 1:-1]
    summed = weights[0] * (centre - padded[:-2, 1:-1, 1:-1]) + weights[1] * (centre - padded[2:, 1:-1, 1:-1])
    summed = summed + weights[2] * (centre - padded[1:-1, :-2, 1:-1]) + weights[3] * (centre - padded[1:-1, 2:, 1:-1])
    summed = summed + weights[4] * (centre - padded[1:-1, 1:-1, :-2]) + weights[5] * (centre - padded[1:-1, 1:-1, 2:])
    return summed * inv_h2


def diagonal_of(weights, inv_h2):
    return (weights[0] + weights[1] + weights[2] + weights[3] + weights[4] + weights[5]) * inv_h2


def coarsen(array_in):
    extent_x, extent_y, extent_z = array_in.shape
    return array_in.reshape(extent_x // 2, 2, extent_y // 2, 2, extent_z // 2, 2).mean(axis=(1, 3, 5))


def refine(array_in):
    extent_x, extent_y, extent_z = array_in.shape
    spread = jnp.broadcast_to(array_in[:, None, :, None, :, None], (extent_x, 2, extent_y, 2, extent_z, 2))
    return spread.reshape(2 * extent_x, 2 * extent_y, 2 * extent_z)


def reference(right_side, coefficient):
    coef_levels = [coefficient]
    for level_index in range(1, LEVELS):
        coef_levels.append(coarsen(coef_levels[-1]))
    level_sets = []
    for level_index in range(LEVELS):
        inv_h2 = 1.0 / 4.0 ** level_index
        weights = face_weights(jnp.pad(coef_levels[level_index], 1))
        level_sets.append((weights, inv_h2, diagonal_of(weights, inv_h2)))

    def apply_level(iterate, level_index):
        weights, inv_h2, diagonal_vals = level_sets[level_index]
        return stencil(jnp.pad(iterate, 1), weights, inv_h2)

    def jacobi_step(iterate, source, level_index):
        return iterate + OMEGA * (source - apply_level(iterate, level_index)) / level_sets[level_index][2]

    def vcycle_at(source, level_index):
        iterate = jnp.zeros_like(source)
        if level_index == LEVELS - 1:
            for repeat in range(BOTTOM):
                iterate = jacobi_step(iterate, source, level_index)
            return iterate
        for repeat in range(NU):
            iterate = jacobi_step(iterate, source, level_index)
        leftover = source - apply_level(iterate, level_index)
        iterate = iterate + refine(vcycle_at(coarsen(leftover), level_index + 1))
        for repeat in range(NU):
            iterate = jacobi_step(iterate, source, level_index)
        return iterate

    solution = vcycle_at(right_side, 0)
    return solution, right_side - apply_level(solution, 0)
```

```python
import functools

import jax
import jax.numpy as jnp
from jax import lax
from jax.experimental import pallas as pl
from jax.experimental.pallas import tpu as pltpu
from jax.sharding import PartitionSpec as P

F32 = jnp.float32
BF16 = jnp.bfloat16
OMEGA = 0.8
BOTTOM = 16
VMEM_LIMIT = 56 * 1024 * 1024

X0, Y0, Z0, OX0, OY0 = 22, 24, 512, 3, 4
X1, Y1, Z1, OX1, OY1 = 24, 24, 256, 8, 8
X2, Y2, Z2, OX2, OY2 = 12, 16, 128, 4, 4
Y3, Y4, LANES = 16, 8, 128


def iota(shape, dim):
    return lax.broadcasted_iota(jnp.int32, shape, dim)


def up_of(cells, dim):
    return pltpu.roll(cells, cells.shape[dim] - 1, dim)


def down_of(cells, dim):
    return pltpu.roll(cells, 1, dim)


def split_dot(cells, pick):
    high = cells.astype(BF16)
    rest = cells - high.astype(F32)
    mid = rest.astype(BF16)
    low = (rest - mid.astype(F32)).astype(BF16)
    dot = functools.partial(jnp.dot, preferred_element_type=F32)
    return dot(high, pick) + (dot(mid, pick) + dot(low, pick))


def split_dot_left(pick, cells):
    high = cells.astype(BF16)
    rest = cells - high.astype(F32)
    mid = rest.astype(BF16)
    low = (rest - mid.astype(F32)).astype(BF16)
    dot = functools.partial(jnp.dot, preferred_element_type=F32)
    return dot(pick, high) + (dot(pick, mid) + dot(pick, low))


def pair_sum_matrix(fine, coarse, offset=0):
    hit = (iota((fine, coarse), 0) // 2) + offset == iota((fine, coarse), 1)
    return hit.astype(F32).astype(BF16)


def copy_matrix(coarse, fine):
    hit = iota((coarse, fine), 0) == iota((coarse, fine), 1) // 2
    return hit.astype(F32).astype(BF16)


def inside(shape, dim, start, count):
    place = iota(shape, dim) + start
    return jnp.logical_and(place >= 0, place < count)


def flag(start, count):
    return jnp.where(jnp.logical_and(start >= 0, start < count), 1.0, 0.0).astype(F32)


def loop(first, last, body):
    def step(i, carry):
        body(i)
        return carry

    lax.fori_loop(first, last, step, 0)


def make_faces(c, wx, wy, wz, d, q, first, last, in_x, in_y, whole_y=0):
    rows, cells = c.shape[1], c.shape[2]
    end_z = iota((rows, cells), 1) == cells - 1
    start_z = iota((rows, cells), 1) == 0
    row = iota((rows, cells), 0)
    wx[first - 1] = 0.5 * (c[first - 1] + c[first])

    def body(i):
        here = c[i]
        after = c[i + 1]
        before = c[i - 1]
        y_up, y_down = up_of(here, 0), down_of(here, 0)
        if whole_y:
            y_up = jnp.where(row == rows - 1, 0.0, y_up)
            y_down = jnp.where(row == 0, 0.0, y_down)
        z_up = jnp.where(end_z, 0.0, up_of(here, 1))
        z_down = jnp.where(start_z, 0.0, down_of(here, 1))
        wx[i] = 0.5 * (here + after)
        side = 0.5 * (here + y_up)
        wy[i] = jnp.where(row == rows - 1, 0.0, side) if whole_y else side
        wz[i] = jnp.where(end_z, 0.0, 0.5 * (here + z_up))
        total = 3.0 * here + 0.5 * ((after + before) + (y_up + y_down) + (z_up + z_down))
        d[i] = total
        q[i] = (in_y * (OMEGA * in_x(i))) / jnp.maximum(total, 1e-30)

    loop(first, last, body)


def neighbours(v, wx, wy, wz, i):
    here = v[i]
    side_y, side_z = wy[i], wz[i]
    along_x = wx[i] * v[i + 1] + wx[i - 1] * v[i - 1]
    along_y = side_y * up_of(here, 0) + down_of(side_y * here, 0)
    along_z = side_z * up_of(here, 1) + down_of(side_z * here, 1)
    return here, along_x + along_y + along_z


def sweep(v, out, b, wx, wy, wz, q, first, last):
    def body(i):
        here, total = neighbours(v, wx, wy, wz, i)
        out[i] = (0.2 * here + b[i]) + q[i] * total

    loop(first, last, body)


def defect(v, source, wx, wy, wz, d, i):
    here, total = neighbours(v, wx, wy, wz, i)
    return (source[i] - d[i] * here) + total


def lanes(cells, k):
    return cells[:, LANES * k : LANES * k + LANES]


def keep(scratch, j, cells):
    for k in range(cells.shape[1] // LANES):
        scratch[j, k] = lanes(cells, k)


def halve_rows(scratch, j, start, count):
    parts = [
        scratch[j, k, pl.ds(start, count, stride=2), :] + scratch[j, k, pl.ds(start + 1, count, stride=2), :]
        for k in range(scratch.shape[1])
    ]
    return jnp.concatenate(parts, axis=1)


def double_rows(scratch, cells, start):
    for k in range(scratch.shape[0]):
        for odd in range(2):
            scratch[k, pl.ds(start + odd, cells.shape[0], stride=2), :] = lanes(cells, k)
    return jnp.concatenate([scratch[k] for k in range(scratch.shape[0])], axis=1)


def call(kernel, out_shape, scratch, in_specs=None, out_specs=None, flops=1000000, bytes_accessed=1000000):
    extra = {}
    if in_specs is not None:
        extra["in_specs"] = in_specs
    if out_specs is not None:
        extra["out_specs"] = out_specs
    return pl.pallas_call(
        kernel,
        out_shape=out_shape,
        scratch_shapes=scratch,
        compiler_params=pltpu.CompilerParams(vmem_limit_bytes=VMEM_LIMIT),
        cost_estimate=pl.CostEstimate(flops=flops, bytes_accessed=bytes_accessed, transcendentals=0),
        **extra,
    )


def struct(*shape):
    return jax.ShapeDtypeStruct(shape, F32)


def vmem(*shape):
    return pltpu.VMEM(shape, F32)


def coarsen_kernel(c_ref, out_ref, pairs):
    for i in range(8):
        keep(pairs, i, c_ref[2 * i] + c_ref[2 * i + 1])
    rows = jnp.concatenate([halve_rows(pairs, i, 0, 8) for i in range(8)], axis=0)
    out_ref[...] = (0.125 * split_dot(rows, pair_sum_matrix(Z0, Z1))).reshape(8, 8, Z1)


def coarsen_own(coefficient):
    return call(coarsen_kernel, struct(8, 8, Z1), [vmem(8, Z0 // LANES, 16, LANES)])(coefficient)


def edge_kernel(count_x, c_ref, g_ref, low_ref, high_ref, top_ref, bottom_ref):
    place = lax.axis_index("gx")
    first = jnp.where(place > 0, 1.0, 0.0).astype(F32)
    last = jnp.where(place < count_x - 1, 1.0, 0.0).astype(F32)
    row = iota((8, Z0), 0)

    def put(i, c, g):
        top_ref[i] = jnp.where(row < 4, pltpu.roll(c[8:16], 4, 0), g[8:16])
        bottom_ref[i] = jnp.where(row < 4, g[0:8], pltpu.roll(c[0:8], 4, 0))

    nothing = jnp.zeros((16, Z0), F32)
    for i in range(3):
        put(i, low_ref[i] * first, low_ref[i + 2] * first if i > 0 else nothing)
        put(19 + i, high_ref[i] * last, high_ref[i + 3] * last if i < 2 else nothing)

    def body(i):
        put(i + 3, c_ref[i], g_ref[i])

    loop(0, 16, body)


def edges_y(coefficient, right_side, low, high, count_x):
    return call(
        functools.partial(edge_kernel, count_x), [struct(X0, 8, Z0), struct(X0, 8, Z0)], []
    )(coefficient, right_side, low, high)


def down0_kernel(
    count_x, count_y,
    c_ref, g_ref, low_ref, high_ref, below_ref, above_ref,
    g1_ref, v_low_ref, v_high_ref, v_own_ref, *rest,
):
    stored, (c, g, wx, wy, wz, d, q, b, v, pairs, sems) = rest[:6], rest[6:]
    place_x, place_y = lax.axis_index("gx"), lax.axis_index("gy")
    first = jnp.where(place_x > 0, 1.0, 0.0).astype(F32)
    last = jnp.where(place_x < count_x - 1, 1.0, 0.0).astype(F32)
    low_y = jnp.where(place_y > 0, 1.0, 0.0).astype(F32)
    high_y = jnp.where(place_y < count_y - 1, 1.0, 0.0).astype(F32)
    row = iota((8, Z0), 0) < 4

    def put(frame, i, own, below, above):
        head, tail = pltpu.roll(own[0:8], 4, 0), pltpu.roll(own[8:16], 4, 0)
        frame[i, 0:8] = jnp.where(row, below, head)
        frame[i, 8:16] = jnp.where(row, head, tail)
        frame[i, 16:24] = jnp.where(row, tail, above)

    def put_both(i, own_c, own_g):
        below, above = below_ref[i] * low_y, above_ref[i] * high_y
        put(c, i, own_c, below, above)
        put(g, i, own_g, pltpu.roll(below, 4, 0), pltpu.roll(above, 4, 0))

    nothing = jnp.zeros((16, Z0), F32)
    for i in range(3):
        put_both(i, low_ref[i] * first, low_ref[i + 2] * first if i > 0 else nothing)
        put_both(19 + i, high_ref[i] * last, high_ref[i + 3] * last if i < 2 else nothing)

    def body(i):
        put_both(i + 3, c_ref[i], g_ref[i])

    loop(0, 16, body)

    in_y = inside((Y0, Z0), 0, place_y * 16 - OY0, 16 * count_y).astype(F32)
    make_faces(
        c, wx, wy, wz, d, q, 1, X0 - 1, lambda i: flag(place_x * 16 - OX0 + i, 16 * count_x), in_y
    )

    def begin(i):
        b[i] = q[i] * g[i]

    loop(1, X0 - 1, begin)
    copies = [
        pltpu.make_async_copy(here, there, sems.at[k])
        for k, (here, there) in enumerate(zip((wx, wy, wz, d, q, b), stored))
    ]
    for copy in copies:
        copy.start()
    sweep(b, v, b, wx, wy, wz, q, 2, X0 - 2)

    def own_of(i):
        own = pltpu.roll(v[i + 3], Y0 - OY0, 0)[0:16]
        v_own_ref[i] = own

    loop(0, 16, own_of)
    for i in range(3):
        v_high_ref[i] = v_own_ref[13 + i]
        v_low_ref[i] = v_own_ref[i]

    def restrict(j):
        i = 2 * j + OX0
        keep(pairs, j, defect(v, g, wx, wy, wz, d, i) + defect(v, g, wx, wy, wz, d, i + 1))

    loop(0, 8, restrict)
    rows = jnp.concatenate([halve_rows(pairs, i, 4, 8) for i in range(8)], axis=0)
    g1_ref[...] = (0.5 * split_dot(rows, pair_sum_matrix(Z0, Z1))).reshape(8, 8, Z1)
    for copy in copies:
        copy.wait()


def down0(count_x, count_y, *operands):
    frame = (X0, Y0, Z0)
    any_space = pl.BlockSpec(memory_space=pl.ANY)
    whole = pl.BlockSpec(memory_space=pltpu.VMEM)
    return call(
        functools.partial(down0_kernel, count_x, count_y),
        [struct(8, 8, Z1), struct(3, 16, Z0), struct(3, 16, Z0), struct(16, 16, Z0)] + [struct(*frame)] * 6,
        [vmem(*frame)] * 9 + [vmem(8, Z0 // LANES, Y0, LANES), pltpu.SemaphoreType.DMA((6,))],
        in_specs=[whole] * 6,
        out_specs=[whole] * 4 + [any_space] * 6,
    )(*operands)


def prepare_kernel(
    count_x, count_y, mid_ref, below_ref, above_ref,
    wx1, wy1, wz1, d1, q1, wx2, wy2, wz2, d2, q2, c3_ref, c1, c2, pairs,
):
    place_x, place_y = lax.axis_index("gx"), lax.axis_index("gy")
    low_y = jnp.where(place_y > 0, 1.0, 0.0).astype(F32)
    high_y = jnp.where(place_y < count_y - 1, 1.0, 0.0).astype(F32)
    c1[:, 0:8, :] = below_ref[...] * low_y
    c1[:, 8:16, :] = mid_ref[...]
    c1[:, 16:24, :] = above_ref[...] * high_y
    in_y = inside((Y1, Z1), 0, place_y * 8 - OY1, 8 * count_y).astype(F32)
    make_faces(
        c1, wx1, wy1, wz1, d1, q1, 2, X1 - 2, lambda i: flag(place_x * 8 - OX1 + i, 8 * count_x), in_y
    )
    for i in range(12):
        keep(pairs, i, c1[2 * i] + c1[2 * i + 1])
    blank = jnp.zeros((4, Z1), F32)
    rows = []
    for i in range(12):
        rows.append(halve_rows(pairs, i, 0, 12))
        rows.append(blank)
    c2[...] = (0.125 * split_dot(jnp.concatenate(rows, axis=0), pair_sum_matrix(Z1, Z2))).reshape(X2, Y2, Z2)
    in_y = inside((Y2, Z2), 0, place_y * 4 - OY2, 4 * count_y).astype(F32)
    make_faces(
        c2, wx2, wy2, wz2, d2, q2, 1, X2 - 1, lambda i: flag(place_x * 4 - OX2 + i, 4 * count_x), in_y
    )
    rows = jnp.concatenate([c2[4] + c2[5], c2[6] + c2[7]], axis=0)
    thin = 0.125 * split_dot(rows, pair_sum_matrix(Z2, LANES, 64))
    row = iota((8, LANES), 0)
    c3 = jnp.zeros((8, LANES), F32)
    for i in range(2):
        for j in range(2):
            at = 16 * i + 4 + 2 * j
            both = thin[at : at + 1] + thin[at + 1 : at + 2]
            c3 = jnp.where(row == 2 * i + j, jnp.broadcast_to(both, (8, LANES)), c3)
    c3_ref[...] = c3


def prepare(count_x, count_y, *operands):
    frame1, frame2 = (X1, Y1, Z1), (X2, Y2, Z2)
    return call(
        functools.partial(prepare_kernel, count_x, count_y),
        [struct(*frame1)] * 5 + [struct(*frame2)] * 5 + [struct(8, LANES)],
        [vmem(*frame1), vmem(*frame2), vmem(12, Z1 // LANES, Y1, LANES)],
    )(*operands)


def down1_kernel(
    count_x, count_y, mid_ref, below_ref, above_ref,
    wx1, wy1, wz1, d1, q1, wx2, wy2, wz2, d2, q2, c3_ref,
    v1_ref, b1_ref, send2_ref, send3_ref, g1, g2, b2, v2, pairs, thin,
):
    place_y = lax.axis_index("gy")
    low_y = jnp.where(place_y > 0, 1.0, 0.0).astype(F32)
    high_y = jnp.where(place_y < count_y - 1, 1.0, 0.0).astype(F32)
    g1[2:22, 0:8, :] = below_ref[...] * low_y
    g1[2:22, 8:16, :] = mid_ref[...]
    g1[2:22, 16:24, :] = above_ref[...] * high_y

    def begin1(i):
        b1_ref[i] = q1[i] * g1[i]

    loop(2, X1 - 2, begin1)
    sweep(b1_ref, v1_ref, b1_ref, wx1, wy1, wz1, q1, 3, X1 - 3)

    def restrict(j):
        i = 2 * j + 4
        after = defect(v1_ref, g1, wx1, wy1, wz1, d1, i + 1)
        keep(pairs, j, defect(v1_ref, g1, wx1, wy1, wz1, d1, i) + after)

    loop(0, 8, restrict)
    rows = jnp.concatenate([halve_rows(pairs, i, 4, 8) for i in range(8)], axis=0)
    small = 0.5 * split_dot(rows, pair_sum_matrix(Z1, Z2))
    g2[...] = jnp.zeros((X2, Y2, Z2), F32)
    for i in range(8):
        g2[2 + i, 2:10, :] = small[8 * i : 8 * i + 8]
    for i in range(2, X2 - 2):
        b2[i] = q2[i] * g2[i]
    sweep(b2, v2, b2, wx2, wy2, wz2, q2, 3, X2 - 3)
    row = iota((8, Z2), 0) < 4
    for i in range(4):
        send2_ref[i] = jnp.where(row, pltpu.roll(v2[4 + i, 0:8, :], 4, 0), g2[4 + i, 0:8, :])
    halves = [
        defect(v2, g2, wx2, wy2, wz2, d2, 4 + 2 * i) + defect(v2, g2, wx2, wy2, wz2, d2, 5 + 2 * i)
        for i in range(2)
    ]
    thin[...] = 0.5 * split_dot(jnp.concatenate(halves, axis=0), pair_sum_matrix(Z2, LANES))
    row = iota((8, LANES), 0)
    source = jnp.zeros((8, LANES), F32)
    for i in range(2):
        for j in range(2):
            at = 16 * i + 4 + 2 * j
            both = thin[at : at + 1, :] + thin[at + 1 : at + 2, :]
            source = jnp.where(row == 2 * i + j, jnp.broadcast_to(both, (8, LANES)), source)
    source = source + c3_ref[...]
    double = jnp.where(row < 4, source, pltpu.roll(source, 4, 0))
    for i in range(count_x * count_y // 2):
        send3_ref[8 * i : 8 * i + 8, :] = double


def down1(count_x, count_y, *operands):
    frame1, frame2 = (X1, Y1, Z1), (X2, Y2, Z2)
    return call(
        functools.partial(down1_kernel, count_x, count_y),
        [struct(*frame1), struct(*frame1), struct(4, 8, Z2), struct(4 * count_x * count_y, LANES)],
        [vmem(*frame1)] + [vmem(*frame2)] * 3 + [vmem(8, Z1 // LANES, Y1, LANES), vmem(32, LANES)],
    )(*operands)


def iterate_edge_kernel(count_x, own_ref, low_ref, high_ref, top_ref, bottom_ref):
    place = lax.axis_index("gx")
    first = jnp.where(place > 0, 1.0, 0.0).astype(F32)
    last = jnp.where(place < count_x - 1, 1.0, 0.0).astype(F32)
    row = iota((8, Z0), 0) < 4

    def slab(i):
        if i < 3:
            return low_ref[i] * first
        if i < 19:
            return own_ref[i - 3]
        return high_ref[i - 19] * last

    for j in range(X0 // 2):
        even, odd = slab(2 * j), slab(2 * j + 1)
        top_ref[j] = jnp.where(row, pltpu.roll(even[8:16], 4, 0), odd[8:16])
        bottom_ref[j] = jnp.where(row, even[0:8], pltpu.roll(odd[0:8], 4, 0))


def iterate_edges(count_x, own, low, high):
    return call(
        functools.partial(iterate_edge_kernel, count_x), [struct(X0 // 2, 8, Z0), struct(X0 // 2, 8, Z0)], []
    )(own, low, high)


def up_kernel(
    count_x, count_y,
    all_ref, mid2, below2, above2, wx2, wy2, wz2, q2,
    v1, b1, wx1, wy1, wz1, q1,
    v_own, v_low, v_high, v_below, v_above, g_ref,
    wx0_hbm, wy0_hbm, wz0_hbm, d0_hbm, q0_hbm, b0_hbm,
    solution_ref, residual_ref,
    c3, wx3, wy3, wz3, d3, q3, b3, v3, w3, thin3,
    c4, wx4, wy4, wz4, d4, q4, g4, v4, w4, thin4,
    v2, w2, b2, w1, spread1, wx0, wy0, wz0, d0, q0, b0, v0, w0, spread0, sems,
):
    place_x, place_y = lax.axis_index("gx"), lax.axis_index("gy")
    copies = [
        pltpu.make_async_copy(there, here, sems.at[k])
        for k, (there, here) in enumerate(
            zip((wx0_hbm, wy0_hbm, wz0_hbm, d0_hbm, q0_hbm, b0_hbm), (wx0, wy0, wz0, d0, q0, b0))
        )
    ]
    for copy in copies:
        copy.start()
    n3, n4 = 2 * count_x, count_x

    c3[...] = jnp.zeros(c3.shape, F32)
    b3[...] = jnp.zeros(b3.shape, F32)
    v3[...] = jnp.zeros(v3.shape, F32)
    w3[...] = jnp.zeros(w3.shape, F32)
    lane = iota((count_y, LANES), 1) < 64
    for i in range(n3):
        base = (i // 2) * count_y * 4 + 2 * (i % 2)
        for j in range(2):
            part = all_ref[pl.ds(base + j, count_y, stride=4), :]
            b3[1 + i, pl.ds(j, count_y, stride=2), :] = jnp.where(lane, part, 0.0)
            c3[1 + i, pl.ds(j, count_y, stride=2), :] = jnp.where(lane, pltpu.roll(part, 64, 1), 0.0)
    in_y = jnp.logical_and(iota((Y3, LANES), 0) < 2 * count_y, iota((Y3, LANES), 1) < 64).astype(F32)
    make_faces(c3, wx3, wy3, wz3, d3, q3, 1, n3 + 1, lambda i: 1.0, in_y, whole_y=1)

    def begin3(i):
        v3[i] = q3[i] * b3[i]

    loop(1, n3 + 1, begin3)

    def sweep3(i):
        here, total = neighbours(v3, wx3, wy3, wz3, i)
        w3[i] = 0.2 * here + q3[i] * (b3[i] + total)

    loop(1, n3 + 1, sweep3)

    def restrict3(j):
        i = 2 * j + 1
        thin3[j] = defect(w3, b3, wx3, wy3, wz3, d3, i) + defect(w3, b3, wx3, wy3, wz3, d3, i + 1)

    loop(0, n4, restrict3)
    valid = iota((Y4, LANES), 0) < count_y
    rows = jnp.concatenate(
        [thin3[i, pl.ds(0, Y4, stride=2), :] + thin3[i, pl.ds(1, Y4, stride=2), :] for i in range(n4)], axis=0
    )
    pick = pair_sum_matrix(LANES, LANES)
    g4[...] = (0.5 * split_dot(rows, pick)).reshape(n4, Y4, LANES)
    for i in range(n4):
        thin3[i] = c3[2 * i + 1] + c3[2 * i + 2]
    rows = jnp.concatenate(
        [thin3[i, pl.ds(0, Y4, stride=2), :] + thin3[i, pl.ds(1, Y4, stride=2), :] for i in range(n4)], axis=0
    )
    c4[...] = jnp.zeros(c4.shape, F32)
    c4[1 : n4 + 1] = (0.125 * split_dot(rows, pick)).reshape(n4, Y4, LANES)
    in_y = jnp.logical_and(valid, iota((Y4, LANES), 1) < 32).astype(F32)
    make_faces(c4, wx4, wy4, wz4, d4, q4, 1, n4 + 1, lambda i: 1.0, in_y, whole_y=1)
    v4[...] = jnp.zeros(v4.shape, F32)
    w4[...] = jnp.zeros(w4.shape, F32)
    for i in range(n4):
        g4[i] = q4[1 + i] * g4[i]
        v4[1 + i] = g4[i]

    def bottom(source, target):
        for i in range(n4):
            here, total = neighbours(source, wx4, wy4, wz4, 1 + i)
            target[1 + i] = (0.2 * here + g4[i]) + q4[1 + i] * total

    def two(step):
        bottom(v4, w4)
        bottom(w4, v4)

    loop(0, (BOTTOM - 2) // 2, two)
    bottom(v4, w4)

    wide = split_dot(w4[1 : n4 + 1].reshape(n4 * Y4, LANES), copy_matrix(LANES, LANES)).reshape(n4, Y4, LANES)
    for i in range(n4):
        thin4[pl.ds(0, Y4, stride=2), :] = wide[i]
        thin4[pl.ds(1, Y4, stride=2), :] = wide[i]
        extra = thin4[...]
        v3[1 + 2 * i] = w3[1 + 2 * i] + extra
        v3[2 + 2 * i] = w3[2 + 2 * i] + extra

    loop(1, n3 + 1, sweep3)

    def sweep3_again(i):
        here, total = neighbours(w3, wx3, wy3, wz3, i)
        v3[i] = 0.2 * here + q3[i] * (b3[i] + total)

    loop(1, n3 + 1, sweep3_again)

    low_y = jnp.where(place_y > 0, 1.0, 0.0).astype(F32)
    high_y = jnp.where(place_y < count_y - 1, 1.0, 0.0).astype(F32)
    near = jnp.zeros((6, Y3, LANES), F32)
    slabs = []
    for j in range(6):
        at = 2 * place_x - 2 + j
        slabs.append(v3[1 + jnp.clip(at, 0, n3 - 1)] * flag(at, n3))
    wide = split_dot(jnp.concatenate(slabs, axis=0), copy_matrix(LANES, LANES))
    target, origin = iota((Y2, Y3), 0), iota((Y2, Y3), 1)
    rows = jnp.logical_and(origin == 2 * place_y - 2 + target // 2, target < 12).astype(F32).astype(BF16)
    half = iota((8, Z2), 0) < 4
    for j in range(6):
        extra = split_dot_left(rows, wide[Y3 * j : Y3 * j + Y3])
        for k in range(2):
            i = 2 * j + k
            below, mid, above = below2[i] * low_y, mid2[i], above2[i] * high_y
            v2[i, 0:8] = jnp.where(half, below, pltpu.roll(mid, 4, 0)) + extra[0:8]
            v2[i, 8:16] = jnp.where(half, above, 0.0) + extra[8:16]
            b2[i, 0:8] = jnp.where(half, pltpu.roll(below, 4, 0), mid)
            b2[i, 8:16] = jnp.where(half, pltpu.roll(above, 4, 0), 0.0)
    for i in range(1, X2 - 1):
        b2[i] = q2[i] * b2[i]
    sweep(v2, w2, b2, wx2, wy2, wz2, q2, 1, X2 - 1)
    sweep(w2, v2, b2, wx2, wy2, wz2, q2, 2, X2 - 2)

    wide = split_dot(v2[2:10].reshape(8 * Y2, Z2), copy_matrix(Z2, Z1)).reshape(8, Y2, Z1)
    spread1[...] = jnp.zeros(spread1.shape, F32)
    for j in range(8):
        extra = double_rows(spread1, wide[j, 2:10], 4)
        for k in range(2):
            i = 4 + 2 * j + k
            v1[i] = v1[i] + extra
    sweep(v1, w1, b1, wx1, wy1, wz1, q1, 5, X1 - 5)
    sweep(w1, v1, b1, wx1, wy1, wz1, q1, 6, X1 - 6)

    wide = split_dot(v1[6:18].reshape(12 * Y1, Z1), copy_matrix(Z1, Z0)).reshape(12, Y1, Z0)
    first = jnp.where(place_x > 0, 1.0, 0.0).astype(F32)
    last = jnp.where(place_x < count_x - 1, 1.0, 0.0).astype(F32)
    half = iota((8, Z0), 0) < 4
    for copy in copies:
        copy.wait()
    for j in range(12):
        extra = double_rows(spread0, wide[j, 6:18], 0)
        for k in range(2):
            i = 2 * j - 1 + k
            if i < 0 or i >= X0:
                continue
            own = v_low[i] * first if i < 3 else v_own[i - 3] if i < 19 else v_high[i - 19] * last
            below, above = v_below[i // 2] * low_y, v_above[i // 2] * high_y
            if i % 2:
                below = pltpu.roll(below, 4, 0)
            else:
                above = pltpu.roll(above, 4, 0)
            head, tail = pltpu.roll(own[0:8], 4, 0), pltpu.roll(own[8:16], 4, 0)
            v0[i, 0:8] = jnp.where(half, below, head) + extra[0:8]
            v0[i, 8:16] = jnp.where(half, head, tail) + extra[8:16]
            v0[i, 16:24] = jnp.where(half, tail, above) + extra[16:24]
    sweep(v0, w0, b0, wx0, wy0, wz0, q0, 1, X0 - 1)
    sweep(w0, v0, b0, wx0, wy0, wz0, q0, 2, X0 - 2)

    def finish(i):
        here, total = neighbours(v0, wx0, wy0, wz0, i + OX0)
        solution_ref[i] = pltpu.roll(here, Y0 - OY0, 0)[0:16]
        residual_ref[i] = g_ref[i] + pltpu.roll(total - d0[i + OX0] * here, Y0 - OY0, 0)[0:16]

    loop(0, 16, finish)


def up(count_x, count_y, *operands):
    any_space = pl.BlockSpec(memory_space=pl.ANY)
    whole = pl.BlockSpec(memory_space=pltpu.VMEM)
    frame0, frame1, frame2 = (X0, Y0, Z0), (X1, Y1, Z1), (X2, Y2, Z2)
    frame3, frame4 = (2 * count_x + 2, Y3, LANES), (count_x + 2, Y4, LANES)
    return call(
        functools.partial(up_kernel, count_x, count_y),
        [struct(16, 16, Z0), struct(16, 16, Z0)],
        [vmem(*frame3)] * 9 + [vmem(count_x, Y3, LANES)]
        + [vmem(*frame4)] * 6 + [vmem(count_x, Y4, LANES)] + [vmem(*frame4)] * 2 + [vmem(Y3, LANES)]
        + [vmem(*frame2)] * 3 + [vmem(*frame1), vmem(Z1 // LANES, Y1, LANES)]
        + [vmem(*frame0)] * 8 + [vmem(Z0 // LANES, Y0, LANES), pltpu.SemaphoreType.DMA((6,))],
        in_specs=[whole] * (len(operands) - 6) + [any_space] * 6,
        out_specs=[whole] * 2,
    )(*operands)


def to_next(cells, axis):
    count = lax.axis_size(axis)
    return lax.ppermute(cells, axis, [(i, (i + 1) % count) for i in range(count)])


def to_previous(cells, axis):
    count = lax.axis_size(axis)
    return lax.ppermute(cells, axis, [((i + 1) % count, i) for i in range(count)])


def shards(right_side, coefficient):
    count_x, count_y = lax.axis_size("gx"), lax.axis_size("gy")
    place_x = lax.axis_index("gx")

    def with_sides(low, cells, high):
        low = jnp.where(place_x > 0, low, 0.0)
        high = jnp.where(place_x < count_x - 1, high, 0.0)
        return jnp.concatenate([low, cells, high], axis=0)

    low = to_next(jnp.concatenate([coefficient[13:16], right_side[14:16]], axis=0), "gx")
    high = to_previous(jnp.concatenate([coefficient[0:3], right_side[0:2]], axis=0), "gx")
    c1 = coarsen_own(coefficient)
    c1_low, c1_high = to_next(c1, "gx"), to_previous(c1, "gx")
    top, bottom = edges_y(coefficient, right_side, low, high, count_x)
    below, above = to_next(top, "gy"), to_previous(bottom, "gy")
    c1_mid = with_sides(c1_low, c1, c1_high)
    c1_below, c1_above = to_next(c1_mid, "gy"), to_previous(c1_mid, "gy")

    g1, v_first, v_last, v_own, wx0, wy0, wz0, d0, q0, b0 = down0(
        count_x, count_y, coefficient, right_side, low, high, below, above
    )

    g1_low, g1_high = to_next(g1[2:8], "gx"), to_previous(g1[0:6], "gx")
    levels = prepare(count_x, count_y, c1_mid, c1_below, c1_above)
    wx1, wy1, wz1, d1, q1, wx2, wy2, wz2, d2, q2, c3 = levels
    g1_mid = with_sides(g1_low, g1, g1_high)
    g1_below, g1_above = to_next(g1_mid, "gy"), to_previous(g1_mid, "gy")
    v_low, v_high = to_next(v_last, "gx"), to_previous(v_first, "gx")
    v_top, v_bottom = iterate_edges(count_x, v_own, v_low, v_high)
    v_below, v_above = to_next(v_top, "gy"), to_previous(v_bottom, "gy")
    v1, b1, send2, send3 = down1(count_x, count_y, g1_mid, g1_below, g1_above, *levels)

    everything = lax.all_to_all(send3, ("gx", "gy"), split_axis=0, concat_axis=0, tiled=True)
    mid2 = with_sides(to_next(send2, "gx"), send2, to_previous(send2, "gx"))
    below2, above2 = to_next(mid2, "gy"), to_previous(mid2, "gy")
    return tuple(
        up(
            count_x, count_y, everything, mid2, below2, above2, wx2, wy2, wz2, q2,
            v1, b1, wx1, wy1, wz1, q1, v_own, v_low, v_high, v_below, v_above, right_side,
            wx0, wy0, wz0, d0, q0, b0,
        )
    )


def solution(mesh):
    specs = (P("gx", "gy", None), P("gx", "gy", None))
    return jax.shard_map(shards, mesh=mesh, in_specs=specs, out_specs=specs, check_vma=False)
```

```python
import functools

import jax
import jax.numpy as jnp
from jax import lax
from jax.experimental import pallas as pl
from jax.experimental.pallas import tpu as pltpu
from jax.sharding import PartitionSpec as P

F32 = jnp.float32
BF16 = jnp.bfloat16
OMEGA = 0.8
BOTTOM = 16
MIB = 1024 * 1024

X0, Y0, Z0, OX0, OY0 = 22, 24, 512, 3, 4
X1, Y1, Z1, OX1, OY1 = 24, 24, 256, 8, 8
X2, Y2, Z2, OX2, OY2 = 12, 16, 128, 4, 4
Y3, Y4, LANES = 16, 8, 128


def iota(shape, dim):
    return lax.broadcasted_iota(jnp.int32, shape, dim)


def up_of(cells, dim):
    return pltpu.roll(cells, cells.shape[dim] - 1, dim)


def down_of(cells, dim):
    return pltpu.roll(cells, 1, dim)


def split_dot(cells, pick):
    high = cells.astype(BF16)
    rest = cells - high.astype(F32)
    mid = rest.astype(BF16)
    low = (rest - mid.astype(F32)).astype(BF16)
    dot = functools.partial(jnp.dot, preferred_element_type=F32)
    return dot(high, pick) + (dot(mid, pick) + dot(low, pick))


def split_dot_left(pick, cells):
    high = cells.astype(BF16)
    rest = cells - high.astype(F32)
    mid = rest.astype(BF16)
    low = (rest - mid.astype(F32)).astype(BF16)
    dot = functools.partial(jnp.dot, preferred_element_type=F32)
    return dot(pick, high) + (dot(pick, mid) + dot(pick, low))


def pair_sum_matrix(fine, coarse, offset=0):
    hit = (iota((fine, coarse), 0) // 2) + offset == iota((fine, coarse), 1)
    return hit.astype(F32).astype(BF16)


def copy_matrix(coarse, fine):
    hit = iota((coarse, fine), 0) == iota((coarse, fine), 1) // 2
    return hit.astype(F32).astype(BF16)


def inside(shape, dim, start, count):
    place = iota(shape, dim) + start
    return jnp.logical_and(place >= 0, place < count)


def flag(start, count):
    return jnp.where(jnp.logical_and(start >= 0, start < count), 1.0, 0.0).astype(F32)


def loop(first, last, body, width=1):
    def run(i, count):
        stores = [store for j in range(count) for store in body(i + j)]
        for ref, at, value in stores:
            ref[at] = value

    count = (last - first) // width

    def step(t, carry):
        run(first + t * width, width)
        return carry

    if count == 1:
        run(first, width)
    else:
        lax.fori_loop(0, count, step, 0)
    if (last - first) % width:
        run(first + count * width, (last - first) % width)


def make_faces(c, wx, wy, wz, d, q, first, last, in_x, in_y, width, whole_y=0):
    rows, cells = c.shape[1], c.shape[2]
    end_z = iota((rows, cells), 1) == cells - 1
    start_z = iota((rows, cells), 1) == 0
    row = iota((rows, cells), 0)
    wx[first - 1] = 0.5 * (c[first - 1] + c[first])

    def body(i):
        here = c[i]
        after = c[i + 1]
        before = c[i - 1]
        y_up, y_down = up_of(here, 0), down_of(here, 0)
        if whole_y:
            y_up = jnp.where(row == rows - 1, 0.0, y_up)
            y_down = jnp.where(row == 0, 0.0, y_down)
        z_up = jnp.where(end_z, 0.0, up_of(here, 1))
        z_down = jnp.where(start_z, 0.0, down_of(here, 1))
        side = 0.5 * (here + y_up)
        side = jnp.where(row == rows - 1, 0.0, side) if whole_y else side
        total = 3.0 * here + 0.5 * ((after + before) + (y_up + y_down) + (z_up + z_down))
        return [
            (wx, i, 0.5 * (here + after)),
            (wy, i, side),
            (wz, i, jnp.where(end_z, 0.0, 0.5 * (here + z_up))),
            (d, i, total),
            (q, i, (in_y * (OMEGA * in_x(i))) / jnp.maximum(total, 1e-30)),
        ]

    loop(first, last, body, width)


def neighbours(v, wx, wy, wz, i):
    here = v[i]
    side_y, side_z = wy[i], wz[i]
    along_x = wx[i] * v[i + 1] + wx[i - 1] * v[i - 1]
    along_y = side_y * up_of(here, 0) + down_of(side_y * here, 0)
    along_z = side_z * up_of(here, 1) + down_of(side_z * here, 1)
    return here, along_x + along_y + along_z


def sweep(v, out, b, wx, wy, wz, q, first, last, width):
    def body(i):
        here, total = neighbours(v, wx, wy, wz, i)
        return [(out, i, (0.2 * here + b[i]) + q[i] * total)]

    loop(first, last, body, width)


def defect(v, source, wx, wy, wz, d, i):
    here, total = neighbours(v, wx, wy, wz, i)
    return (source[i] - d[i] * here) + total


def lanes(cells, k):
    return cells[:, LANES * k : LANES * k + LANES]


def keep(scratch, j, cells):
    for k in range(cells.shape[1] // LANES):
        scratch[j, k] = lanes(cells, k)


def halve_rows(scratch, j, start, count):
    parts = [
        scratch[j, k, pl.ds(start, count, stride=2), :] + scratch[j, k, pl.ds(start + 1, count, stride=2), :]
        for k in range(scratch.shape[1])
    ]
    return jnp.concatenate(parts, axis=1)


def double_rows(scratch, cells, start):
    for k in range(scratch.shape[0]):
        for odd in range(2):
            scratch[k, pl.ds(start + odd, cells.shape[0], stride=2), :] = lanes(cells, k)
    return jnp.concatenate([scratch[k] for k in range(scratch.shape[0])], axis=1)


def call(kernel, out_shape, scratch, limit, in_specs=None, out_specs=None, flops=1000000, bytes_accessed=1000000):
    extra = {}
    if in_specs is not None:
        extra["in_specs"] = in_specs
    if out_specs is not None:
        extra["out_specs"] = out_specs
    return pl.pallas_call(
        kernel,
        out_shape=out_shape,
        scratch_shapes=scratch,
        compiler_params=pltpu.CompilerParams(vmem_limit_bytes=limit * MIB),
        cost_estimate=pl.CostEstimate(flops=flops, bytes_accessed=bytes_accessed, transcendentals=0),
        **extra,
    )


def struct(*shape):
    return jax.ShapeDtypeStruct(shape, F32)


def vmem(*shape):
    return pltpu.VMEM(shape, F32)


def place_of(i):
    row, cell = 8 * ((i // 2) % 2), Z1 * (i % 2)
    return 5 + i // 4, slice(row, row + 8), slice(cell, cell + Z1)


def begin_kernel(c_ref, g_ref, next_ref, previous_ref, c1_ref, pairs):
    for i in range(8):
        keep(pairs, i, c_ref[2 * i] + c_ref[2 * i + 1])
    for i in range(3):
        next_ref[i] = c_ref[13 + i]
        previous_ref[i] = c_ref[i]
    for i in range(2):
        next_ref[3 + i] = g_ref[14 + i]
        previous_ref[3 + i] = g_ref[i]
    rows = jnp.concatenate([halve_rows(pairs, i, 0, 8) for i in range(8)], axis=0)
    small = 0.125 * split_dot(rows, pair_sum_matrix(Z0, Z1))
    for i in range(8):
        block = small[8 * i : 8 * i + 8]
        c1_ref[i] = block
        next_ref[place_of(i)] = block
        previous_ref[place_of(i)] = block


def begin(coefficient, right_side):
    return call(
        begin_kernel, [struct(7, 16, Z0), struct(7, 16, Z0), struct(8, 8, Z1)], [vmem(8, Z0 // LANES, 16, LANES)], 60
    )(coefficient, right_side)


def edge_kernel(count_x, c_ref, g_ref, c1_ref, low_ref, high_ref, top_ref, bottom_ref):
    place = lax.axis_index("gx")
    first = jnp.where(place > 0, 1.0, 0.0).astype(F32)
    last = jnp.where(place < count_x - 1, 1.0, 0.0).astype(F32)
    row = iota((8, Z0), 0)

    def put(i, c, g):
        return [
            (top_ref, i, jnp.where(row < 4, pltpu.roll(c[8:16], 4, 0), g[8:16])),
            (bottom_ref, i, jnp.where(row < 4, g[0:8], pltpu.roll(c[0:8], 4, 0))),
        ]

    def put_now(*what):
        for ref, at, value in put(*what):
            ref[at] = value

    nothing = jnp.zeros((16, Z0), F32)
    for i in range(3):
        put_now(i, low_ref[i] * first, low_ref[i + 2] * first if i > 0 else nothing)
        put_now(19 + i, high_ref[i] * last, high_ref[i + 3] * last if i < 2 else nothing)

    def body(i):
        return put(i + 3, c_ref[i], g_ref[i])

    loop(0, 16, body, 2)
    for i in range(24):
        part = low_ref[place_of(i)] * first if i < 8 else c1_ref[i - 8] if i < 16 else high_ref[place_of(i - 16)] * last
        for ref in (top_ref, bottom_ref):
            ref[X0 + i // 2, :, Z1 * (i % 2) : Z1 * (i % 2) + Z1] = part


def edges_y(count_x, *operands):
    return call(
        functools.partial(edge_kernel, count_x), [struct(X0 + 12, 8, Z0), struct(X0 + 12, 8, Z0)], [], 8
    )(*operands)


def ends(axis, count):
    place = lax.axis_index(axis)
    low = jnp.where(place > 0, 1.0, 0.0).astype(F32)
    return low, jnp.where(place < count - 1, 1.0, 0.0).astype(F32)


def window0(low_ref, high_ref, below_ref, above_ref, c_ref, g_ref, first, last, low_y, high_y):
    row = iota((8, Z0), 0) < 4
    nothing = jnp.zeros((16, Z0), F32)

    def put(own, below, above):
        head, tail = pltpu.roll(own[0:8], 4, 0), pltpu.roll(own[8:16], 4, 0)
        parts = [jnp.where(row, below, head), jnp.where(row, head, tail), jnp.where(row, tail, above)]
        return jnp.concatenate(parts, axis=0)

    def c_slab(i, own):
        return put(own, below_ref[i] * low_y, above_ref[i] * high_y)

    def g_slab(i, own):
        return put(own, pltpu.roll(below_ref[i], 4, 0) * low_y, pltpu.roll(above_ref[i], 4, 0) * high_y)

    def fill(c, g):
        for i in range(3):
            c[i] = c_slab(i, low_ref[i] * first)
            c[19 + i] = c_slab(19 + i, high_ref[i] * last)
            g[i] = g_slab(i, low_ref[i + 2] * first if i > 0 else nothing)
            g[19 + i] = g_slab(19 + i, high_ref[i + 3] * last if i < 2 else nothing)

        def body(i):
            return [(c, i + 3, c_slab(i + 3, c_ref[i])), (g, i + 3, g_slab(i + 3, g_ref[i]))]

        loop(0, 16, body)

    return fill


def down0_kernel(
    count_x, count_y,
    c_ref, g_ref, low_ref, high_ref, below_ref, above_ref,
    g1_ref, v_own_ref, c, g, wx, wy, wz, d, q, b, v, pairs,
):
    place_x, place_y = lax.axis_index("gx"), lax.axis_index("gy")
    sides = ends("gx", count_x) + ends("gy", count_y)
    window0(low_ref, high_ref, below_ref, above_ref, c_ref, g_ref, *sides)(c, g)
    in_y = inside((Y0, Z0), 0, place_y * 16 - OY0, 16 * count_y).astype(F32)
    make_faces(
        c, wx, wy, wz, d, q, 1, X0 - 1, lambda i: flag(place_x * 16 - OX0 + i, 16 * count_x), in_y, 1
    )

    def begin(i):
        return [(b, i, q[i] * g[i])]

    loop(1, X0 - 1, begin, 2)
    sweep(b, v, b, wx, wy, wz, q, 2, X0 - 2, 2)

    def own_of(i):
        return [(v_own_ref, i, pltpu.roll(v[i + 3], Y0 - OY0, 0)[0:16])]

    loop(0, 16, own_of, 2)

    def restrict(j):
        i = 2 * j + OX0
        both = defect(v, g, wx, wy, wz, d, i) + defect(v, g, wx, wy, wz, d, i + 1)
        return [(pairs, (j, k), lanes(both, k)) for k in range(Z0 // LANES)]

    loop(0, 8, restrict)
    rows = jnp.concatenate([halve_rows(pairs, i, 4, 8) for i in range(8)], axis=0)
    g1_ref[...] = (0.5 * split_dot(rows, pair_sum_matrix(Z0, Z1))).reshape(8, 8, Z1)


def down0(count_x, count_y, *operands):
    frame = (X0, Y0, Z0)
    return call(
        functools.partial(down0_kernel, count_x, count_y),
        [struct(8, 8, Z1), struct(16, 16, Z0)],
        [vmem(*frame)] * 9 + [vmem(8, Z0 // LANES, Y0, LANES)],
        18,
    )(*operands)


def fill_c1(c1, c1_ref, low_ref, high_ref, below_ref, above_ref, first, last, low_y, high_y):
    for i in range(24):
        at = X0 + i // 2, slice(0, 8), slice(Z1 * (i % 2), Z1 * (i % 2) + Z1)
        part = low_ref[place_of(i)] * first if i < 8 else c1_ref[i - 8] if i < 16 else high_ref[place_of(i - 16)] * last
        c1[i, 0:8, :] = below_ref[at] * low_y
        c1[i, 8:16, :] = part
        c1[i, 16:24, :] = above_ref[at] * high_y


def prepare_kernel(
    count_x, count_y, c1_ref, low_ref, high_ref, below_ref, above_ref,
    wx1, wy1, wz1, d1, q1, wx2, wy2, wz2, d2, q2, c3_ref, c1, c2, pairs,
):
    place_x, place_y = lax.axis_index("gx"), lax.axis_index("gy")
    sides = ends("gx", count_x) + ends("gy", count_y)
    fill_c1(c1, c1_ref, low_ref, high_ref, below_ref, above_ref, *sides)
    in_y = inside((Y1, Z1), 0, place_y * 8 - OY1, 8 * count_y).astype(F32)
    make_faces(
        c1, wx1, wy1, wz1, d1, q1, 2, X1 - 2, lambda i: flag(place_x * 8 - OX1 + i, 8 * count_x), in_y, 2
    )
    for i in range(12):
        keep(pairs, i, c1[2 * i] + c1[2 * i + 1])
    blank = jnp.zeros((4, Z1), F32)
    rows = []
    for i in range(12):
        rows.append(halve_rows(pairs, i, 0, 12))
        rows.append(blank)
    c2[...] = (0.125 * split_dot(jnp.concatenate(rows, axis=0), pair_sum_matrix(Z1, Z2))).reshape(X2, Y2, Z2)
    in_y = inside((Y2, Z2), 0, place_y * 4 - OY2, 4 * count_y).astype(F32)
    make_faces(
        c2, wx2, wy2, wz2, d2, q2, 1, X2 - 1, lambda i: flag(place_x * 4 - OX2 + i, 4 * count_x), in_y, 10
    )
    rows = jnp.concatenate([c2[4] + c2[5], c2[6] + c2[7]], axis=0)
    thin = 0.125 * split_dot(rows, pair_sum_matrix(Z2, LANES, 64))
    row = iota((8, LANES), 0)
    c3 = jnp.zeros((8, LANES), F32)
    for i in range(2):
        for j in range(2):
            at = 16 * i + 4 + 2 * j
            both = thin[at : at + 1] + thin[at + 1 : at + 2]
            c3 = jnp.where(row == 2 * i + j, jnp.broadcast_to(both, (8, LANES)), c3)
    c3_ref[...] = c3


def prepare(count_x, count_y, *operands):
    frame1, frame2 = (X1, Y1, Z1), (X2, Y2, Z2)
    return call(
        functools.partial(prepare_kernel, count_x, count_y),
        [struct(*frame1)] * 5 + [struct(*frame2)] * 5 + [struct(8, LANES)],
        [vmem(*frame1), vmem(*frame2), vmem(12, Z1 // LANES, Y1, LANES)],
        8,
    )(*operands)


def fill_g1(g1, mid_ref, below_ref, above_ref, low_y, high_y):
    g1[2:22, 0:8, :] = below_ref[...] * low_y
    g1[2:22, 8:16, :] = mid_ref[...]
    g1[2:22, 16:24, :] = above_ref[...] * high_y


def down1_kernel(
    count_x, count_y, v_own_ref, mid_ref, below_ref, above_ref,
    wx1, wy1, wz1, d1, q1, wx2, wy2, wz2, d2, q2, c3_ref,
    v_far, next_ref, previous_ref, send2_ref, send3_ref, v1_ref, b1_ref, g1, g2, b2, v2, pairs, thin,
):
    place_y = lax.axis_index("gy")
    low_y = jnp.where(place_y > 0, 1.0, 0.0).astype(F32)
    high_y = jnp.where(place_y < count_y - 1, 1.0, 0.0).astype(F32)
    fill_g1(g1, mid_ref, below_ref, above_ref, low_y, high_y)

    def begin1(i):
        return [(b1_ref, i, q1[i] * g1[i])]

    loop(2, X1 - 2, begin1, 4)
    sweep(b1_ref, v1_ref, b1_ref, wx1, wy1, wz1, q1, 3, X1 - 3, 3)

    def restrict(j):
        i = 2 * j + 4
        after = defect(v1_ref, g1, wx1, wy1, wz1, d1, i + 1)
        both = defect(v1_ref, g1, wx1, wy1, wz1, d1, i) + after
        return [(pairs, (j, k), lanes(both, k)) for k in range(Z1 // LANES)]

    loop(0, 8, restrict, 2)
    rows = jnp.concatenate([halve_rows(pairs, i, 4, 8) for i in range(8)], axis=0)
    small = 0.5 * split_dot(rows, pair_sum_matrix(Z1, Z2))
    g2[...] = jnp.zeros((X2, Y2, Z2), F32)
    for i in range(8):
        g2[2 + i, 2:10, :] = small[8 * i : 8 * i + 8]
    for i in range(2, X2 - 2):
        b2[i] = q2[i] * g2[i]
    sweep(b2, v2, b2, wx2, wy2, wz2, q2, 3, X2 - 3, 6)
    row = iota((8, Z2), 0) < 4
    for i in range(4):
        both = jnp.where(row, pltpu.roll(v2[4 + i, 0:8, :], 4, 0), g2[4 + i, 0:8, :])
        send2_ref[:, LANES * i : LANES * i + LANES] = both
        next_ref[6, :, LANES * i : LANES * i + LANES] = both
        previous_ref[6, :, LANES * i : LANES * i + LANES] = both
    for i in range(3):
        for half in range(2):
            next_ref[2 * i + half] = v_own_ref[13 + i, 8 * half : 8 * half + 8, :]
            previous_ref[2 * i + half] = v_own_ref[i, 8 * half : 8 * half + 8, :]
    halves = [
        defect(v2, g2, wx2, wy2, wz2, d2, 4 + 2 * i) + defect(v2, g2, wx2, wy2, wz2, d2, 5 + 2 * i)
        for i in range(2)
    ]
    thin[...] = 0.5 * split_dot(jnp.concatenate(halves, axis=0), pair_sum_matrix(Z2, LANES))
    row = iota((8, LANES), 0)
    source = jnp.zeros((8, LANES), F32)
    for i in range(2):
        for j in range(2):
            at = 16 * i + 4 + 2 * j
            both = thin[at : at + 1, :] + thin[at + 1 : at + 2, :]
            source = jnp.where(row == 2 * i + j, jnp.broadcast_to(both, (8, LANES)), source)
    source = source + c3_ref[...]
    double = jnp.where(row < 4, source, pltpu.roll(source, 4, 0))
    for i in range(count_x * count_y // 2):
        send3_ref[8 * i : 8 * i + 8, :] = double
    v_far[...] = v1_ref[4:20]


def down1(count_x, count_y, *operands):
    frame1, frame2 = (X1, Y1, Z1), (X2, Y2, Z2)
    return call(
        functools.partial(down1_kernel, count_x, count_y),
        [struct(16, Y1, Z1), struct(7, 8, Z0), struct(7, 8, Z0), struct(8, Z0)]
        + [struct(4 * count_x * count_y, LANES)],
        [vmem(*frame1)] * 3 + [vmem(*frame2)] * 3 + [vmem(8, Z1 // LANES, Y1, LANES), vmem(32, LANES)],
        8,
    )(*operands)


def iterate_edge_kernel(count_x, own_ref, own2_ref, low_ref, high_ref, top_ref, bottom_ref):
    place = lax.axis_index("gx")
    first = jnp.where(place > 0, 1.0, 0.0).astype(F32)
    last = jnp.where(place < count_x - 1, 1.0, 0.0).astype(F32)
    row = iota((8, Z0), 0) < 4

    def slab(i, half):
        if i < 3:
            return low_ref[2 * i + half] * first
        if i < 19:
            return own_ref[i - 3, 8 * half : 8 * half + 8, :]
        return high_ref[2 * (i - 19) + half] * last

    for j in range(X0 // 2):
        top_ref[j] = jnp.where(row, pltpu.roll(slab(2 * j, 1), 4, 0), slab(2 * j + 1, 1))
        bottom_ref[j] = jnp.where(row, slab(2 * j, 0), pltpu.roll(slab(2 * j + 1, 0), 4, 0))
    for ref in (top_ref, bottom_ref):
        ref[11] = low_ref[6] * first
        ref[12] = own2_ref[...]
        ref[13] = high_ref[6] * last


def iterate_edges(count_x, *operands):
    return call(
        functools.partial(iterate_edge_kernel, count_x), [struct(14, 8, Z0), struct(14, 8, Z0)], [], 8
    )(*operands)


def coarse_kernel(
    count_x, count_y, all_ref, v3,
    c3, wx3, wy3, wz3, d3, q3, b3, w3, thin3,
    c4, wx4, wy4, wz4, d4, q4, g4, v4, w4, thin4,
):
    n3, n4 = 2 * count_x, count_x

    c3[...] = jnp.zeros(c3.shape, F32)
    b3[...] = jnp.zeros(b3.shape, F32)
    v3[...] = jnp.zeros(v3.shape, F32)
    w3[...] = jnp.zeros(w3.shape, F32)
    lane = iota((count_y, LANES), 1) < 64
    for i in range(n3):
        base = (i // 2) * count_y * 4 + 2 * (i % 2)
        for j in range(2):
            part = all_ref[pl.ds(base + j, count_y, stride=4), :]
            b3[1 + i, pl.ds(j, count_y, stride=2), :] = jnp.where(lane, part, 0.0)
            c3[1 + i, pl.ds(j, count_y, stride=2), :] = jnp.where(lane, pltpu.roll(part, 64, 1), 0.0)
    in_y = jnp.logical_and(iota((Y3, LANES), 0) < 2 * count_y, iota((Y3, LANES), 1) < 64).astype(F32)
    make_faces(c3, wx3, wy3, wz3, d3, q3, 1, n3 + 1, lambda i: 1.0, in_y, 8, whole_y=1)

    def begin3(i):
        return [(v3, i, q3[i] * b3[i])]

    loop(1, n3 + 1, begin3, 8)

    def sweep3(i):
        here, total = neighbours(v3, wx3, wy3, wz3, i)
        return [(w3, i, 0.2 * here + q3[i] * (b3[i] + total))]

    loop(1, n3 + 1, sweep3, 8)

    def restrict3(j):
        i = 2 * j + 1
        both = defect(w3, b3, wx3, wy3, wz3, d3, i) + defect(w3, b3, wx3, wy3, wz3, d3, i + 1)
        return [(thin3, j, both)]

    loop(0, n4, restrict3, 4)
    valid = iota((Y4, LANES), 0) < count_y
    rows = jnp.concatenate(
        [thin3[i, pl.ds(0, Y4, stride=2), :] + thin3[i, pl.ds(1, Y4, stride=2), :] for i in range(n4)], axis=0
    )
    pick = pair_sum_matrix(LANES, LANES)
    g4[...] = (0.5 * split_dot(rows, pick)).reshape(n4, Y4, LANES)
    for i in range(n4):
        thin3[i] = c3[2 * i + 1] + c3[2 * i + 2]
    rows = jnp.concatenate(
        [thin3[i, pl.ds(0, Y4, stride=2), :] + thin3[i, pl.ds(1, Y4, stride=2), :] for i in range(n4)], axis=0
    )
    c4[...] = jnp.zeros(c4.shape, F32)
    c4[1 : n4 + 1] = (0.125 * split_dot(rows, pick)).reshape(n4, Y4, LANES)
    in_y = jnp.logical_and(valid, iota((Y4, LANES), 1) < 32).astype(F32)
    make_faces(c4, wx4, wy4, wz4, d4, q4, 1, n4 + 1, lambda i: 1.0, in_y, n4, whole_y=1)
    v4[...] = jnp.zeros(v4.shape, F32)
    w4[...] = jnp.zeros(w4.shape, F32)
    for i in range(n4):
        g4[i] = q4[1 + i] * g4[i]
        v4[1 + i] = g4[i]

    def bottom(source, target):
        def body(i):
            here, total = neighbours(source, wx4, wy4, wz4, 1 + i)
            return [(target, 1 + i, (0.2 * here + g4[i]) + q4[1 + i] * total)]

        loop(0, n4, body, n4)

    def two(step):
        bottom(v4, w4)
        bottom(w4, v4)
        return []

    loop(0, (BOTTOM - 2) // 2, two)
    bottom(v4, w4)

    wide = split_dot(w4[1 : n4 + 1].reshape(n4 * Y4, LANES), copy_matrix(LANES, LANES)).reshape(n4, Y4, LANES)
    for i in range(n4):
        thin4[pl.ds(0, Y4, stride=2), :] = wide[i]
        thin4[pl.ds(1, Y4, stride=2), :] = wide[i]
        extra = thin4[...]
        v3[1 + 2 * i] = w3[1 + 2 * i] + extra
        v3[2 + 2 * i] = w3[2 + 2 * i] + extra

    loop(1, n3 + 1, sweep3, 8)

    def sweep3_again(i):
        here, total = neighbours(w3, wx3, wy3, wz3, i)
        return [(v3, i, 0.2 * here + q3[i] * (b3[i] + total))]

    loop(1, n3 + 1, sweep3_again, 8)


def coarse(count_x, count_y, everything):
    frame3, frame4 = (2 * count_x + 2, Y3, LANES), (count_x + 2, Y4, LANES)
    return call(
        functools.partial(coarse_kernel, count_x, count_y),
        struct(*frame3),
        [vmem(*frame3)] * 8 + [vmem(count_x, Y3, LANES)]
        + [vmem(*frame4)] * 6 + [vmem(count_x, Y4, LANES)] + [vmem(*frame4)] * 2 + [vmem(Y3, LANES)],
        8,
        flops=20000000,
        bytes_accessed=10000000,
    )(everything)


def up_kernel(
    count_x, count_y,
    v3, wx2, wy2, wz2, q2, own2, low_ref, high_ref, below_ref, above_ref, v_own, v1_ref,
    g1_mid, g1_below, g1_above, c1_ref, c_ref, g_ref, low0, high0, below0, above0,
    solution_ref, residual_ref,
    v2, w2, b2, v1, b1, c1, wx1, wy1, wz1, d1, q1, w1, spread1,
    c0, wx0, wy0, wz0, d0, q0, b0, v0, w0, spread0,
):
    place_x, place_y = lax.axis_index("gx"), lax.axis_index("gy")
    n3 = 2 * count_x
    sides = ends("gx", count_x) + ends("gy", count_y)
    first, last, low_y, high_y = sides

    fill_c1(c1, c1_ref, low0, high0, below0, above0, *sides)
    fill_g1(w1, g1_mid, g1_below, g1_above, low_y, high_y)
    in_y = inside((Y1, Z1), 0, place_y * 8 - OY1, 8 * count_y).astype(F32)
    make_faces(
        c1, wx1, wy1, wz1, d1, q1, 5, X1 - 5, lambda i: flag(place_x * 8 - OX1 + i, 8 * count_x), in_y, 2
    )

    def begin1(i):
        return [(b1, i, q1[i] * w1[i])]

    loop(5, X1 - 5, begin1, 2)
    window0(low0, high0, below0, above0, c_ref, g_ref, *sides)(c0, w0)
    in_y = inside((Y0, Z0), 0, place_y * 16 - OY0, 16 * count_y).astype(F32)
    make_faces(
        c0, wx0, wy0, wz0, d0, q0, 1, X0 - 1, lambda i: flag(place_x * 16 - OX0 + i, 16 * count_x), in_y, 1
    )

    def begin0(i):
        return [(b0, i, q0[i] * w0[i])]

    loop(1, X0 - 1, begin0, 2)

    slabs = []
    for j in range(6):
        at = 2 * place_x - 2 + j
        slabs.append(v3[1 + jnp.clip(at, 0, n3 - 1)] * flag(at, n3))
    wide = split_dot(jnp.concatenate(slabs, axis=0), copy_matrix(LANES, LANES))
    target, origin = iota((Y2, Y3), 0), iota((Y2, Y3), 1)
    rows = jnp.logical_and(origin == 2 * place_y - 2 + target // 2, target < 12).astype(F32).astype(BF16)
    half = iota((8, Z2), 0) < 4
    for j in range(6):
        extra = split_dot_left(rows, wide[Y3 * j : Y3 * j + Y3])
        for k in range(2):
            i = 2 * j + k
            at = slice(LANES * (i % 4), LANES * (i % 4) + LANES)
            mid = own2[:, at] if i // 4 == 1 else low_ref[6, :, at] * first if i < 4 else high_ref[6, :, at] * last
            below = below_ref[11 + i // 4, :, at] * low_y
            above = above_ref[11 + i // 4, :, at] * high_y
            v2[i, 0:8] = jnp.where(half, below, pltpu.roll(mid, 4, 0)) + extra[0:8]
            v2[i, 8:16] = jnp.where(half, above, 0.0) + extra[8:16]
            b2[i, 0:8] = jnp.where(half, pltpu.roll(below, 4, 0), mid)
            b2[i, 8:16] = jnp.where(half, pltpu.roll(above, 4, 0), 0.0)
    for i in range(1, X2 - 1):
        b2[i] = q2[i] * b2[i]
    sweep(v2, w2, b2, wx2, wy2, wz2, q2, 1, X2 - 1, 10)
    sweep(w2, v2, b2, wx2, wy2, wz2, q2, 2, X2 - 2, 8)

    wide = split_dot(v2[2:10].reshape(8 * Y2, Z2), copy_matrix(Z2, Z1)).reshape(8, Y2, Z1)
    spread1[...] = jnp.zeros(spread1.shape, F32)
    for j in range(8):
        extra = double_rows(spread1, wide[j, 2:10], 4)
        for k in range(2):
            i = 4 + 2 * j + k
            v1[i] = v1_ref[i - 4] + extra
    sweep(v1, w1, b1, wx1, wy1, wz1, q1, 5, X1 - 5, 3)
    sweep(w1, v1, b1, wx1, wy1, wz1, q1, 6, X1 - 6, 3)

    wide = split_dot(v1[6:18].reshape(12 * Y1, Z1), copy_matrix(Z1, Z0)).reshape(12, Y1, Z0)
    half = iota((8, Z0), 0) < 4
    for j in range(12):
        extra = double_rows(spread0, wide[j, 6:18], 0)
        for k in range(2):
            i = 2 * j - 1 + k
            if i < 0 or i >= X0:
                continue
            if i < 3:
                own = [low_ref[2 * i + side] * first for side in range(2)]
            elif i < 19:
                own = [v_own[i - 3, 8 * side : 8 * side + 8, :] for side in range(2)]
            else:
                own = [high_ref[2 * (i - 19) + side] * last for side in range(2)]
            below, above = below_ref[i // 2] * low_y, above_ref[i // 2] * high_y
            if i % 2:
                below = pltpu.roll(below, 4, 0)
            else:
                above = pltpu.roll(above, 4, 0)
            head, tail = pltpu.roll(own[0], 4, 0), pltpu.roll(own[1], 4, 0)
            v0[i, 0:8] = jnp.where(half, below, head) + extra[0:8]
            v0[i, 8:16] = jnp.where(half, head, tail) + extra[8:16]
            v0[i, 16:24] = jnp.where(half, tail, above) + extra[16:24]
    sweep(v0, w0, b0, wx0, wy0, wz0, q0, 1, X0 - 1, 2)
    sweep(w0, v0, b0, wx0, wy0, wz0, q0, 2, X0 - 2, 2)

    def finish(i):
        here, total = neighbours(v0, wx0, wy0, wz0, i + OX0)
        left = pltpu.roll(total - d0[i + OX0] * here, Y0 - OY0, 0)[0:16]
        return [(solution_ref, i, pltpu.roll(here, Y0 - OY0, 0)[0:16]), (residual_ref, i, g_ref[i] + left)]

    loop(0, 16, finish, 2)


def up(count_x, count_y, *operands):
    frame0, frame1, frame2 = (X0, Y0, Z0), (X1, Y1, Z1), (X2, Y2, Z2)
    return call(
        functools.partial(up_kernel, count_x, count_y),
        [struct(16, 16, Z0), struct(16, 16, Z0)],
        [vmem(*frame2)] * 3 + [vmem(*frame1)] * 9 + [vmem(Z1 // LANES, Y1, LANES)]
        + [vmem(*frame0)] * 9 + [vmem(Z0 // LANES, Y0, LANES)],
        24,
    )(*operands)


def to_next(cells, axis):
    count = lax.axis_size(axis)
    return lax.ppermute(cells, axis, [(i, (i + 1) % count) for i in range(count)])


def to_previous(cells, axis):
    count = lax.axis_size(axis)
    return lax.ppermute(cells, axis, [((i + 1) % count, i) for i in range(count)])


def shards(right_side, coefficient):
    count_x, count_y = lax.axis_size("gx"), lax.axis_size("gy")
    place_x = lax.axis_index("gx")

    def with_sides(low, cells, high):
        low = jnp.where(place_x > 0, low, 0.0)
        high = jnp.where(place_x < count_x - 1, high, 0.0)
        return jnp.concatenate([low, cells, high], axis=0)

    to_right, to_left, c1 = begin(coefficient, right_side)
    low, high = to_next(to_right, "gx"), to_previous(to_left, "gx")
    top, bottom = edges_y(count_x, coefficient, right_side, c1, low, high)
    below, above = to_next(top, "gy"), to_previous(bottom, "gy")
    g1, v_own = down0(count_x, count_y, coefficient, right_side, low, high, below, above)

    g1_low, g1_high = to_next(g1[2:8], "gx"), to_previous(g1[0:6], "gx")
    levels = prepare(count_x, count_y, c1, low, high, below, above)
    wx2, wy2, wz2, q2 = levels[5], levels[6], levels[7], levels[9]
    g1_mid = with_sides(g1_low, g1, g1_high)
    g1_below, g1_above = to_next(g1_mid, "gy"), to_previous(g1_mid, "gy")
    v1, to_right, to_left, own2, send3 = down1(count_x, count_y, v_own, g1_mid, g1_below, g1_above, *levels)

    low2, high2 = to_next(to_right, "gx"), to_previous(to_left, "gx")
    everything = lax.all_to_all(send3, ("gx", "gy"), split_axis=0, concat_axis=0, tiled=True)
    top, bottom = iterate_edges(count_x, v_own, own2, low2, high2)
    below2, above2 = to_next(top, "gy"), to_previous(bottom, "gy")
    v3 = coarse(count_x, count_y, everything)
    return tuple(
        up(
            count_x, count_y, v3, wx2, wy2, wz2, q2, own2, low2, high2, below2, above2, v_own, v1,
            g1_mid, g1_below, g1_above, c1, coefficient, right_side, low, high, below, above,
        )
    )


def solution(mesh):
    specs = (P("gx", "gy", None), P("gx", "gy", None))
    return jax.shard_map(shards, mesh=mesh, in_specs=specs, out_specs=specs, check_vma=False)
```

```python
import functools

import jax
import jax.numpy as jnp
from jax import lax
from jax.experimental import pallas as pl
from jax.experimental.pallas import tpu as pltpu
from jax.sharding import PartitionSpec as P

F32 = jnp.float32
BF16 = jnp.bfloat16
OMEGA = 0.8
BOTTOM = 16
MIB = 1024 * 1024

X0, Y0, Z0, OX0, OY0 = 22, 24, 512, 3, 4
X1, Y1, Z1, OX1, OY1 = 24, 24, 256, 8, 8
X2, Y2, Z2, OX2, OY2 = 12, 16, 128, 4, 4
Y3, Y4, LANES = 16, 8, 128
C_TILES, CG_TILES = 11, 16


def iota(shape, dim):
    return lax.broadcasted_iota(jnp.int32, shape, dim)


def up_of(cells, dim):
    if dim == 0 or cells.shape[1] == LANES:
        return pltpu.roll(cells, cells.shape[dim] - 1, dim)
    return jnp.concatenate([cells[:, LANES:], pltpu.roll(cells[:, :LANES], LANES - 1, 1)], axis=1)


def down_of(cells, dim):
    if dim == 0 or cells.shape[1] == LANES:
        return pltpu.roll(cells, 1, dim)
    return jnp.concatenate([pltpu.roll(cells[:, -LANES:], 1, 1), cells[:, :-LANES]], axis=1)


def cell_of(position, count):
    pieces = count // LANES
    return pieces * (position % LANES) + position // LANES


def deal_matrix(count):
    hit = iota((count, count), 0) == cell_of(iota((count, count), 1), count)
    return hit.astype(F32).astype(BF16)


def collect_matrix(count):
    hit = cell_of(iota((count, count), 0), count) == iota((count, count), 1)
    return hit.astype(F32).astype(BF16)


def pair_sums(cells):
    pieces = [lanes(cells, k) for k in range(cells.shape[1] // LANES)]
    sums = [even + odd for even, odd in zip(pieces[::2], pieces[1::2])]
    return jnp.concatenate(sums, axis=1) if len(sums) > 1 else sums[0]


def split_dot(cells, pick):
    high = cells.astype(BF16)
    rest = cells - high.astype(F32)
    mid = rest.astype(BF16)
    low = (rest - mid.astype(F32)).astype(BF16)
    dot = functools.partial(jnp.dot, preferred_element_type=F32)
    return dot(high, pick) + (dot(mid, pick) + dot(low, pick))


def split_dot_left(pick, cells):
    high = cells.astype(BF16)
    rest = cells - high.astype(F32)
    mid = rest.astype(BF16)
    low = (rest - mid.astype(F32)).astype(BF16)
    dot = functools.partial(jnp.dot, preferred_element_type=F32)
    return dot(pick, high) + (dot(pick, mid) + dot(pick, low))


def pair_sum_matrix(fine, coarse, offset=0):
    hit = (iota((fine, coarse), 0) // 2) + offset == iota((fine, coarse), 1)
    return hit.astype(F32).astype(BF16)


def pair_deal_matrix(fine, coarse):
    hit = iota((fine, coarse), 0) // 2 == cell_of(iota((fine, coarse), 1), coarse)
    return hit.astype(F32).astype(BF16)


def copy_matrix(coarse, fine):
    hit = iota((coarse, fine), 0) == iota((coarse, fine), 1) // 2
    return hit.astype(F32).astype(BF16)


def inside(shape, dim, start, count):
    place = iota(shape, dim) + start
    return jnp.logical_and(place >= 0, place < count)


def flag(start, count):
    return jnp.where(jnp.logical_and(start >= 0, start < count), 1.0, 0.0).astype(F32)


def loop(first, last, body, width=1):
    def run(i, count):
        stores = [store for j in range(count) for store in body(i + j)]
        for ref, at, value in stores:
            ref[at] = value

    count = (last - first) // width

    def step(t, carry):
        run(first + t * width, width)
        return carry

    if count == 1:
        run(first, width)
    else:
        lax.fori_loop(0, count, step, 0)
    if (last - first) % width:
        run(first + count * width, (last - first) % width)


def inverse(total):
    total = jnp.maximum(total, 1e-30)
    guess = pl.reciprocal(total, approx=True)
    guess = guess * (2.0 - total * guess)
    return guess * (2.0 - total * guess)


def make_faces(c, wx, wy, wz, d, q, first, last, in_x, in_y, width, whole_y=0):
    rows, cells = c.shape[1], c.shape[2]
    end_z = iota((rows, cells), 1) == cells - 1
    start_z = iota((rows, cells), 1) == 0
    row = iota((rows, cells), 0)
    wx[first - 1] = 0.5 * (c[first - 1] + c[first])

    def body(i):
        here = c[i]
        after = c[i + 1]
        before = c[i - 1]
        y_up, y_down = up_of(here, 0), down_of(here, 0)
        if whole_y:
            y_up = jnp.where(row == rows - 1, 0.0, y_up)
            y_down = jnp.where(row == 0, 0.0, y_down)
        z_up = jnp.where(end_z, 0.0, up_of(here, 1))
        z_down = jnp.where(start_z, 0.0, down_of(here, 1))
        side = 0.5 * (here + y_up)
        side = jnp.where(row == rows - 1, 0.0, side) if whole_y else side
        total = 3.0 * here + 0.5 * ((after + before) + (y_up + y_down) + (z_up + z_down))
        return [
            (wx, i, 0.5 * (here + after)),
            (wy, i, side),
            (wz, i, jnp.where(end_z, 0.0, 0.5 * (here + z_up))),
            (d, i, total),
            (q, i, (in_y * (OMEGA * in_x(i))) * inverse(total)),
        ]

    loop(first, last, body, width)


def neighbours(v, wx, wy, wz, i):
    here = v[i]
    side_y, side_z = wy[i], wz[i]
    along_x = wx[i] * v[i + 1] + wx[i - 1] * v[i - 1]
    along_y = side_y * up_of(here, 0) + down_of(side_y * here, 0)
    along_z = side_z * up_of(here, 1) + down_of(side_z * here, 1)
    return here, along_x + along_y + along_z


def sweep(v, out, b, wx, wy, wz, q, first, last, width):
    def body(i):
        here, total = neighbours(v, wx, wy, wz, i)
        return [(out, i, (0.2 * here + b[i]) + q[i] * total)]

    loop(first, last, body, width)


def defect(v, source, wx, wy, wz, d, i):
    here, total = neighbours(v, wx, wy, wz, i)
    return (source[i] - d[i] * here) + total


def lanes(cells, k):
    return cells[:, LANES * k : LANES * k + LANES]


def keep(scratch, j, cells):
    for k in range(cells.shape[1] // LANES):
        scratch[j, k] = lanes(cells, k)


def halve_rows(scratch, j, start, count):
    parts = [
        scratch[j, k, pl.ds(start, count, stride=2), :] + scratch[j, k, pl.ds(start + 1, count, stride=2), :]
        for k in range(scratch.shape[1])
    ]
    return jnp.concatenate(parts, axis=1)


def double_rows(scratch, cells, start):
    for k in range(scratch.shape[0]):
        for odd in range(2):
            scratch[k, pl.ds(start + odd, cells.shape[0], stride=2), :] = lanes(cells, k)
    return jnp.concatenate([scratch[k] for k in range(scratch.shape[0])], axis=1)


def call(kernel, out_shape, scratch, limit, in_specs=None, out_specs=None, flops=1000000, bytes_accessed=1000000):
    extra = {}
    if in_specs is not None:
        extra["in_specs"] = in_specs
    if out_specs is not None:
        extra["out_specs"] = out_specs
    return pl.pallas_call(
        kernel,
        out_shape=out_shape,
        scratch_shapes=scratch,
        compiler_params=pltpu.CompilerParams(vmem_limit_bytes=limit * MIB),
        cost_estimate=pl.CostEstimate(flops=flops, bytes_accessed=bytes_accessed, transcendentals=0),
        **extra,
    )


def struct(*shape):
    return jax.ShapeDtypeStruct(shape, F32)


def vmem(*shape):
    return pltpu.VMEM(shape, F32)


WHOLE = pl.BlockSpec(memory_space=pltpu.VMEM)
FAR = pl.BlockSpec(memory_space=pl.ANY)
FAR_COUNT = 26


def start_copies(sources, targets, sems, first):
    copies = [
        pltpu.make_async_copy(source, target, sems.at[first + k])
        for k, (source, target) in enumerate(zip(sources, targets))
    ]
    for copy in copies:
        copy.start()
    return copies


def wait_copies(copies):
    for copy in copies:
        copy.wait()


def place_of(i):
    row, cell = 8 * ((i // 2) % 2), Z1 * (i % 2)
    return 5 + i // 4, slice(row, row + 8), slice(cell, cell + Z1)


def begin_kernel(c_ref, g_ref, next_ref, previous_ref, c1_ref, pairs):
    for i in range(8):
        keep(pairs, i, c_ref[2 * i] + c_ref[2 * i + 1])
    for i in range(3):
        next_ref[i] = c_ref[13 + i]
        previous_ref[i] = c_ref[i]
    for i in range(2):
        next_ref[3 + i] = g_ref[14 + i]
        previous_ref[3 + i] = g_ref[i]
    rows = jnp.concatenate([halve_rows(pairs, i, 0, 8) for i in range(8)], axis=0)
    small = 0.125 * split_dot(rows, pair_deal_matrix(Z0, Z1))
    for i in range(8):
        block = small[8 * i : 8 * i + 8]
        c1_ref[i] = block
        next_ref[place_of(i)] = block
        previous_ref[place_of(i)] = block


def begin(coefficient, right_side):
    return call(
        begin_kernel, [struct(7, 16, Z0), struct(7, 16, Z0), struct(8, 8, Z1)], [vmem(8, Z0 // LANES, 16, LANES)], 8
    )(coefficient, right_side)


def deal_kernel(c_ref, g_ref, c_out, g_out):
    pick = deal_matrix(Z0)
    for ref, out in ((c_ref, c_out), (g_ref, g_out)):
        out[...] = split_dot(ref[...].reshape(256, Z0), pick).reshape(16, 16, Z0)


def deal(coefficient, right_side):
    return call(deal_kernel, [struct(16, 16, Z0), struct(16, 16, Z0)], [], 8)(coefficient, right_side)


def edge_kernel(count_x, c_ref, g_ref, c1_ref, low_raw, high_raw, top_ref, bottom_ref, low_ref, high_ref):
    pick = deal_matrix(Z0)
    for raw, out in ((low_raw, low_ref), (high_raw, high_ref)):
        out[0:5] = split_dot(raw[0:5].reshape(80, Z0), pick).reshape(5, 16, Z0)
        out[5:7] = raw[5:7]
    place = lax.axis_index("gx")
    first = jnp.where(place > 0, 1.0, 0.0).astype(F32)
    last = jnp.where(place < count_x - 1, 1.0, 0.0).astype(F32)
    row = iota((8, Z0), 0)

    def c_part(i, half):
        rows = slice(8 * half, 8 * half + 8)
        if i < 3:
            return low_ref[i, rows, :] * first
        return c_ref[i - 3, rows, :] if i < 19 else high_ref[i - 19, rows, :] * last

    def g_part(i, half):
        rows = slice(8 * half, 8 * half + 8)
        if i < 3:
            return low_ref[i + 2, rows, :] * first
        return g_ref[i - 3, rows, :] if i < 19 else high_ref[i - 16, rows, :] * last

    for j in range(X0 // 2):
        top_ref[j] = jnp.where(row < 4, pltpu.roll(c_part(2 * j, 1), 4, 0), c_part(2 * j + 1, 1))
        bottom_ref[j] = jnp.where(row < 4, c_part(2 * j, 0), pltpu.roll(c_part(2 * j + 1, 0), 4, 0))
    for j in range(5):
        top, bottom = g_part(1 + 4 * j, 1), g_part(1 + 4 * j, 0)
        top = pltpu.roll(top, 2, 0)
        for k in range(1, 4):
            part = g_part(1 + 4 * j + k, 1)
            part = pltpu.roll(part, (2 * k + 2) % 8, 0) if k < 3 else part
            top = jnp.where(row // 2 == k, part, top)
            bottom = jnp.where(row // 2 == k, pltpu.roll(g_part(1 + 4 * j + k, 0), 2 * k, 0), bottom)
        top_ref[C_TILES + j] = top
        bottom_ref[C_TILES + j] = bottom
    for i in range(24):
        part = low_ref[place_of(i)] * first if i < 8 else c1_ref[i - 8] if i < 16 else high_ref[place_of(i - 16)] * last
        for ref in (top_ref, bottom_ref):
            ref[CG_TILES + i // 2, :, Z1 * (i % 2) : Z1 * (i % 2) + Z1] = part


def edges_y(count_x, *operands):
    return call(
        functools.partial(edge_kernel, count_x), [struct(CG_TILES + 12, 8, Z0)] * 2 + [struct(7, 16, Z0)] * 2, [], 8
    )(*operands)


def ends(axis, count):
    place = lax.axis_index(axis)
    low = jnp.where(place > 0, 1.0, 0.0).astype(F32)
    return low, jnp.where(place < count - 1, 1.0, 0.0).astype(F32)


def window0(low_ref, high_ref, below_ref, above_ref, c_ref, g_ref, first, last, low_y, high_y):
    row = iota((8, Z0), 0) < 4

    def put(own, below, above):
        head, tail = pltpu.roll(own[0:8], 4, 0), pltpu.roll(own[8:16], 4, 0)
        parts = [jnp.where(row, below, head), jnp.where(row, head, tail), jnp.where(row, tail, above)]
        return jnp.concatenate(parts, axis=0)

    def turn(cells, rows):
        return pltpu.roll(cells, rows % 8, 0) if rows % 8 else cells

    def c_slab(i, own):
        odd = i % 2
        below = turn(below_ref[i // 2], 4 * odd) * low_y
        return put(own, below, turn(above_ref[i // 2], 4 - 4 * odd) * high_y)

    def g_slab(i, own):
        tile, k = C_TILES + (i - 1) // 4, (i - 1) % 4
        below = turn(below_ref[tile], 2 - 2 * k) * low_y
        return put(own, below, turn(above_ref[tile], 4 - 2 * k) * high_y)

    def fill(c, g):
        for i in range(3):
            c[i] = c_slab(i, low_ref[i] * first)
            c[19 + i] = c_slab(19 + i, high_ref[i] * last)
        for i in range(3, 19):
            c[i] = c_slab(i, c_ref[i - 3])
        for i in (1, 2):
            g[i] = g_slab(i, low_ref[i + 2] * first)
            g[18 + i] = g_slab(18 + i, high_ref[i + 2] * last)
        for i in range(3, 19):
            g[i] = g_slab(i, g_ref[i - 3])

    return fill


def down0_kernel(
    count_x, count_y,
    c_ref, g_ref, low_ref, high_ref, below_ref, above_ref,
    g1_ref, v_own_ref, c, g, wx, wy, wz, d, q, b, v, pairs,
):
    place_x, place_y = lax.axis_index("gx"), lax.axis_index("gy")
    sides = ends("gx", count_x) + ends("gy", count_y)
    window0(low_ref, high_ref, below_ref, above_ref, c_ref, g_ref, *sides)(c, g)
    in_y = inside((Y0, Z0), 0, place_y * 16 - OY0, 16 * count_y).astype(F32)
    make_faces(
        c, wx, wy, wz, d, q, 1, X0 - 1, lambda i: flag(place_x * 16 - OX0 + i, 16 * count_x), in_y, 2
    )

    def begin(i):
        return [(b, i, q[i] * g[i])]

    loop(1, X0 - 1, begin, 2)
    sweep(b, v, b, wx, wy, wz, q, 2, X0 - 2, 3)

    def own_of(i):
        return [(v_own_ref, i, pltpu.roll(v[i + 3], Y0 - OY0, 0)[0:16])]

    loop(0, 16, own_of, 2)

    def restrict(j):
        i = 2 * j + OX0
        both = defect(v, g, wx, wy, wz, d, i) + defect(v, g, wx, wy, wz, d, i + 1)
        return [(pairs, (j, k), lanes(both, k)) for k in range(Z0 // LANES)]

    loop(0, 8, restrict)
    rows = jnp.concatenate([halve_rows(pairs, i, 4, 8) for i in range(8)], axis=0)
    g1_ref[...] = (0.5 * pair_sums(rows)).reshape(8, 8, Z1)


def down0(count_x, count_y, *operands):
    frame = (X0, Y0, Z0)
    return call(
        functools.partial(down0_kernel, count_x, count_y),
        [struct(8, 8, Z1), struct(16, 16, Z0)],
        [vmem(*frame)] * 9 + [vmem(8, Z0 // LANES, Y0, LANES)],
        18,
    )(*operands)


def fill_c1(c1, c1_ref, low_ref, high_ref, below_ref, above_ref, first, last, low_y, high_y):
    for i in range(24):
        at = CG_TILES + i // 2, slice(0, 8), slice(Z1 * (i % 2), Z1 * (i % 2) + Z1)
        part = low_ref[place_of(i)] * first if i < 8 else c1_ref[i - 8] if i < 16 else high_ref[place_of(i - 16)] * last
        c1[i, 0:8, :] = below_ref[at] * low_y
        c1[i, 8:16, :] = part
        c1[i, 16:24, :] = above_ref[at] * high_y


def prepare_kernel(
    count_x, count_y, c1_ref, low_ref, high_ref, below_ref, above_ref,
    wx1, wy1, wz1, d1, q1, wx2, wy2, wz2, d2, q2, c3_ref, c1, c2, pairs,
):
    place_x, place_y = lax.axis_index("gx"), lax.axis_index("gy")
    sides = ends("gx", count_x) + ends("gy", count_y)
    fill_c1(c1, c1_ref, low_ref, high_ref, below_ref, above_ref, *sides)
    in_y = inside((Y1, Z1), 0, place_y * 8 - OY1, 8 * count_y).astype(F32)
    make_faces(
        c1, wx1, wy1, wz1, d1, q1, 2, X1 - 2, lambda i: flag(place_x * 8 - OX1 + i, 8 * count_x), in_y, 2
    )
    for i in range(12):
        keep(pairs, i, c1[2 * i] + c1[2 * i + 1])
    blank = jnp.zeros((4, Z1), F32)
    rows = []
    for i in range(12):
        rows.append(halve_rows(pairs, i, 0, 12))
        rows.append(blank)
    c2[...] = (0.125 * pair_sums(jnp.concatenate(rows, axis=0))).reshape(X2, Y2, Z2)
    in_y = inside((Y2, Z2), 0, place_y * 4 - OY2, 4 * count_y).astype(F32)
    make_faces(
        c2, wx2, wy2, wz2, d2, q2, 1, X2 - 1, lambda i: flag(place_x * 4 - OX2 + i, 4 * count_x), in_y, 10
    )
    rows = jnp.concatenate([c2[4] + c2[5], c2[6] + c2[7]], axis=0)
    thin = 0.125 * split_dot(rows, pair_sum_matrix(Z2, LANES, 64))
    row = iota((8, LANES), 0)
    c3 = jnp.zeros((8, LANES), F32)
    for i in range(2):
        for j in range(2):
            at = 16 * i + 4 + 2 * j
            both = thin[at : at + 1] + thin[at + 1 : at + 2]
            c3 = jnp.where(row == 2 * i + j, jnp.broadcast_to(both, (8, LANES)), c3)
    c3_ref[...] = c3


def prepare(count_x, count_y, *operands):
    frame1, frame2 = (X1, Y1, Z1), (X2, Y2, Z2)
    return call(
        functools.partial(prepare_kernel, count_x, count_y),
        [struct(*frame1)] * 5 + [struct(*frame2)] * 5 + [struct(8, LANES)],
        [vmem(*frame1), vmem(*frame2), vmem(12, Z1 // LANES, Y1, LANES)],
        8,
    )(*operands)


def fill_g1(g1, mid_ref, below_ref, above_ref, low_y, high_y):
    g1[2:22, 0:8, :] = below_ref[...] * low_y
    g1[2:22, 8:16, :] = mid_ref[...]
    g1[2:22, 16:24, :] = above_ref[...] * high_y


def down1_kernel(
    count_x, count_y, v_own_ref, mid_ref, below_ref, above_ref,
    wx1, wy1, wz1, d1, q1, wx2, wy2, wz2, d2, q2, c3_ref,
    v_far, next_ref, previous_ref, send2_ref, send3_ref, v1_ref, b1_ref, g1, g2, b2, v2, pairs, thin,
):
    place_y = lax.axis_index("gy")
    low_y = jnp.where(place_y > 0, 1.0, 0.0).astype(F32)
    high_y = jnp.where(place_y < count_y - 1, 1.0, 0.0).astype(F32)
    fill_g1(g1, mid_ref, below_ref, above_ref, low_y, high_y)

    def begin1(i):
        return [(b1_ref, i, q1[i] * g1[i])]

    loop(2, X1 - 2, begin1, 4)
    sweep(b1_ref, v1_ref, b1_ref, wx1, wy1, wz1, q1, 3, X1 - 3, 3)

    def restrict(j):
        i = 2 * j + 4
        after = defect(v1_ref, g1, wx1, wy1, wz1, d1, i + 1)
        both = defect(v1_ref, g1, wx1, wy1, wz1, d1, i) + after
        return [(pairs, (j, k), lanes(both, k)) for k in range(Z1 // LANES)]

    loop(0, 8, restrict, 2)
    rows = jnp.concatenate([halve_rows(pairs, i, 4, 8) for i in range(8)], axis=0)
    small = 0.5 * pair_sums(rows)
    g2[...] = jnp.zeros((X2, Y2, Z2), F32)
    for i in range(8):
        g2[2 + i, 2:10, :] = small[8 * i : 8 * i + 8]
    for i in range(2, X2 - 2):
        b2[i] = q2[i] * g2[i]
    sweep(b2, v2, b2, wx2, wy2, wz2, q2, 3, X2 - 3, 6)
    row = iota((8, Z2), 0) < 4
    for i in range(4):
        both = jnp.where(row, pltpu.roll(v2[4 + i, 0:8, :], 4, 0), g2[4 + i, 0:8, :])
        send2_ref[:, LANES * i : LANES * i + LANES] = both
        next_ref[6, :, LANES * i : LANES * i + LANES] = both
        previous_ref[6, :, LANES * i : LANES * i + LANES] = both
    for i in range(3):
        for half in range(2):
            next_ref[2 * i + half] = v_own_ref[13 + i, 8 * half : 8 * half + 8, :]
            previous_ref[2 * i + half] = v_own_ref[i, 8 * half : 8 * half + 8, :]
    halves = [
        defect(v2, g2, wx2, wy2, wz2, d2, 4 + 2 * i) + defect(v2, g2, wx2, wy2, wz2, d2, 5 + 2 * i)
        for i in range(2)
    ]
    thin[...] = 0.5 * split_dot(jnp.concatenate(halves, axis=0), pair_sum_matrix(Z2, LANES))
    row = iota((8, LANES), 0)
    source = jnp.zeros((8, LANES), F32)
    for i in range(2):
        for j in range(2):
            at = 16 * i + 4 + 2 * j
            both = thin[at : at + 1, :] + thin[at + 1 : at + 2, :]
            source = jnp.where(row == 2 * i + j, jnp.broadcast_to(both, (8, LANES)), source)
    source = source + c3_ref[...]
    double = jnp.where(row < 4, source, pltpu.roll(source, 4, 0))
    for i in range(count_x * count_y // 2):
        send3_ref[8 * i : 8 * i + 8, :] = double
    v_far[...] = v1_ref[4:20]


def down1(count_x, count_y, *operands):
    frame1, frame2 = (X1, Y1, Z1), (X2, Y2, Z2)
    return call(
        functools.partial(down1_kernel, count_x, count_y),
        [struct(16, Y1, Z1), struct(7, 8, Z0), struct(7, 8, Z0), struct(8, Z0)]
        + [struct(4 * count_x * count_y, LANES)],
        [vmem(*frame1)] * 3 + [vmem(*frame2)] * 3 + [vmem(8, Z1 // LANES, Y1, LANES), vmem(32, LANES)],
        8,
    )(*operands)


def iterate_edge_kernel(count_x, own_ref, own2_ref, low_ref, high_ref, top_ref, bottom_ref):
    place = lax.axis_index("gx")
    first = jnp.where(place > 0, 1.0, 0.0).astype(F32)
    last = jnp.where(place < count_x - 1, 1.0, 0.0).astype(F32)
    row = iota((8, Z0), 0) < 4

    def slab(i, half):
        if i < 3:
            return low_ref[2 * i + half] * first
        if i < 19:
            return own_ref[i - 3, 8 * half : 8 * half + 8, :]
        return high_ref[2 * (i - 19) + half] * last

    for j in range(X0 // 2):
        top_ref[j] = jnp.where(row, pltpu.roll(slab(2 * j, 1), 4, 0), slab(2 * j + 1, 1))
        bottom_ref[j] = jnp.where(row, slab(2 * j, 0), pltpu.roll(slab(2 * j + 1, 0), 4, 0))
    for ref in (top_ref, bottom_ref):
        ref[11] = low_ref[6] * first
        ref[12] = own2_ref[...]
        ref[13] = high_ref[6] * last


def iterate_edges(count_x, *operands):
    return call(
        functools.partial(iterate_edge_kernel, count_x), [struct(14, 8, Z0), struct(14, 8, Z0)], [], 8
    )(*operands)


def weights0_kernel(
    count_x, count_y, c_ref, g_ref, low0, high0, below0, above0, *rest,
):
    stored, (c, g, wx, wy, wz, d, q, b, sems) = rest[:6], rest[6:]
    place_x, place_y = lax.axis_index("gx"), lax.axis_index("gy")
    sides = ends("gx", count_x) + ends("gy", count_y)
    window0(low0, high0, below0, above0, c_ref, g_ref, *sides)(c, g)
    in_y = inside((Y0, Z0), 0, place_y * 16 - OY0, 16 * count_y).astype(F32)
    make_faces(
        c, wx, wy, wz, d, q, 1, X0 - 1, lambda i: flag(place_x * 16 - OX0 + i, 16 * count_x), in_y, 2
    )
    copies = start_copies((wx, wy, wz, d, q), stored[:5], sems, 0)

    def begin(i):
        return [(b, i, q[i] * g[i])]

    loop(1, X0 - 1, begin, 2)
    copies += start_copies((b,), stored[5:], sems, 5)
    wait_copies(copies)


def weights0(count_x, count_y, *operands):
    frame0 = (X0, Y0, Z0)
    return call(
        functools.partial(weights0_kernel, count_x, count_y),
        [struct(*frame0)] * 6,
        [vmem(*frame0)] * 8 + [pltpu.SemaphoreType.DMA((6,))],
        60,
        in_specs=[WHOLE] * 6,
        out_specs=[FAR] * 6,
        flops=20000000,
        bytes_accessed=20000000,
    )(*operands)


def solve_coarse(
    count_x, count_y, all_ref, v3,
    c3, wx3, wy3, wz3, d3, q3, b3, w3, thin3,
    c4, wx4, wy4, wz4, d4, q4, g4, v4, w4, thin4,
):
    n3, n4 = 2 * count_x, count_x

    c3[...] = jnp.zeros(c3.shape, F32)
    b3[...] = jnp.zeros(b3.shape, F32)
    v3[...] = jnp.zeros(v3.shape, F32)
    w3[...] = jnp.zeros(w3.shape, F32)
    lane = iota((count_y, LANES), 1) < 64
    for i in range(n3):
        base = (i // 2) * count_y * 4 + 2 * (i % 2)
        for j in range(2):
            part = all_ref[pl.ds(base + j, count_y, stride=4), :]
            b3[1 + i, pl.ds(j, count_y, stride=2), :] = jnp.where(lane, part, 0.0)
            c3[1 + i, pl.ds(j, count_y, stride=2), :] = jnp.where(lane, pltpu.roll(part, 64, 1), 0.0)
    in_y = jnp.logical_and(iota((Y3, LANES), 0) < 2 * count_y, iota((Y3, LANES), 1) < 64).astype(F32)
    make_faces(c3, wx3, wy3, wz3, d3, q3, 1, n3 + 1, lambda i: 1.0, in_y, 8, whole_y=1)

    def begin3(i):
        return [(v3, i, q3[i] * b3[i])]

    loop(1, n3 + 1, begin3, 8)

    def sweep3(i):
        here, total = neighbours(v3, wx3, wy3, wz3, i)
        return [(w3, i, 0.2 * here + q3[i] * (b3[i] + total))]

    loop(1, n3 + 1, sweep3, 16)

    def restrict3(j):
        i = 2 * j + 1
        both = defect(w3, b3, wx3, wy3, wz3, d3, i) + defect(w3, b3, wx3, wy3, wz3, d3, i + 1)
        return [(thin3, j, both)]

    loop(0, n4, restrict3, 4)
    valid = iota((Y4, LANES), 0) < count_y
    rows = jnp.concatenate(
        [thin3[i, pl.ds(0, Y4, stride=2), :] + thin3[i, pl.ds(1, Y4, stride=2), :] for i in range(n4)], axis=0
    )
    pick = pair_sum_matrix(LANES, LANES)
    g4[...] = (0.5 * split_dot(rows, pick)).reshape(n4, Y4, LANES)
    for i in range(n4):
        thin3[i] = c3[2 * i + 1] + c3[2 * i + 2]
    rows = jnp.concatenate(
        [thin3[i, pl.ds(0, Y4, stride=2), :] + thin3[i, pl.ds(1, Y4, stride=2), :] for i in range(n4)], axis=0
    )
    c4[...] = jnp.zeros(c4.shape, F32)
    c4[1 : n4 + 1] = (0.125 * split_dot(rows, pick)).reshape(n4, Y4, LANES)
    in_y = jnp.logical_and(valid, iota((Y4, LANES), 1) < 32).astype(F32)
    make_faces(c4, wx4, wy4, wz4, d4, q4, 1, n4 + 1, lambda i: 1.0, in_y, n4, whole_y=1)
    v4[...] = jnp.zeros(v4.shape, F32)
    w4[...] = jnp.zeros(w4.shape, F32)
    for i in range(n4):
        g4[i] = q4[1 + i] * g4[i]
        v4[1 + i] = g4[i]

    def bottom(source, target):
        def body(i):
            here, total = neighbours(source, wx4, wy4, wz4, 1 + i)
            return [(target, 1 + i, (0.2 * here + g4[i]) + q4[1 + i] * total)]

        loop(0, n4, body, n4)

    def two(step):
        bottom(v4, w4)
        bottom(w4, v4)
        return []

    loop(0, (BOTTOM - 2) // 2, two)
    bottom(v4, w4)

    wide = split_dot(w4[1 : n4 + 1].reshape(n4 * Y4, LANES), copy_matrix(LANES, LANES)).reshape(n4, Y4, LANES)
    for i in range(n4):
        thin4[pl.ds(0, Y4, stride=2), :] = wide[i]
        thin4[pl.ds(1, Y4, stride=2), :] = wide[i]
        extra = thin4[...]
        v3[1 + 2 * i] = w3[1 + 2 * i] + extra
        v3[2 + 2 * i] = w3[2 + 2 * i] + extra

    loop(1, n3 + 1, sweep3, 8)

    def sweep3_again(i):
        here, total = neighbours(w3, wx3, wy3, wz3, i)
        return [(v3, i, 0.2 * here + q3[i] * (b3[i] + total))]

    loop(1, n3 + 1, sweep3_again, 16)


def up_kernel(
    count_x, count_y,
    all_ref, *rest,
):
    far, rest = rest[:FAR_COUNT], rest[FAR_COUNT:]
    solution_far, residual_far = rest[:2]
    near, rest = rest[2 : 2 + FAR_COUNT], rest[2 + FAR_COUNT :]
    grids, rest = rest[:20], rest[20:]
    v2, w2, b2, v1, b1, c1, wx1, wy1, wz1, d1, q1, w1, spread1 = rest[:13]
    v0, w0, spread0, solution_ref, residual_ref, sems = rest[13:]
    (wx2, wy2, wz2, q2, own2, low_ref, high_ref, below_ref, above_ref,
     g1_mid, g1_below, g1_above, c1_ref, low0, high0, below0, above0, v1_ref, v_own,
     wx0, wy0, wz0, q0, b0, d0, g_ref) = near
    copies = start_copies(far, near, sems, 0)
    v3 = grids[0]
    solve_coarse(count_x, count_y, all_ref, *grids)
    wait_copies(copies[:19])
    place_x, place_y = lax.axis_index("gx"), lax.axis_index("gy")
    n3 = 2 * count_x
    sides = ends("gx", count_x) + ends("gy", count_y)
    first, last, low_y, high_y = sides

    fill_c1(c1, c1_ref, low0, high0, below0, above0, *sides)
    fill_g1(w1, g1_mid, g1_below, g1_above, low_y, high_y)
    in_y = inside((Y1, Z1), 0, place_y * 8 - OY1, 8 * count_y).astype(F32)
    make_faces(
        c1, wx1, wy1, wz1, d1, q1, 5, X1 - 5, lambda i: flag(place_x * 8 - OX1 + i, 8 * count_x), in_y, 2
    )

    def begin1(i):
        return [(b1, i, q1[i] * w1[i])]

    loop(5, X1 - 5, begin1, 2)

    slabs = []
    for j in range(6):
        at = 2 * place_x - 2 + j
        slabs.append(v3[1 + jnp.clip(at, 0, n3 - 1)] * flag(at, n3))
    wide = split_dot(jnp.concatenate(slabs, axis=0), copy_matrix(LANES, LANES))
    target, origin = iota((Y2, Y3), 0), iota((Y2, Y3), 1)
    rows = jnp.logical_and(origin == 2 * place_y - 2 + target // 2, target < 12).astype(F32).astype(BF16)
    half = iota((8, Z2), 0) < 4
    for j in range(6):
        extra = split_dot_left(rows, wide[Y3 * j : Y3 * j + Y3])
        for k in range(2):
            i = 2 * j + k
            at = slice(LANES * (i % 4), LANES * (i % 4) + LANES)
            mid = own2[:, at] if i // 4 == 1 else low_ref[6, :, at] * first if i < 4 else high_ref[6, :, at] * last
            below = below_ref[11 + i // 4, :, at] * low_y
            above = above_ref[11 + i // 4, :, at] * high_y
            v2[i, 0:8] = jnp.where(half, below, pltpu.roll(mid, 4, 0)) + extra[0:8]
            v2[i, 8:16] = jnp.where(half, above, 0.0) + extra[8:16]
            b2[i, 0:8] = jnp.where(half, pltpu.roll(below, 4, 0), mid)
            b2[i, 8:16] = jnp.where(half, pltpu.roll(above, 4, 0), 0.0)
    for i in range(1, X2 - 1):
        b2[i] = q2[i] * b2[i]
    sweep(v2, w2, b2, wx2, wy2, wz2, q2, 1, X2 - 1, 10)
    sweep(w2, v2, b2, wx2, wy2, wz2, q2, 2, X2 - 2, 8)

    spread1[...] = jnp.zeros(spread1.shape, F32)
    for j in range(8):
        extra = double_rows(spread1, v2[2 + j, 2:10], 4)
        extra = jnp.concatenate([extra, extra], axis=1)
        for k in range(2):
            i = 4 + 2 * j + k
            v1[i] = v1_ref[i - 4] + extra
    sweep(v1, w1, b1, wx1, wy1, wz1, q1, 5, X1 - 5, 7)
    sweep(w1, v1, b1, wx1, wy1, wz1, q1, 6, X1 - 6, 6)

    half = iota((8, Z0), 0) < 4
    wait_copies(copies[19:])
    for j in range(12):
        extra = double_rows(spread0, v1[6 + j, 6:18], 0)
        extra = jnp.concatenate([lanes(extra, k // 2) for k in range(Z0 // LANES)], axis=1)
        for k in range(2):
            i = 2 * j - 1 + k
            if i < 0 or i >= X0:
                continue
            if i < 3:
                own = [low_ref[2 * i + side] * first for side in range(2)]
            elif i < 19:
                own = [v_own[i - 3, 8 * side : 8 * side + 8, :] for side in range(2)]
            else:
                own = [high_ref[2 * (i - 19) + side] * last for side in range(2)]
            below, above = below_ref[i // 2] * low_y, above_ref[i // 2] * high_y
            if i % 2:
                below = pltpu.roll(below, 4, 0)
            else:
                above = pltpu.roll(above, 4, 0)
            head, tail = pltpu.roll(own[0], 4, 0), pltpu.roll(own[1], 4, 0)
            v0[i, 0:8] = jnp.where(half, below, head) + extra[0:8]
            v0[i, 8:16] = jnp.where(half, head, tail) + extra[8:16]
            v0[i, 16:24] = jnp.where(half, tail, above) + extra[16:24]
    sweep(v0, w0, b0, wx0, wy0, wz0, q0, 1, X0 - 1, 2)
    sweep(w0, v0, b0, wx0, wy0, wz0, q0, 2, X0 - 2, 2)

    pick = collect_matrix(Z0)
    rows = jnp.concatenate([pltpu.roll(v0[i + OX0], Y0 - OY0, 0)[0:16] for i in range(16)], axis=0)
    solution_ref[...] = split_dot(rows, pick).reshape(16, 16, Z0)
    copies = start_copies((solution_ref,), (solution_far,), sems, FAR_COUNT)

    def finish(i):
        here, total = neighbours(v0, wx0, wy0, wz0, i + OX0)
        return [(residual_ref, i, pltpu.roll(total - d0[i + OX0] * here, Y0 - OY0, 0)[0:16])]

    loop(0, 16, finish, 2)
    for part in range(2):
        here = pl.ds(8 * part, 8)
        rows = residual_ref[here].reshape(128, Z0)
        residual_ref[here] = g_ref[here] + split_dot(rows, pick).reshape(8, 16, Z0)
        copies += start_copies((residual_ref.at[here],), (residual_far.at[here],), sems, FAR_COUNT + 1 + part)
    wait_copies(copies)


def up(count_x, count_y, everything, *operands):
    frame0, frame1, frame2 = (X0, Y0, Z0), (X1, Y1, Z1), (X2, Y2, Z2)
    frame3, frame4 = (2 * count_x + 2, Y3, LANES), (count_x + 2, Y4, LANES)
    return call(
        functools.partial(up_kernel, count_x, count_y),
        [struct(16, 16, Z0), struct(16, 16, Z0)],
        [vmem(*operand.shape) for operand in operands]
        + [vmem(*frame3)] * 9 + [vmem(count_x, Y3, LANES)]
        + [vmem(*frame4)] * 6 + [vmem(count_x, Y4, LANES)] + [vmem(*frame4)] * 2 + [vmem(Y3, LANES)]
        + [vmem(*frame2)] * 3 + [vmem(*frame1)] * 9 + [vmem(1, Y1, LANES)]
        + [vmem(*frame0)] * 2 + [vmem(Z1 // LANES, Y0, LANES)] + [vmem(16, 16, Z0)] * 2
        + [pltpu.SemaphoreType.DMA((FAR_COUNT + 3,))],
        60,
        in_specs=[WHOLE] + [FAR] * FAR_COUNT,
        out_specs=[FAR] * 2,
    )(everything, *operands)


def to_next(cells, axis):
    count = lax.axis_size(axis)
    return lax.ppermute(cells, axis, [(i, (i + 1) % count) for i in range(count)])


def to_previous(cells, axis):
    count = lax.axis_size(axis)
    return lax.ppermute(cells, axis, [((i + 1) % count, i) for i in range(count)])


def shards(right_side, coefficient):
    count_x, count_y = lax.axis_size("gx"), lax.axis_size("gy")
    place_x = lax.axis_index("gx")

    def with_sides(low, cells, high):
        low = jnp.where(place_x > 0, low, 0.0)
        high = jnp.where(place_x < count_x - 1, high, 0.0)
        return jnp.concatenate([low, cells, high], axis=0)

    to_right, to_left, c1 = begin(coefficient, right_side)
    low, high = to_next(to_right, "gx"), to_previous(to_left, "gx")
    c_own, g_own = deal(coefficient, right_side)
    top, bottom, low, high = edges_y(count_x, c_own, g_own, c1, low, high)
    below, above = to_next(top, "gy"), to_previous(bottom, "gy")
    g1, v_own = down0(count_x, count_y, c_own, g_own, low, high, below, above)

    g1_low, g1_high = to_next(g1[2:8], "gx"), to_previous(g1[0:6], "gx")
    levels = prepare(count_x, count_y, c1, low, high, below, above)
    wx2, wy2, wz2, q2 = levels[5], levels[6], levels[7], levels[9]
    g1_mid = with_sides(g1_low, g1, g1_high)
    g1_below, g1_above = to_next(g1_mid, "gy"), to_previous(g1_mid, "gy")
    v1, to_right, to_left, own2, send3 = down1(count_x, count_y, v_own, g1_mid, g1_below, g1_above, *levels)

    low2, high2 = to_next(to_right, "gx"), to_previous(to_left, "gx")
    everything = lax.all_to_all(send3, ("gx", "gy"), split_axis=0, concat_axis=0, tiled=True)
    top, bottom = iterate_edges(count_x, v_own, own2, low2, high2)
    below2, above2 = to_next(top, "gy"), to_previous(bottom, "gy")
    c_own, send3 = lax.optimization_barrier((c_own, send3))
    weights = weights0(count_x, count_y, c_own, g_own, low, high, below, above)
    wx0, wy0, wz0, d0, q0, b0 = weights
    return tuple(
        up(
            count_x, count_y, everything, wx2, wy2, wz2, q2, own2, low2, high2, below2, above2,
            g1_mid, g1_below, g1_above, c1, low, high, below, above, v1, v_own,
            wx0, wy0, wz0, q0, b0, d0, right_side,
        )
    )


def solution(mesh):
    specs = (P("gx", "gy", None), P("gx", "gy", None))
    return jax.shard_map(shards, mesh=mesh, in_specs=specs, out_specs=specs, check_vma=False)
```

```python
import functools

import jax
import jax.numpy as jnp
from jax import lax
from jax.experimental import pallas as pl
from jax.experimental.pallas import tpu as pltpu
from jax.sharding import PartitionSpec as P

F32 = jnp.float32
BF16 = jnp.bfloat16
OMEGA = 0.8
BOTTOM = 16
MIB = 1024 * 1024

X0, Y0, Z0, OX0, OY0 = 22, 24, 512, 3, 4
X1, Y1, Z1, OX1, OY1 = 24, 24, 256, 8, 8
X2, Y2, Z2, OX2, OY2 = 12, 16, 128, 4, 4
Y3, Y4, LANES = 16, 8, 128
C_TILES, CG_TILES = 11, 16


def iota(shape, dim):
    return lax.broadcasted_iota(jnp.int32, shape, dim)


def up_of(cells, dim):
    if dim == 0 or cells.shape[1] == LANES:
        return pltpu.roll(cells, cells.shape[dim] - 1, dim)
    return jnp.concatenate([cells[:, LANES:], pltpu.roll(cells[:, :LANES], LANES - 1, 1)], axis=1)


def down_of(cells, dim):
    if dim == 0 or cells.shape[1] == LANES:
        return pltpu.roll(cells, 1, dim)
    return jnp.concatenate([pltpu.roll(cells[:, -LANES:], 1, 1), cells[:, :-LANES]], axis=1)


def cell_of(position, count):
    pieces = count // LANES
    return pieces * (position % LANES) + position // LANES


def deal_matrix(count):
    hit = iota((count, count), 0) == cell_of(iota((count, count), 1), count)
    return hit.astype(F32).astype(BF16)


def collect_matrix(count):
    hit = cell_of(iota((count, count), 0), count) == iota((count, count), 1)
    return hit.astype(F32).astype(BF16)


def pair_sums(cells):
    pieces = [lanes(cells, k) for k in range(cells.shape[1] // LANES)]
    sums = [even + odd for even, odd in zip(pieces[::2], pieces[1::2])]
    return jnp.concatenate(sums, axis=1) if len(sums) > 1 else sums[0]


def split_dot(cells, pick):
    high = cells.astype(BF16)
    rest = cells - high.astype(F32)
    mid = rest.astype(BF16)
    low = (rest - mid.astype(F32)).astype(BF16)
    dot = functools.partial(jnp.dot, preferred_element_type=F32)
    return dot(high, pick) + (dot(mid, pick) + dot(low, pick))


def split_dot_left(pick, cells):
    high = cells.astype(BF16)
    rest = cells - high.astype(F32)
    mid = rest.astype(BF16)
    low = (rest - mid.astype(F32)).astype(BF16)
    dot = functools.partial(jnp.dot, preferred_element_type=F32)
    return dot(pick, high) + (dot(pick, mid) + dot(pick, low))


def pair_sum_matrix(fine, coarse, offset=0):
    hit = (iota((fine, coarse), 0) // 2) + offset == iota((fine, coarse), 1)
    return hit.astype(F32).astype(BF16)


def pair_deal_matrix(fine, coarse):
    hit = iota((fine, coarse), 0) // 2 == cell_of(iota((fine, coarse), 1), coarse)
    return hit.astype(F32).astype(BF16)


def copy_matrix(coarse, fine):
    hit = iota((coarse, fine), 0) == iota((coarse, fine), 1) // 2
    return hit.astype(F32).astype(BF16)


def inside(shape, dim, start, count):
    place = iota(shape, dim) + start
    return jnp.logical_and(place >= 0, place < count)


def flag(start, count):
    return jnp.where(jnp.logical_and(start >= 0, start < count), 1.0, 0.0).astype(F32)


def loop(first, last, body, width=1):
    def run(i, count):
        stores = [store for j in range(count) for store in body(i + j)]
        for ref, at, value in stores:
            ref[at] = value

    count = (last - first) // width

    def step(t, carry):
        run(first + t * width, width)
        return carry

    if count == 1:
        run(first, width)
    else:
        lax.fori_loop(0, count, step, 0)
    if (last - first) % width:
        run(first + count * width, (last - first) % width)


def inverse(total):
    total = jnp.maximum(total, 1e-30)
    guess = pl.reciprocal(total, approx=True)
    guess = guess * (2.0 - total * guess)
    return guess * (2.0 - total * guess)


def make_faces(c, wx, wy, wz, d, q, first, last, in_x, in_y, width, whole_y=0, period=0):
    rows, cells = c.shape[1], c.shape[2]
    period = period or cells
    end_z = iota((rows, cells), 1) % period == period - 1
    start_z = iota((rows, cells), 1) % period == 0
    row = iota((rows, cells), 0)
    wx[first - 1] = 0.5 * (c[first - 1] + c[first])

    def body(i):
        here = c[i]
        after = c[i + 1]
        before = c[i - 1]
        y_up, y_down = up_of(here, 0), down_of(here, 0)
        if whole_y:
            y_up = jnp.where(row == rows - 1, 0.0, y_up)
            y_down = jnp.where(row == 0, 0.0, y_down)
        z_up = jnp.where(end_z, 0.0, up_of(here, 1))
        z_down = jnp.where(start_z, 0.0, down_of(here, 1))
        side = 0.5 * (here + y_up)
        side = jnp.where(row == rows - 1, 0.0, side) if whole_y else side
        total = 3.0 * here + 0.5 * ((after + before) + (y_up + y_down) + (z_up + z_down))
        return [
            (wx, i, 0.5 * (here + after)),
            (wy, i, side),
            (wz, i, jnp.where(end_z, 0.0, 0.5 * (here + z_up))),
            (d, i, total),
            (q, i, (in_y * (OMEGA * in_x(i))) * inverse(total)),
        ]

    loop(first, last, body, width)


def neighbours(v, wx, wy, wz, i):
    here = v[i]
    side_y, side_z = wy[i], wz[i]
    along_x = wx[i] * v[i + 1] + wx[i - 1] * v[i - 1]
    along_y = side_y * up_of(here, 0) + down_of(side_y * here, 0)
    along_z = side_z * up_of(here, 1) + down_of(side_z * here, 1)
    return here, along_x + along_y + along_z


def sweep(v, out, b, wx, wy, wz, q, first, last, width):
    def body(i):
        here, total = neighbours(v, wx, wy, wz, i)
        return [(out, i, (0.2 * here + b[i]) + q[i] * total)]

    loop(first, last, body, width)


def defect(v, source, wx, wy, wz, d, i):
    here, total = neighbours(v, wx, wy, wz, i)
    return (source[i] - d[i] * here) + total


def lanes(cells, k):
    return cells[:, LANES * k : LANES * k + LANES]


def keep(scratch, j, cells):
    for k in range(cells.shape[1] // LANES):
        scratch[j, k] = lanes(cells, k)


def halve_rows(scratch, j, start, count):
    parts = [
        scratch[j, k, pl.ds(start, count, stride=2), :] + scratch[j, k, pl.ds(start + 1, count, stride=2), :]
        for k in range(scratch.shape[1])
    ]
    return jnp.concatenate(parts, axis=1)


def double_rows(scratch, j, cells, start):
    for k in range(scratch.shape[1]):
        for odd in range(2):
            scratch[j, k, pl.ds(start + odd, cells.shape[0], stride=2), :] = lanes(cells, k)


def doubled(scratch, j):
    return [scratch[j, k] for k in range(scratch.shape[1])]


def call(kernel, out_shape, scratch, limit, in_specs=None, out_specs=None, flops=1000000, bytes_accessed=1000000):
    extra = {}
    if in_specs is not None:
        extra["in_specs"] = in_specs
    if out_specs is not None:
        extra["out_specs"] = out_specs
    return pl.pallas_call(
        kernel,
        out_shape=out_shape,
        scratch_shapes=scratch,
        compiler_params=pltpu.CompilerParams(vmem_limit_bytes=limit * MIB),
        cost_estimate=pl.CostEstimate(flops=flops, bytes_accessed=bytes_accessed, transcendentals=0),
        **extra,
    )


def struct(*shape):
    return jax.ShapeDtypeStruct(shape, F32)


def vmem(*shape):
    return pltpu.VMEM(shape, F32)


WHOLE = pl.BlockSpec(memory_space=pltpu.VMEM)
FAR = pl.BlockSpec(memory_space=pl.ANY)
FAR_COUNT = 26


def start_copies(sources, targets, sems, first):
    copies = [
        pltpu.make_async_copy(source, target, sems.at[first + k])
        for k, (source, target) in enumerate(zip(sources, targets))
    ]
    for copy in copies:
        copy.start()
    return copies


def wait_copies(copies):
    for copy in copies:
        copy.wait()


def place_of(i):
    row, cell = 8 * ((i // 2) % 2), Z1 * (i % 2)
    return 5 + i // 4, slice(row, row + 8), slice(cell, cell + Z1)


def begin_kernel(c_ref, g_ref, next_ref, previous_ref, c1_ref, pairs):
    for i in range(8):
        keep(pairs, i, c_ref[2 * i] + c_ref[2 * i + 1])
    for i in range(3):
        next_ref[i] = c_ref[13 + i]
        previous_ref[i] = c_ref[i]
    for i in range(2):
        next_ref[3 + i] = g_ref[14 + i]
        previous_ref[3 + i] = g_ref[i]
    rows = jnp.concatenate([halve_rows(pairs, i, 0, 8) for i in range(8)], axis=0)
    small = 0.125 * split_dot(rows, pair_deal_matrix(Z0, Z1))
    for i in range(8):
        block = small[8 * i : 8 * i + 8]
        c1_ref[i] = block
        next_ref[place_of(i)] = block
        previous_ref[place_of(i)] = block


def begin(coefficient, right_side):
    return call(
        begin_kernel, [struct(7, 16, Z0), struct(7, 16, Z0), struct(8, 8, Z1)], [vmem(8, Z0 // LANES, 16, LANES)], 8
    )(coefficient, right_side)


def deal_kernel(c_ref, g_ref, c_out, g_out, pick_out):
    pick = deal_matrix(Z0)
    pick_out[...] = pick
    for ref, out in ((c_ref, c_out), (g_ref, g_out)):
        out[...] = split_dot(ref[...].reshape(256, Z0), pick).reshape(16, 16, Z0)


def deal(coefficient, right_side):
    pick = jax.ShapeDtypeStruct((Z0, Z0), BF16)
    return call(deal_kernel, [struct(16, 16, Z0), struct(16, 16, Z0), pick], [], 8)(coefficient, right_side)


def edge_kernel(
    count_x, pick_ref, c_ref, g_ref, c1_ref, low_raw, high_raw, top_ref, bottom_ref, low_ref, high_ref
):
    pick = pick_ref[...]
    for raw, out in ((low_raw, low_ref), (high_raw, high_ref)):
        out[0:5] = split_dot(raw[0:5].reshape(80, Z0), pick).reshape(5, 16, Z0)
        out[5:7] = raw[5:7]
    place = lax.axis_index("gx")
    first = jnp.where(place > 0, 1.0, 0.0).astype(F32)
    last = jnp.where(place < count_x - 1, 1.0, 0.0).astype(F32)
    row = iota((8, Z0), 0)

    def c_part(i, half):
        rows = slice(8 * half, 8 * half + 8)
        if i < 3:
            return low_ref[i, rows, :] * first
        return c_ref[i - 3, rows, :] if i < 19 else high_ref[i - 19, rows, :] * last

    def g_part(i, half):
        rows = slice(8 * half, 8 * half + 8)
        if i < 3:
            return low_ref[i + 2, rows, :] * first
        return g_ref[i - 3, rows, :] if i < 19 else high_ref[i - 16, rows, :] * last

    for j in range(X0 // 2):
        top_ref[j] = jnp.where(row < 4, pltpu.roll(c_part(2 * j, 1), 4, 0), c_part(2 * j + 1, 1))
        bottom_ref[j] = jnp.where(row < 4, c_part(2 * j, 0), pltpu.roll(c_part(2 * j + 1, 0), 4, 0))
    for j in range(5):
        top, bottom = g_part(1 + 4 * j, 1), g_part(1 + 4 * j, 0)
        top = pltpu.roll(top, 2, 0)
        for k in range(1, 4):
            part = g_part(1 + 4 * j + k, 1)
            part = pltpu.roll(part, (2 * k + 2) % 8, 0) if k < 3 else part
            top = jnp.where(row // 2 == k, part, top)
            bottom = jnp.where(row // 2 == k, pltpu.roll(g_part(1 + 4 * j + k, 0), 2 * k, 0), bottom)
        top_ref[C_TILES + j] = top
        bottom_ref[C_TILES + j] = bottom
    for i in range(24):
        part = low_ref[place_of(i)] * first if i < 8 else c1_ref[i - 8] if i < 16 else high_ref[place_of(i - 16)] * last
        for ref in (top_ref, bottom_ref):
            ref[CG_TILES + i // 2, :, Z1 * (i % 2) : Z1 * (i % 2) + Z1] = part


def edges_y(count_x, *operands):
    return call(
        functools.partial(edge_kernel, count_x), [struct(CG_TILES + 12, 8, Z0)] * 2 + [struct(7, 16, Z0)] * 2, [], 8
    )(*operands)


def ends(axis, count):
    place = lax.axis_index(axis)
    low = jnp.where(place > 0, 1.0, 0.0).astype(F32)
    return low, jnp.where(place < count - 1, 1.0, 0.0).astype(F32)


def window0(low_ref, high_ref, below_ref, above_ref, c_ref, g_ref, first, last, low_y, high_y):
    row = iota((8, Z0), 0) < 4

    def put(own, below, above):
        head, tail = pltpu.roll(own[0:8], 4, 0), pltpu.roll(own[8:16], 4, 0)
        parts = [jnp.where(row, below, head), jnp.where(row, head, tail), jnp.where(row, tail, above)]
        return jnp.concatenate(parts, axis=0)

    def turn(cells, rows):
        return pltpu.roll(cells, rows % 8, 0) if rows % 8 else cells

    def c_slab(i, own):
        odd = i % 2
        below = turn(below_ref[i // 2], 4 * odd) * low_y
        return put(own, below, turn(above_ref[i // 2], 4 - 4 * odd) * high_y)

    def g_slab(i, own):
        tile, k = C_TILES + (i - 1) // 4, (i - 1) % 4
        below = turn(below_ref[tile], 2 - 2 * k) * low_y
        return put(own, below, turn(above_ref[tile], 4 - 2 * k) * high_y)

    def fill(c, g):
        for i in range(3):
            c[i] = c_slab(i, low_ref[i] * first)
            c[19 + i] = c_slab(19 + i, high_ref[i] * last)
        for i in range(3, 19):
            c[i] = c_slab(i, c_ref[i - 3])
        for i in (1, 2):
            g[i] = g_slab(i, low_ref[i + 2] * first)
            g[18 + i] = g_slab(18 + i, high_ref[i + 2] * last)
        for i in range(3, 19):
            g[i] = g_slab(i, g_ref[i - 3])

    return fill


def down0_kernel(
    count_x, count_y,
    c_ref, g_ref, low_ref, high_ref, below_ref, above_ref,
    g1_ref, v_own_ref, c, g, wx, wy, wz, d, q, b, v, pairs,
):
    place_x, place_y = lax.axis_index("gx"), lax.axis_index("gy")
    sides = ends("gx", count_x) + ends("gy", count_y)
    window0(low_ref, high_ref, below_ref, above_ref, c_ref, g_ref, *sides)(c, g)
    in_y = inside((Y0, Z0), 0, place_y * 16 - OY0, 16 * count_y).astype(F32)
    make_faces(
        c, wx, wy, wz, d, q, 1, X0 - 1, lambda i: flag(place_x * 16 - OX0 + i, 16 * count_x), in_y, 2
    )

    def begin(i):
        return [(b, i, q[i] * g[i])]

    loop(1, X0 - 1, begin, 2)
    sweep(b, v, b, wx, wy, wz, q, 2, X0 - 2, 3)

    def own_of(i):
        return [(v_own_ref, i, pltpu.roll(v[i + 3], Y0 - OY0, 0)[0:16])]

    loop(0, 16, own_of, 2)

    def restrict(j):
        i = 2 * j + OX0
        both = defect(v, g, wx, wy, wz, d, i) + defect(v, g, wx, wy, wz, d, i + 1)
        return [(pairs, (j, k), lanes(both, k)) for k in range(Z0 // LANES)]

    loop(0, 8, restrict)
    rows = jnp.concatenate([halve_rows(pairs, i, 4, 8) for i in range(8)], axis=0)
    g1_ref[...] = (0.5 * pair_sums(rows)).reshape(8, 8, Z1)


def down0(count_x, count_y, *operands):
    frame = (X0, Y0, Z0)
    return call(
        functools.partial(down0_kernel, count_x, count_y),
        [struct(8, 8, Z1), struct(16, 16, Z0)],
        [vmem(*frame)] * 9 + [vmem(8, Z0 // LANES, Y0, LANES)],
        18,
    )(*operands)


def fill_c1(c1, c1_ref, low_ref, high_ref, below_ref, above_ref, first, last, low_y, high_y):
    for i in range(24):
        at = CG_TILES + i // 2, slice(0, 8), slice(Z1 * (i % 2), Z1 * (i % 2) + Z1)
        part = low_ref[place_of(i)] * first if i < 8 else c1_ref[i - 8] if i < 16 else high_ref[place_of(i - 16)] * last
        c1[i, 0:8, :] = below_ref[at] * low_y
        c1[i, 8:16, :] = part
        c1[i, 16:24, :] = above_ref[at] * high_y


def prepare_kernel(
    count_x, count_y, c1_ref, low_ref, high_ref, below_ref, above_ref,
    wx1, wy1, wz1, d1, q1, wx2, wy2, wz2, d2, q2, c3_ref, c1, c2, pairs,
):
    place_x, place_y = lax.axis_index("gx"), lax.axis_index("gy")
    sides = ends("gx", count_x) + ends("gy", count_y)
    fill_c1(c1, c1_ref, low_ref, high_ref, below_ref, above_ref, *sides)
    in_y = inside((Y1, Z1), 0, place_y * 8 - OY1, 8 * count_y).astype(F32)
    make_faces(
        c1, wx1, wy1, wz1, d1, q1, 2, X1 - 2, lambda i: flag(place_x * 8 - OX1 + i, 8 * count_x), in_y, 2
    )
    for i in range(12):
        keep(pairs, i, c1[2 * i] + c1[2 * i + 1])
    blank = jnp.zeros((4, Z1), F32)
    rows = []
    for i in range(12):
        rows.append(halve_rows(pairs, i, 0, 12))
        rows.append(blank)
    c2[...] = (0.125 * pair_sums(jnp.concatenate(rows, axis=0))).reshape(X2, Y2, Z2)
    in_y = inside((Y2, Z2), 0, place_y * 4 - OY2, 4 * count_y).astype(F32)
    make_faces(
        c2, wx2, wy2, wz2, d2, q2, 1, X2 - 1, lambda i: flag(place_x * 4 - OX2 + i, 4 * count_x), in_y, 10
    )
    rows = jnp.concatenate([c2[4] + c2[5], c2[6] + c2[7]], axis=0)
    thin = 0.125 * split_dot(rows, pair_sum_matrix(Z2, LANES, 64))
    row = iota((8, LANES), 0)
    c3 = jnp.zeros((8, LANES), F32)
    for i in range(2):
        for j in range(2):
            at = 16 * i + 4 + 2 * j
            both = thin[at : at + 1] + thin[at + 1 : at + 2]
            c3 = jnp.where(row == 2 * i + j, jnp.broadcast_to(both, (8, LANES)), c3)
    c3_ref[...] = c3


def prepare(count_x, count_y, *operands):
    frame1, frame2 = (X1, Y1, Z1), (X2, Y2, Z2)
    return call(
        functools.partial(prepare_kernel, count_x, count_y),
        [struct(*frame1)] * 5 + [struct(*frame2)] * 5 + [struct(8, LANES)],
        [vmem(*frame1), vmem(*frame2), vmem(12, Z1 // LANES, Y1, LANES)],
        8,
    )(*operands)


def fill_g1(g1, mid_ref, below_ref, above_ref, low_y, high_y):
    g1[2:22, 0:8, :] = below_ref[...] * low_y
    g1[2:22, 8:16, :] = mid_ref[...]
    g1[2:22, 16:24, :] = above_ref[...] * high_y


def down1_kernel(
    count_x, count_y, mid_ref, below_ref, above_ref,
    wx1, wy1, wz1, d1, q1, wx2, wy2, wz2, d2, q2, c3_ref,
    v_far, send2_ref, send3_ref, v1_ref, b1_ref, g1, g2, b2, v2, pairs, thin,
):
    place_y = lax.axis_index("gy")
    low_y = jnp.where(place_y > 0, 1.0, 0.0).astype(F32)
    high_y = jnp.where(place_y < count_y - 1, 1.0, 0.0).astype(F32)
    fill_g1(g1, mid_ref, below_ref, above_ref, low_y, high_y)

    def begin1(i):
        return [(b1_ref, i, q1[i] * g1[i])]

    loop(2, X1 - 2, begin1, 4)
    sweep(b1_ref, v1_ref, b1_ref, wx1, wy1, wz1, q1, 3, X1 - 3, 3)

    def restrict(j):
        i = 2 * j + 4
        after = defect(v1_ref, g1, wx1, wy1, wz1, d1, i + 1)
        both = defect(v1_ref, g1, wx1, wy1, wz1, d1, i) + after
        return [(pairs, (j, k), lanes(both, k)) for k in range(Z1 // LANES)]

    loop(0, 8, restrict, 2)
    rows = jnp.concatenate([halve_rows(pairs, i, 4, 8) for i in range(8)], axis=0)
    small = 0.5 * pair_sums(rows)
    g2[...] = jnp.zeros((X2, Y2, Z2), F32)
    for i in range(8):
        g2[2 + i, 2:10, :] = small[8 * i : 8 * i + 8]
    for i in range(2, X2 - 2):
        b2[i] = q2[i] * g2[i]
    sweep(b2, v2, b2, wx2, wy2, wz2, q2, 3, X2 - 3, 6)
    row = iota((8, Z2), 0) < 4
    for i in range(4):
        both = jnp.where(row, pltpu.roll(v2[4 + i, 0:8, :], 4, 0), g2[4 + i, 0:8, :])
        send2_ref[:, LANES * i : LANES * i + LANES] = both
    halves = [
        defect(v2, g2, wx2, wy2, wz2, d2, 4 + 2 * i) + defect(v2, g2, wx2, wy2, wz2, d2, 5 + 2 * i)
        for i in range(2)
    ]
    thin[...] = 0.5 * split_dot(jnp.concatenate(halves, axis=0), pair_sum_matrix(Z2, LANES))
    row = iota((8, LANES), 0)
    source = jnp.zeros((8, LANES), F32)
    for i in range(2):
        for j in range(2):
            at = 16 * i + 4 + 2 * j
            both = thin[at : at + 1, :] + thin[at + 1 : at + 2, :]
            source = jnp.where(row == 2 * i + j, jnp.broadcast_to(both, (8, LANES)), source)
    source = source + c3_ref[...]
    double = jnp.where(row < 4, source, pltpu.roll(source, 4, 0))
    for i in range(count_x * count_y // 2):
        send3_ref[8 * i : 8 * i + 8, :] = double
    v_far[...] = v1_ref[4:20]


def down1(count_x, count_y, *operands):
    frame1, frame2 = (X1, Y1, Z1), (X2, Y2, Z2)
    return call(
        functools.partial(down1_kernel, count_x, count_y),
        [struct(16, Y1, Z1), struct(8, Z0)]
        + [struct(4 * count_x * count_y, LANES)],
        [vmem(*frame1)] * 3 + [vmem(*frame2)] * 3 + [vmem(8, Z1 // LANES, Y1, LANES), vmem(32, LANES)],
        8,
    )(*operands)


def iterate_side_kernel(own_ref, own2_ref, next_ref, previous_ref):
    for i in range(3):
        for half in range(2):
            next_ref[2 * i + half] = own_ref[13 + i, 8 * half : 8 * half + 8, :]
            previous_ref[2 * i + half] = own_ref[i, 8 * half : 8 * half + 8, :]
    next_ref[6] = own2_ref[...]
    previous_ref[6] = own2_ref[...]


def iterate_sides(*operands):
    return call(iterate_side_kernel, [struct(7, 8, Z0), struct(7, 8, Z0)], [], 8)(*operands)


def iterate_edge_kernel(count_x, own_ref, own2_ref, low_ref, high_ref, top_ref, bottom_ref):
    place = lax.axis_index("gx")
    first = jnp.where(place > 0, 1.0, 0.0).astype(F32)
    last = jnp.where(place < count_x - 1, 1.0, 0.0).astype(F32)
    row = iota((8, Z0), 0) < 4

    def slab(i, half):
        if i < 3:
            return low_ref[2 * i + half] * first
        if i < 19:
            return own_ref[i - 3, 8 * half : 8 * half + 8, :]
        return high_ref[2 * (i - 19) + half] * last

    for j in range(X0 // 2):
        top_ref[j] = jnp.where(row, pltpu.roll(slab(2 * j, 1), 4, 0), slab(2 * j + 1, 1))
        bottom_ref[j] = jnp.where(row, slab(2 * j, 0), pltpu.roll(slab(2 * j + 1, 0), 4, 0))
    for ref in (top_ref, bottom_ref):
        ref[11] = low_ref[6] * first
        ref[12] = own2_ref[...]
        ref[13] = high_ref[6] * last


def iterate_edges(count_x, *operands):
    return call(
        functools.partial(iterate_edge_kernel, count_x), [struct(14, 8, Z0), struct(14, 8, Z0)], [], 8
    )(*operands)


def weights0_kernel(
    count_x, count_y, c_ref, g_ref, low0, high0, below0, above0, *rest,
):
    stored, (c, g, wx, wy, wz, d, q, b, sems) = rest[:6], rest[6:]
    place_x, place_y = lax.axis_index("gx"), lax.axis_index("gy")
    sides = ends("gx", count_x) + ends("gy", count_y)
    window0(low0, high0, below0, above0, c_ref, g_ref, *sides)(c, g)
    in_y = inside((Y0, Z0), 0, place_y * 16 - OY0, 16 * count_y).astype(F32)
    make_faces(
        c, wx, wy, wz, d, q, 1, X0 - 1, lambda i: flag(place_x * 16 - OX0 + i, 16 * count_x), in_y, 2
    )
    copies = start_copies((wx, wy, wz, d, q), stored[:5], sems, 0)

    def begin(i):
        return [(b, i, q[i] * g[i])]

    loop(1, X0 - 1, begin, 2)
    copies += start_copies((b,), stored[5:], sems, 5)
    wait_copies(copies)


def weights0(count_x, count_y, *operands):
    frame0 = (X0, Y0, Z0)
    return call(
        functools.partial(weights0_kernel, count_x, count_y),
        [struct(*frame0)] * 6,
        [vmem(*frame0)] * 8 + [pltpu.SemaphoreType.DMA((6,))],
        60,
        in_specs=[WHOLE] * 6,
        out_specs=[FAR] * 6,
        flops=20000000,
        bytes_accessed=20000000,
    )(*operands)


def join_halves(frame, count):
    first = iota(frame.shape[1:], 1) < 64
    frame[0] = jnp.where(first, 0.0, pltpu.roll(frame[count], 64, 1))
    frame[count + 1] = jnp.where(first, pltpu.roll(frame[1], 64, 1), 0.0)


def halves_matrix(of_fine):
    fine, coarse = iota((LANES, LANES), of_fine), iota((LANES, LANES), 1 - of_fine)
    hit = jnp.logical_and(fine // 64 == coarse // 64, (fine % 64) // 2 == coarse % 64)
    return hit.astype(F32).astype(BF16)


def solve_coarse(
    count_x, count_y, all_ref, v3,
    c3, wx3, wy3, wz3, d3, q3, b3, w3, thin3,
    c4, wx4, wy4, wz4, d4, q4, g4, v4, thin4,
):
    h3, h4 = count_x, count_x // 2

    if 2 * count_y < Y3:
        c3[...] = jnp.zeros(c3.shape, F32)
        b3[...] = jnp.zeros(b3.shape, F32)
    first = iota((count_y, LANES), 1) < 64
    for i in range(h3):
        for j in range(2):
            parts = []
            for x in (i, i + h3):
                base = (x // 2) * count_y * 4 + 2 * (x % 2)
                parts.append(all_ref[pl.ds(base + j, count_y, stride=4), :])
            rows = pl.ds(j, count_y, stride=2)
            b3[1 + i, rows, :] = jnp.where(first, parts[0], pltpu.roll(parts[1], 64, 1))
            c3[1 + i, rows, :] = jnp.where(first, pltpu.roll(parts[0], 64, 1), parts[1])
    join_halves(c3, h3)
    in_y = (iota((Y3, LANES), 0) < 2 * count_y).astype(F32)
    make_faces(c3, wx3, wy3, wz3, d3, q3, 1, h3 + 1, lambda i: 1.0, in_y, min(8, h3), whole_y=1, period=64)

    def begin3(i):
        return [(v3, i, q3[i] * b3[i])]

    loop(1, h3 + 1, begin3, h3)
    join_halves(v3, h3)

    def sweep3(i):
        here, total = neighbours(v3, wx3, wy3, wz3, i)
        return [(w3, i, 0.2 * here + q3[i] * (b3[i] + total))]

    loop(1, h3 + 1, sweep3, h3)
    join_halves(w3, h3)

    def restrict3(j):
        i = 2 * j + 1
        both = defect(w3, b3, wx3, wy3, wz3, d3, i) + defect(w3, b3, wx3, wy3, wz3, d3, i + 1)
        return [(thin3, j, both), (thin3, h4 + j, c3[i] + c3[i + 1])]

    loop(0, h4, restrict3, min(4, h4))
    rows = jnp.concatenate(
        [thin3[i, pl.ds(0, Y4, stride=2), :] + thin3[i, pl.ds(1, Y4, stride=2), :] for i in range(2 * h4)], axis=0
    )
    both = split_dot(rows, halves_matrix(0)).reshape(2 * h4, Y4, LANES)
    g4[...] = 0.5 * both[:h4]
    c4[1 : h4 + 1] = 0.125 * both[h4:]
    join_halves(c4, h4)
    in_y = jnp.logical_and(iota((Y4, LANES), 0) < count_y, iota((Y4, LANES), 1) % 64 < 32).astype(F32)
    make_faces(c4, wx4, wy4, wz4, d4, q4, 1, h4 + 1, lambda i: 1.0, in_y, h4, whole_y=1, period=64)

    along_x = [wx4[i] for i in range(h4 + 1)]
    along_y, along_z = [wy4[1 + i] for i in range(h4)], [wz4[1 + i] for i in range(h4)]
    scale = [q4[1 + i] for i in range(h4)]
    start = [scale[i] * g4[i] for i in range(h4)]
    first = iota((Y4, LANES), 1) < 64

    def bottom(step, v):
        before = jnp.where(first, 0.0, pltpu.roll(v[-1], 64, 1))
        after = jnp.where(first, pltpu.roll(v[0], 64, 1), 0.0)
        padded = (before, *v, after)
        out = []
        for i, here in enumerate(v):
            total = along_x[i + 1] * padded[i + 2] + along_x[i] * padded[i]
            total += along_y[i] * up_of(here, 0) + down_of(along_y[i] * here, 0)
            total += along_z[i] * up_of(here, 1) + down_of(along_z[i] * here, 1)
            out.append((0.2 * here + start[i]) + scale[i] * total)
        return tuple(out)

    final = lax.fori_loop(0, BOTTOM - 1, bottom, tuple(start))

    wide = split_dot(jnp.concatenate(final, axis=0), halves_matrix(1)).reshape(h4, Y4, LANES)
    for i in range(h4):
        thin4[i, pl.ds(0, Y4, stride=2), :] = wide[i]
        thin4[i, pl.ds(1, Y4, stride=2), :] = wide[i]
    for i in range(h4):
        extra = thin4[i]
        v3[1 + 2 * i] = w3[1 + 2 * i] + extra
        v3[2 + 2 * i] = w3[2 + 2 * i] + extra
    join_halves(v3, h3)
    loop(1, h3 + 1, sweep3, h3)
    join_halves(w3, h3)

    def sweep3_again(i):
        here, total = neighbours(w3, wx3, wy3, wz3, i)
        return [(v3, i, 0.2 * here + q3[i] * (b3[i] + total))]

    loop(1, h3 + 1, sweep3_again, h3)


def up_kernel(
    count_x, count_y,
    all_ref, *rest,
):
    far, rest = rest[:FAR_COUNT], rest[FAR_COUNT:]
    solution_far, residual_far = rest[:2]
    near, rest = rest[2 : 2 + FAR_COUNT], rest[2 + FAR_COUNT :]
    grids, rest = rest[:19], rest[19:]
    v2, w2, b2, v1, b1, c1, wx1, wy1, wz1, d1, q1, w1, spread1 = rest[:13]
    v0, w0, spread0, solution_ref, residual_ref, sems = rest[13:]
    (wx2, wy2, wz2, q2, own2, low_ref, high_ref, below_ref, above_ref,
     g1_mid, g1_below, g1_above, c1_ref, low0, high0, below0, above0, v1_ref, v_own,
     wx0, wy0, wz0, q0, b0, d0, g_ref) = near
    copies = start_copies(far, near, sems, 0)
    v3 = grids[0]
    solve_coarse(count_x, count_y, all_ref, *grids)
    wait_copies(copies[:19])
    place_x, place_y = lax.axis_index("gx"), lax.axis_index("gy")
    n3, h3 = 2 * count_x, count_x
    sides = ends("gx", count_x) + ends("gy", count_y)
    first, last, low_y, high_y = sides

    fill_c1(c1, c1_ref, low0, high0, below0, above0, *sides)
    fill_g1(w1, g1_mid, g1_below, g1_above, low_y, high_y)
    in_y = inside((Y1, Z1), 0, place_y * 8 - OY1, 8 * count_y).astype(F32)
    make_faces(
        c1, wx1, wy1, wz1, d1, q1, 5, X1 - 5, lambda i: flag(place_x * 8 - OX1 + i, 8 * count_x), in_y, 2
    )

    def begin1(i):
        return [(b1, i, q1[i] * w1[i])]

    loop(5, X1 - 5, begin1, 2)

    slabs = []
    for j in range(6):
        at = 2 * place_x - 2 + j
        cells = v3[1 + jnp.clip(at - jnp.where(at < h3, 0, h3), 0, h3 - 1)]
        slabs.append(cells * flag(at, h3) + pltpu.roll(cells, 64, 1) * flag(at - h3, h3))
    wide = split_dot(jnp.concatenate(slabs, axis=0), copy_matrix(LANES, LANES))
    target, origin = iota((Y2, Y3), 0), iota((Y2, Y3), 1)
    rows = jnp.logical_and(origin == 2 * place_y - 2 + target // 2, target < 12).astype(F32).astype(BF16)
    half = iota((8, Z2), 0) < 4
    wide = jnp.concatenate([wide[Y3 * j : Y3 * j + Y3] for j in range(6)], axis=1)
    wide = split_dot_left(rows, wide)
    for j in range(6):
        extra = lanes(wide, j)
        for k in range(2):
            i = 2 * j + k
            at = slice(LANES * (i % 4), LANES * (i % 4) + LANES)
            mid = own2[:, at] if i // 4 == 1 else low_ref[6, :, at] * first if i < 4 else high_ref[6, :, at] * last
            below = below_ref[11 + i // 4, :, at] * low_y
            above = above_ref[11 + i // 4, :, at] * high_y
            v2[i, 0:8] = jnp.where(half, below, pltpu.roll(mid, 4, 0)) + extra[0:8]
            v2[i, 8:16] = jnp.where(half, above, 0.0) + extra[8:16]
            b2[i, 0:8] = jnp.where(half, pltpu.roll(below, 4, 0), mid)
            b2[i, 8:16] = jnp.where(half, pltpu.roll(above, 4, 0), 0.0)
    for i in range(1, X2 - 1):
        b2[i] = q2[i] * b2[i]
    sweep(v2, w2, b2, wx2, wy2, wz2, q2, 1, X2 - 1, 10)
    sweep(w2, v2, b2, wx2, wy2, wz2, q2, 2, X2 - 2, 8)

    spread1[...] = jnp.zeros(spread1.shape, F32)
    for j in range(8):
        double_rows(spread1, j, v2[2 + j, 2:10], 4)
    for j in range(8):
        extra = doubled(spread1, j)
        extra = jnp.concatenate([extra[0], extra[0]], axis=1)
        for k in range(2):
            i = 4 + 2 * j + k
            v1[i] = v1_ref[i - 4] + extra
    sweep(v1, w1, b1, wx1, wy1, wz1, q1, 5, X1 - 5, 7)
    sweep(w1, v1, b1, wx1, wy1, wz1, q1, 6, X1 - 6, 6)

    half = iota((8, Z0), 0) < 4
    wait_copies(copies[19:])
    for j in range(12):
        double_rows(spread0, j, v1[6 + j, 6:18], 0)
    for j in range(12):
        extra = doubled(spread0, j)
        extra = jnp.concatenate([extra[k // 2] for k in range(Z0 // LANES)], axis=1)
        for k in range(2):
            i = 2 * j - 1 + k
            if i < 0 or i >= X0:
                continue
            if i < 3:
                own = [low_ref[2 * i + side] * first for side in range(2)]
            elif i < 19:
                own = [v_own[i - 3, 8 * side : 8 * side + 8, :] for side in range(2)]
            else:
                own = [high_ref[2 * (i - 19) + side] * last for side in range(2)]
            below, above = below_ref[i // 2] * low_y, above_ref[i // 2] * high_y
            if i % 2:
                below = pltpu.roll(below, 4, 0)
            else:
                above = pltpu.roll(above, 4, 0)
            head, tail = pltpu.roll(own[0], 4, 0), pltpu.roll(own[1], 4, 0)
            v0[i, 0:8] = jnp.where(half, below, head) + extra[0:8]
            v0[i, 8:16] = jnp.where(half, head, tail) + extra[8:16]
            v0[i, 16:24] = jnp.where(half, tail, above) + extra[16:24]
    sweep(v0, w0, b0, wx0, wy0, wz0, q0, 1, X0 - 1, 2)
    sweep(w0, v0, b0, wx0, wy0, wz0, q0, 2, X0 - 2, 2)

    pick = collect_matrix(Z0)
    rows = jnp.concatenate([pltpu.roll(v0[i + OX0], Y0 - OY0, 0)[0:16] for i in range(16)], axis=0)
    solution_ref[...] = split_dot(rows, pick).reshape(16, 16, Z0)
    copies = start_copies((solution_ref,), (solution_far,), sems, FAR_COUNT)

    def finish(i):
        here, total = neighbours(v0, wx0, wy0, wz0, i + OX0)
        return [(residual_ref, i, pltpu.roll(total - d0[i + OX0] * here, Y0 - OY0, 0)[0:16])]

    loop(0, 16, finish, 2)
    for part in range(2):
        here = pl.ds(8 * part, 8)
        rows = residual_ref[here].reshape(128, Z0)
        residual_ref[here] = g_ref[here] + split_dot(rows, pick).reshape(8, 16, Z0)
        copies += start_copies((residual_ref.at[here],), (residual_far.at[here],), sems, FAR_COUNT + 1 + part)
    wait_copies(copies)


def up(count_x, count_y, everything, *operands):
    frame0, frame1, frame2 = (X0, Y0, Z0), (X1, Y1, Z1), (X2, Y2, Z2)
    frame3, frame4 = (count_x + 2, Y3, LANES), (count_x // 2 + 2, Y4, LANES)
    return call(
        functools.partial(up_kernel, count_x, count_y),
        [struct(16, 16, Z0), struct(16, 16, Z0)],
        [vmem(*operand.shape) for operand in operands]
        + [vmem(*frame3)] * 9 + [vmem(count_x, Y3, LANES)]
        + [vmem(*frame4)] * 6 + [vmem(count_x // 2, Y4, LANES), vmem(*frame4), vmem(count_x // 2, Y3, LANES)]
        + [vmem(*frame2)] * 3 + [vmem(*frame1)] * 9 + [vmem(8, 1, Y1, LANES)]
        + [vmem(*frame0)] * 2 + [vmem(12, Z1 // LANES, Y0, LANES)] + [vmem(16, 16, Z0)] * 2
        + [pltpu.SemaphoreType.DMA((FAR_COUNT + 3,))],
        60,
        in_specs=[WHOLE] + [FAR] * FAR_COUNT,
        out_specs=[FAR] * 2,
    )(everything, *operands)


def to_next(cells, axis):
    count = lax.axis_size(axis)
    return lax.ppermute(cells, axis, [(i, (i + 1) % count) for i in range(count)])


def to_previous(cells, axis):
    count = lax.axis_size(axis)
    return lax.ppermute(cells, axis, [((i + 1) % count, i) for i in range(count)])


def shards(right_side, coefficient):
    count_x, count_y = lax.axis_size("gx"), lax.axis_size("gy")
    place_x = lax.axis_index("gx")

    def with_sides(low, cells, high):
        low = jnp.where(place_x > 0, low, 0.0)
        high = jnp.where(place_x < count_x - 1, high, 0.0)
        return jnp.concatenate([low, cells, high], axis=0)

    to_right, to_left, c1 = begin(coefficient, right_side)
    low, high = to_next(to_right, "gx"), to_previous(to_left, "gx")
    c_own, g_own, pick = deal(coefficient, right_side)
    top, bottom, low, high = edges_y(count_x, pick, c_own, g_own, c1, low, high)
    below, above = to_next(top, "gy"), to_previous(bottom, "gy")
    g1, v_own = down0(count_x, count_y, c_own, g_own, low, high, below, above)

    g1_low, g1_high = to_next(g1[2:8], "gx"), to_previous(g1[0:6], "gx")
    levels = prepare(count_x, count_y, c1, low, high, below, above)
    wx2, wy2, wz2, q2 = levels[5], levels[6], levels[7], levels[9]
    g1_mid = with_sides(g1_low, g1, g1_high)
    g1_below, g1_above = to_next(g1_mid, "gy"), to_previous(g1_mid, "gy")
    v1, own2, send3 = down1(count_x, count_y, g1_mid, g1_below, g1_above, *levels)

    everything = lax.all_to_all(send3, ("gx", "gy"), split_axis=0, concat_axis=0, tiled=True)
    to_right, to_left = iterate_sides(v_own, own2)
    low2, high2 = to_next(to_right, "gx"), to_previous(to_left, "gx")
    top, bottom = iterate_edges(count_x, v_own, own2, low2, high2)
    below2, above2 = to_next(top, "gy"), to_previous(bottom, "gy")
    c_own, send3 = lax.optimization_barrier((c_own, send3))
    weights = weights0(count_x, count_y, c_own, g_own, low, high, below, above)
    wx0, wy0, wz0, d0, q0, b0 = weights
    return tuple(
        up(
            count_x, count_y, everything, wx2, wy2, wz2, q2, own2, low2, high2, below2, above2,
            g1_mid, g1_below, g1_above, c1, low, high, below, above, v1, v_own,
            wx0, wy0, wz0, q0, b0, d0, right_side,
        )
    )


def solution(mesh):
    specs = (P("gx", "gy", None), P("gx", "gy", None))
    return jax.shard_map(shards, mesh=mesh, in_specs=specs, out_specs=specs, check_vma=False)
```

```python
import functools

import jax
import jax.numpy as jnp
from jax import lax
from jax.experimental import pallas as pl
from jax.experimental.pallas import tpu as pltpu
from jax.sharding import PartitionSpec as P

F32 = jnp.float32
BF16 = jnp.bfloat16
OMEGA = 0.8
BOTTOM = 16
MIB = 1024 * 1024

X0, Y0, Z0, OX0, OY0 = 22, 24, 512, 3, 4
X1, Y1, Z1, OX1, OY1 = 24, 24, 256, 8, 8
X2, Y2, Z2, OX2, OY2 = 12, 16, 128, 4, 4
Y3, Y4, LANES = 16, 8, 128
C_TILES, CG_TILES = 11, 16


def iota(shape, dim):
    return lax.broadcasted_iota(jnp.int32, shape, dim)


def up_of(cells, dim):
    if dim == 0 or cells.shape[1] == LANES:
        return pltpu.roll(cells, cells.shape[dim] - 1, dim)
    return jnp.concatenate([cells[:, LANES:], pltpu.roll(cells[:, :LANES], LANES - 1, 1)], axis=1)


def down_of(cells, dim):
    if dim == 0 or cells.shape[1] == LANES:
        return pltpu.roll(cells, 1, dim)
    return jnp.concatenate([pltpu.roll(cells[:, -LANES:], 1, 1), cells[:, :-LANES]], axis=1)


def cell_of(position, count):
    pieces = count // LANES
    return pieces * (position % LANES) + position // LANES


def deal_matrix(count):
    hit = iota((count, count), 0) == cell_of(iota((count, count), 1), count)
    return hit.astype(F32).astype(BF16)


def collect_matrix(count):
    hit = cell_of(iota((count, count), 0), count) == iota((count, count), 1)
    return hit.astype(F32).astype(BF16)


def pair_sums(cells):
    pieces = [lanes(cells, k) for k in range(cells.shape[1] // LANES)]
    sums = [even + odd for even, odd in zip(pieces[::2], pieces[1::2])]
    return jnp.concatenate(sums, axis=1) if len(sums) > 1 else sums[0]


def split_dot(cells, pick):
    high = cells.astype(BF16)
    rest = cells - high.astype(F32)
    mid = rest.astype(BF16)
    low = (rest - mid.astype(F32)).astype(BF16)
    count = cells.shape[0]
    all_pieces = jnp.dot(jnp.concatenate([high, mid, low], axis=0), pick, preferred_element_type=F32)
    return all_pieces[:count] + (all_pieces[count : 2 * count] + all_pieces[2 * count :])


def split_dot_left(pick, cells):
    high = cells.astype(BF16)
    rest = cells - high.astype(F32)
    mid = rest.astype(BF16)
    low = (rest - mid.astype(F32)).astype(BF16)
    dot = functools.partial(jnp.dot, preferred_element_type=F32)
    return dot(pick, high) + (dot(pick, mid) + dot(pick, low))


def pair_sum_matrix(fine, coarse, offset=0):
    hit = (iota((fine, coarse), 0) // 2) + offset == iota((fine, coarse), 1)
    return hit.astype(F32).astype(BF16)


def pair_deal_matrix(fine, coarse):
    hit = iota((fine, coarse), 0) // 2 == cell_of(iota((fine, coarse), 1), coarse)
    return hit.astype(F32).astype(BF16)


def copy_matrix(coarse, fine):
    hit = iota((coarse, fine), 0) == iota((coarse, fine), 1) // 2
    return hit.astype(F32).astype(BF16)


def inside(shape, dim, start, count):
    place = iota(shape, dim) + start
    return jnp.logical_and(place >= 0, place < count)


def flag(start, count):
    return jnp.where(jnp.logical_and(start >= 0, start < count), 1.0, 0.0).astype(F32)


def loop(first, last, body, width=1):
    def run(i, count):
        stores = [store for j in range(count) for store in body(i + j)]
        for ref, at, value in stores:
            ref[at] = value

    count = (last - first) // width

    def step(t, carry):
        run(first + t * width, width)
        return carry

    if count == 1:
        run(first, width)
    else:
        lax.fori_loop(0, count, step, 0)
    if (last - first) % width:
        run(first + count * width, (last - first) % width)


def inverse(total):
    total = jnp.maximum(total, 1e-30)
    guess = pl.reciprocal(total, approx=True)
    guess = guess * (2.0 - total * guess)
    return guess * (2.0 - total * guess)


def make_faces(c, wx, wy, wz, d, q, first, last, in_x, in_y, width, whole_y=0, period=0):
    rows, cells = c.shape[1], c.shape[2]
    period = period or cells
    end_z = iota((rows, cells), 1) % period == period - 1
    start_z = iota((rows, cells), 1) % period == 0
    row = iota((rows, cells), 0)
    wx[first - 1] = 0.5 * (c[first - 1] + c[first])

    def body(i):
        here = c[i]
        after = c[i + 1]
        before = c[i - 1]
        y_up, y_down = up_of(here, 0), down_of(here, 0)
        if whole_y:
            y_up = jnp.where(row == rows - 1, 0.0, y_up)
            y_down = jnp.where(row == 0, 0.0, y_down)
        z_up = jnp.where(end_z, 0.0, up_of(here, 1))
        z_down = jnp.where(start_z, 0.0, down_of(here, 1))
        side = 0.5 * (here + y_up)
        side = jnp.where(row == rows - 1, 0.0, side) if whole_y else side
        total = 3.0 * here + 0.5 * ((after + before) + (y_up + y_down) + (z_up + z_down))
        return [
            (wx, i, 0.5 * (here + after)),
            (wy, i, side),
            (wz, i, jnp.where(end_z, 0.0, 0.5 * (here + z_up))),
            (d, i, total),
            (q, i, (in_y * (OMEGA * in_x(i))) * inverse(total)),
        ]

    loop(first, last, body, width)


def neighbours(v, wx, wy, wz, i):
    here = v[i]
    side_y, side_z = wy[i], wz[i]
    along_x = wx[i] * v[i + 1] + wx[i - 1] * v[i - 1]
    along_y = side_y * up_of(here, 0) + down_of(side_y * here, 0)
    along_z = side_z * up_of(here, 1) + down_of(side_z * here, 1)
    return here, along_x + along_y + along_z


def sweep(v, out, b, wx, wy, wz, q, first, last, width):
    def body(i):
        here, total = neighbours(v, wx, wy, wz, i)
        return [(out, i, (0.2 * here + b[i]) + q[i] * total)]

    loop(first, last, body, width)


def defect(v, source, wx, wy, wz, d, i):
    here, total = neighbours(v, wx, wy, wz, i)
    return (source[i] - d[i] * here) + total


def lanes(cells, k):
    return cells[:, LANES * k : LANES * k + LANES]


def keep(scratch, j, cells):
    for k in range(cells.shape[1] // LANES):
        scratch[j, k] = lanes(cells, k)


def halve_rows(scratch, j, start, count):
    parts = [
        scratch[j, k, pl.ds(start, count, stride=2), :] + scratch[j, k, pl.ds(start + 1, count, stride=2), :]
        for k in range(scratch.shape[1])
    ]
    return jnp.concatenate(parts, axis=1)


def double_rows(scratch, j, cells, start):
    for k in range(scratch.shape[1]):
        for odd in range(2):
            scratch[j, k, pl.ds(start + odd, cells.shape[0], stride=2), :] = lanes(cells, k)


def doubled(scratch, j):
    return [scratch[j, k] for k in range(scratch.shape[1])]


def call(kernel, out_shape, scratch, limit, in_specs=None, out_specs=None, flops=1000000, bytes_accessed=1000000):
    extra = {}
    if in_specs is not None:
        extra["in_specs"] = in_specs
    if out_specs is not None:
        extra["out_specs"] = out_specs
    return pl.pallas_call(
        kernel,
        out_shape=out_shape,
        scratch_shapes=scratch,
        compiler_params=pltpu.CompilerParams(vmem_limit_bytes=limit * MIB),
        cost_estimate=pl.CostEstimate(flops=flops, bytes_accessed=bytes_accessed, transcendentals=0),
        **extra,
    )


def struct(*shape):
    return jax.ShapeDtypeStruct(shape, F32)


def vmem(*shape):
    return pltpu.VMEM(shape, F32)


WHOLE = pl.BlockSpec(memory_space=pltpu.VMEM)
FAR = pl.BlockSpec(memory_space=pl.ANY)
FAR_COUNT = 26


def start_copies(sources, targets, sems, first):
    copies = [
        pltpu.make_async_copy(source, target, sems.at[first + k])
        for k, (source, target) in enumerate(zip(sources, targets))
    ]
    for copy in copies:
        copy.start()
    return copies


def wait_copies(copies):
    for copy in copies:
        copy.wait()


def place_of(i):
    row, cell = 8 * ((i // 2) % 2), Z1 * (i % 2)
    return 5 + i // 4, slice(row, row + 8), slice(cell, cell + Z1)


def begin_kernel(c_ref, g_ref, next_ref, previous_ref, c1_ref, pairs):
    for i in range(8):
        keep(pairs, i, c_ref[2 * i] + c_ref[2 * i + 1])
    for i in range(3):
        next_ref[i] = c_ref[13 + i]
        previous_ref[i] = c_ref[i]
    for i in range(2):
        next_ref[3 + i] = g_ref[14 + i]
        previous_ref[3 + i] = g_ref[i]
    rows = jnp.concatenate([halve_rows(pairs, i, 0, 8) for i in range(8)], axis=0)
    small = 0.125 * split_dot(rows, pair_deal_matrix(Z0, Z1))
    for i in range(8):
        block = small[8 * i : 8 * i + 8]
        c1_ref[i] = block
        next_ref[place_of(i)] = block
        previous_ref[place_of(i)] = block


def begin(coefficient, right_side):
    return call(
        begin_kernel, [struct(7, 16, Z0), struct(7, 16, Z0), struct(8, 8, Z1)], [vmem(8, Z0 // LANES, 16, LANES)], 8
    )(coefficient, right_side)


def deal_kernel(c_ref, g_ref, c_out, g_out, pick_out):
    pick = deal_matrix(Z0)
    pick_out[...] = pick
    for ref, out in ((c_ref, c_out), (g_ref, g_out)):
        out[...] = split_dot(ref[...].reshape(256, Z0), pick).reshape(16, 16, Z0)


def deal(coefficient, right_side):
    pick = jax.ShapeDtypeStruct((Z0, Z0), BF16)
    return call(deal_kernel, [struct(16, 16, Z0), struct(16, 16, Z0), pick], [], 8)(coefficient, right_side)


def edge_kernel(
    count_x, pick_ref, c_ref, g_ref, c1_ref, low_raw, high_raw, top_ref, bottom_ref, low_ref, high_ref
):
    pick = pick_ref[...]
    for raw, out in ((low_raw, low_ref), (high_raw, high_ref)):
        out[0:5] = split_dot(raw[0:5].reshape(80, Z0), pick).reshape(5, 16, Z0)
        out[5:7] = raw[5:7]
    place = lax.axis_index("gx")
    first = jnp.where(place > 0, 1.0, 0.0).astype(F32)
    last = jnp.where(place < count_x - 1, 1.0, 0.0).astype(F32)
    row = iota((8, Z0), 0)

    def c_part(i, half):
        rows = slice(8 * half, 8 * half + 8)
        if i < 3:
            return low_ref[i, rows, :] * first
        return c_ref[i - 3, rows, :] if i < 19 else high_ref[i - 19, rows, :] * last

    def g_part(i, half):
        rows = slice(8 * half, 8 * half + 8)
        if i < 3:
            return low_ref[i + 2, rows, :] * first
        return g_ref[i - 3, rows, :] if i < 19 else high_ref[i - 16, rows, :] * last

    for j in range(X0 // 2):
        top_ref[j] = jnp.where(row < 4, pltpu.roll(c_part(2 * j, 1), 4, 0), c_part(2 * j + 1, 1))
        bottom_ref[j] = jnp.where(row < 4, c_part(2 * j, 0), pltpu.roll(c_part(2 * j + 1, 0), 4, 0))
    for j in range(5):
        top, bottom = g_part(1 + 4 * j, 1), g_part(1 + 4 * j, 0)
        top = pltpu.roll(top, 2, 0)
        for k in range(1, 4):
            part = g_part(1 + 4 * j + k, 1)
            part = pltpu.roll(part, (2 * k + 2) % 8, 0) if k < 3 else part
            top = jnp.where(row // 2 == k, part, top)
            bottom = jnp.where(row // 2 == k, pltpu.roll(g_part(1 + 4 * j + k, 0), 2 * k, 0), bottom)
        top_ref[C_TILES + j] = top
        bottom_ref[C_TILES + j] = bottom
    for i in range(24):
        part = low_ref[place_of(i)] * first if i < 8 else c1_ref[i - 8] if i < 16 else high_ref[place_of(i - 16)] * last
        for ref in (top_ref, bottom_ref):
            ref[CG_TILES + i // 2, :, Z1 * (i % 2) : Z1 * (i % 2) + Z1] = part


def edges_y(count_x, *operands):
    return call(
        functools.partial(edge_kernel, count_x), [struct(CG_TILES + 12, 8, Z0)] * 2 + [struct(7, 16, Z0)] * 2, [], 8
    )(*operands)


def ends(axis, count):
    place = lax.axis_index(axis)
    low = jnp.where(place > 0, 1.0, 0.0).astype(F32)
    return low, jnp.where(place < count - 1, 1.0, 0.0).astype(F32)


def window0(low_ref, high_ref, below_ref, above_ref, c_ref, g_ref, first, last, low_y, high_y):
    row = iota((8, Z0), 0) < 4

    def put(own, below, above):
        head, tail = pltpu.roll(own[0:8], 4, 0), pltpu.roll(own[8:16], 4, 0)
        parts = [jnp.where(row, below, head), jnp.where(row, head, tail), jnp.where(row, tail, above)]
        return jnp.concatenate(parts, axis=0)

    def turn(cells, rows):
        return pltpu.roll(cells, rows % 8, 0) if rows % 8 else cells

    def c_slab(i, own):
        odd = i % 2
        below = turn(below_ref[i // 2], 4 * odd) * low_y
        return put(own, below, turn(above_ref[i // 2], 4 - 4 * odd) * high_y)

    def g_slab(i, own):
        tile, k = C_TILES + (i - 1) // 4, (i - 1) % 4
        below = turn(below_ref[tile], 2 - 2 * k) * low_y
        return put(own, below, turn(above_ref[tile], 4 - 2 * k) * high_y)

    def fill(c, g):
        for i in range(3):
            c[i] = c_slab(i, low_ref[i] * first)
            c[19 + i] = c_slab(19 + i, high_ref[i] * last)
        for i in range(3, 19):
            c[i] = c_slab(i, c_ref[i - 3])
        for i in (1, 2):
            g[i] = g_slab(i, low_ref[i + 2] * first)
            g[18 + i] = g_slab(18 + i, high_ref[i + 2] * last)
        for i in range(3, 19):
            g[i] = g_slab(i, g_ref[i - 3])

    return fill


def down0_kernel(
    count_x, count_y,
    c_ref, g_ref, low_ref, high_ref, below_ref, above_ref,
    g1_ref, v_own_ref, c, g, wx, wy, wz, d, q, b, v, pairs,
):
    place_x, place_y = lax.axis_index("gx"), lax.axis_index("gy")
    sides = ends("gx", count_x) + ends("gy", count_y)
    window0(low_ref, high_ref, below_ref, above_ref, c_ref, g_ref, *sides)(c, g)
    in_y = inside((Y0, Z0), 0, place_y * 16 - OY0, 16 * count_y).astype(F32)
    make_faces(
        c, wx, wy, wz, d, q, 1, X0 - 1, lambda i: flag(place_x * 16 - OX0 + i, 16 * count_x), in_y, 4
    )

    def begin(i):
        return [(b, i, q[i] * g[i])]

    loop(1, X0 - 1, begin, 2)
    sweep(b, v, b, wx, wy, wz, q, 2, X0 - 2, 6)

    def own_of(i):
        return [(v_own_ref, i, pltpu.roll(v[i + 3], Y0 - OY0, 0)[0:16])]

    loop(0, 16, own_of, 2)

    def restrict(j):
        i = 2 * j + OX0
        both = defect(v, g, wx, wy, wz, d, i) + defect(v, g, wx, wy, wz, d, i + 1)
        return [(pairs, (j, k), lanes(both, k)) for k in range(Z0 // LANES)]

    loop(0, 8, restrict, 2)
    rows = jnp.concatenate([halve_rows(pairs, i, 4, 8) for i in range(8)], axis=0)
    g1_ref[...] = (0.5 * pair_sums(rows)).reshape(8, 8, Z1)


def down0(count_x, count_y, *operands):
    frame = (X0, Y0, Z0)
    return call(
        functools.partial(down0_kernel, count_x, count_y),
        [struct(8, 8, Z1), struct(16, 16, Z0)],
        [vmem(*frame)] * 9 + [vmem(8, Z0 // LANES, Y0, LANES)],
        18,
    )(*operands)


def fill_c1(c1, c1_ref, low_ref, high_ref, below_ref, above_ref, first, last, low_y, high_y):
    for i in range(24):
        at = CG_TILES + i // 2, slice(0, 8), slice(Z1 * (i % 2), Z1 * (i % 2) + Z1)
        part = low_ref[place_of(i)] * first if i < 8 else c1_ref[i - 8] if i < 16 else high_ref[place_of(i - 16)] * last
        c1[i, 0:8, :] = below_ref[at] * low_y
        c1[i, 8:16, :] = part
        c1[i, 16:24, :] = above_ref[at] * high_y


def prepare_kernel(
    count_x, count_y, c1_ref, low_ref, high_ref, below_ref, above_ref,
    wx1, wy1, wz1, d1, q1, wx2, wy2, wz2, d2, q2, c3_ref, c1, c2, pairs,
):
    place_x, place_y = lax.axis_index("gx"), lax.axis_index("gy")
    sides = ends("gx", count_x) + ends("gy", count_y)
    fill_c1(c1, c1_ref, low_ref, high_ref, below_ref, above_ref, *sides)
    in_y = inside((Y1, Z1), 0, place_y * 8 - OY1, 8 * count_y).astype(F32)
    make_faces(
        c1, wx1, wy1, wz1, d1, q1, 2, X1 - 2, lambda i: flag(place_x * 8 - OX1 + i, 8 * count_x), in_y, 5
    )
    for i in range(12):
        keep(pairs, i, c1[2 * i] + c1[2 * i + 1])
    blank = jnp.zeros((4, Z1), F32)
    rows = []
    for i in range(12):
        rows.append(halve_rows(pairs, i, 0, 12))
        rows.append(blank)
    c2[...] = (0.125 * pair_sums(jnp.concatenate(rows, axis=0))).reshape(X2, Y2, Z2)
    in_y = inside((Y2, Z2), 0, place_y * 4 - OY2, 4 * count_y).astype(F32)
    make_faces(
        c2, wx2, wy2, wz2, d2, q2, 1, X2 - 1, lambda i: flag(place_x * 4 - OX2 + i, 4 * count_x), in_y, 10
    )
    rows = jnp.concatenate([c2[4] + c2[5], c2[6] + c2[7]], axis=0)
    thin = 0.125 * split_dot(rows, pair_sum_matrix(Z2, LANES, 64))
    row = iota((8, LANES), 0)
    c3 = jnp.zeros((8, LANES), F32)
    for i in range(2):
        for j in range(2):
            at = 16 * i + 4 + 2 * j
            both = thin[at : at + 1] + thin[at + 1 : at + 2]
            c3 = jnp.where(row == 2 * i + j, jnp.broadcast_to(both, (8, LANES)), c3)
    c3_ref[...] = c3


def prepare(count_x, count_y, *operands):
    frame1, frame2 = (X1, Y1, Z1), (X2, Y2, Z2)
    return call(
        functools.partial(prepare_kernel, count_x, count_y),
        [struct(*frame1)] * 5 + [struct(*frame2)] * 5 + [struct(8, LANES)],
        [vmem(*frame1), vmem(*frame2), vmem(12, Z1 // LANES, Y1, LANES)],
        8,
    )(*operands)


def fill_g1(g1, mid_ref, below_ref, above_ref, low_y, high_y):
    g1[2:22, 0:8, :] = below_ref[...] * low_y
    g1[2:22, 8:16, :] = mid_ref[...]
    g1[2:22, 16:24, :] = above_ref[...] * high_y


def down1_kernel(
    count_x, count_y, mid_ref, below_ref, above_ref,
    wx1, wy1, wz1, d1, q1, wx2, wy2, wz2, d2, q2, c3_ref,
    v_far, send2_ref, send3_ref, v1_ref, b1_ref, g1, g2, b2, v2, pairs, thin,
):
    place_y = lax.axis_index("gy")
    low_y = jnp.where(place_y > 0, 1.0, 0.0).astype(F32)
    high_y = jnp.where(place_y < count_y - 1, 1.0, 0.0).astype(F32)
    fill_g1(g1, mid_ref, below_ref, above_ref, low_y, high_y)

    def begin1(i):
        return [(b1_ref, i, q1[i] * g1[i])]

    loop(2, X1 - 2, begin1, 10)
    sweep(b1_ref, v1_ref, b1_ref, wx1, wy1, wz1, q1, 3, X1 - 3, 6)

    def restrict(j):
        i = 2 * j + 4
        after = defect(v1_ref, g1, wx1, wy1, wz1, d1, i + 1)
        both = defect(v1_ref, g1, wx1, wy1, wz1, d1, i) + after
        return [(pairs, (j, k), lanes(both, k)) for k in range(Z1 // LANES)]

    loop(0, 8, restrict, 4)
    rows = jnp.concatenate([halve_rows(pairs, i, 4, 8) for i in range(8)], axis=0)
    small = 0.5 * pair_sums(rows)
    g2[...] = jnp.zeros((X2, Y2, Z2), F32)
    for i in range(8):
        g2[2 + i, 2:10, :] = small[8 * i : 8 * i + 8]
    for i in range(2, X2 - 2):
        b2[i] = q2[i] * g2[i]
    sweep(b2, v2, b2, wx2, wy2, wz2, q2, 3, X2 - 3, 6)
    row = iota((8, Z2), 0) < 4
    for i in range(4):
        both = jnp.where(row, pltpu.roll(v2[4 + i, 0:8, :], 4, 0), g2[4 + i, 0:8, :])
        send2_ref[:, LANES * i : LANES * i + LANES] = both
    halves = [
        defect(v2, g2, wx2, wy2, wz2, d2, 4 + 2 * i) + defect(v2, g2, wx2, wy2, wz2, d2, 5 + 2 * i)
        for i in range(2)
    ]
    thin[...] = 0.5 * split_dot(jnp.concatenate(halves, axis=0), pair_sum_matrix(Z2, LANES))
    row = iota((8, LANES), 0)
    source = jnp.zeros((8, LANES), F32)
    for i in range(2):
        for j in range(2):
            at = 16 * i + 4 + 2 * j
            both = thin[at : at + 1, :] + thin[at + 1 : at + 2, :]
            source = jnp.where(row == 2 * i + j, jnp.broadcast_to(both, (8, LANES)), source)
    source = source + c3_ref[...]
    double = jnp.where(row < 4, source, pltpu.roll(source, 4, 0))
    for i in range(count_x * count_y // 2):
        send3_ref[8 * i : 8 * i + 8, :] = double
    v_far[...] = v1_ref[4:20]


def down1(count_x, count_y, *operands):
    frame1, frame2 = (X1, Y1, Z1), (X2, Y2, Z2)
    return call(
        functools.partial(down1_kernel, count_x, count_y),
        [struct(16, Y1, Z1), struct(8, Z0)]
        + [struct(4 * count_x * count_y, LANES)],
        [vmem(*frame1)] * 3 + [vmem(*frame2)] * 3 + [vmem(8, Z1 // LANES, Y1, LANES), vmem(32, LANES)],
        8,
    )(*operands)


def iterate_side_kernel(own_ref, own2_ref, next_ref, previous_ref):
    for i in range(3):
        for half in range(2):
            next_ref[2 * i + half] = own_ref[13 + i, 8 * half : 8 * half + 8, :]
            previous_ref[2 * i + half] = own_ref[i, 8 * half : 8 * half + 8, :]
    next_ref[6] = own2_ref[...]
    previous_ref[6] = own2_ref[...]


def iterate_sides(*operands):
    return call(iterate_side_kernel, [struct(7, 8, Z0), struct(7, 8, Z0)], [], 8)(*operands)


def iterate_edge_kernel(count_x, own_ref, own2_ref, low_ref, high_ref, top_ref, bottom_ref):
    place = lax.axis_index("gx")
    first = jnp.where(place > 0, 1.0, 0.0).astype(F32)
    last = jnp.where(place < count_x - 1, 1.0, 0.0).astype(F32)
    row = iota((8, Z0), 0) < 4

    def slab(i, half):
        if i < 3:
            return low_ref[2 * i + half] * first
        if i < 19:
            return own_ref[i - 3, 8 * half : 8 * half + 8, :]
        return high_ref[2 * (i - 19) + half] * last

    for j in range(X0 // 2):
        top_ref[j] = jnp.where(row, pltpu.roll(slab(2 * j, 1), 4, 0), slab(2 * j + 1, 1))
        bottom_ref[j] = jnp.where(row, slab(2 * j, 0), pltpu.roll(slab(2 * j + 1, 0), 4, 0))
    for ref in (top_ref, bottom_ref):
        ref[11] = low_ref[6] * first
        ref[12] = own2_ref[...]
        ref[13] = high_ref[6] * last


def iterate_edges(count_x, *operands):
    return call(
        functools.partial(iterate_edge_kernel, count_x), [struct(14, 8, Z0), struct(14, 8, Z0)], [], 8
    )(*operands)


def weights0_kernel(
    count_x, count_y, c_ref, g_ref, low0, high0, below0, above0, *rest,
):
    stored, (c, g, wx, wy, wz, d, q, b, sems) = rest[:6], rest[6:]
    place_x, place_y = lax.axis_index("gx"), lax.axis_index("gy")
    sides = ends("gx", count_x) + ends("gy", count_y)
    window0(low0, high0, below0, above0, c_ref, g_ref, *sides)(c, g)
    in_y = inside((Y0, Z0), 0, place_y * 16 - OY0, 16 * count_y).astype(F32)
    make_faces(
        c, wx, wy, wz, d, q, 1, X0 - 1, lambda i: flag(place_x * 16 - OX0 + i, 16 * count_x), in_y, 2
    )
    copies = start_copies((wx, wy, wz, d, q), stored[:5], sems, 0)

    def begin(i):
        return [(b, i, q[i] * g[i])]

    loop(1, X0 - 1, begin, 2)
    copies += start_copies((b,), stored[5:], sems, 5)
    wait_copies(copies)


def weights0(count_x, count_y, *operands):
    frame0 = (X0, Y0, Z0)
    return call(
        functools.partial(weights0_kernel, count_x, count_y),
        [struct(*frame0)] * 6,
        [vmem(*frame0)] * 8 + [pltpu.SemaphoreType.DMA((6,))],
        60,
        in_specs=[WHOLE] * 6,
        out_specs=[FAR] * 6,
        flops=20000000,
        bytes_accessed=20000000,
    )(*operands)


def join_halves(frame, count):
    first = iota(frame.shape[1:], 1) < 64
    frame[0] = jnp.where(first, 0.0, pltpu.roll(frame[count], 64, 1))
    frame[count + 1] = jnp.where(first, pltpu.roll(frame[1], 64, 1), 0.0)


def halves_matrix(of_fine):
    fine, coarse = iota((LANES, LANES), of_fine), iota((LANES, LANES), 1 - of_fine)
    hit = jnp.logical_and(fine // 64 == coarse // 64, (fine % 64) // 2 == coarse % 64)
    return hit.astype(F32).astype(BF16)


def solve_coarse(
    count_x, count_y, all_ref, v3,
    c3, wx3, wy3, wz3, d3, q3, b3, w3, thin3,
    c4, wx4, wy4, wz4, d4, q4, g4, v4, thin4,
):
    h3, h4 = count_x, count_x // 2

    if 2 * count_y < Y3:
        c3[...] = jnp.zeros(c3.shape, F32)
        b3[...] = jnp.zeros(b3.shape, F32)
    first = iota((count_y, LANES), 1) < 64
    for i in range(h3):
        for j in range(2):
            parts = []
            for x in (i, i + h3):
                base = (x // 2) * count_y * 4 + 2 * (x % 2)
                parts.append(all_ref[pl.ds(base + j, count_y, stride=4), :])
            rows = pl.ds(j, count_y, stride=2)
            b3[1 + i, rows, :] = jnp.where(first, parts[0], pltpu.roll(parts[1], 64, 1))
            c3[1 + i, rows, :] = jnp.where(first, pltpu.roll(parts[0], 64, 1), parts[1])
    join_halves(c3, h3)
    in_y = (iota((Y3, LANES), 0) < 2 * count_y).astype(F32)
    make_faces(c3, wx3, wy3, wz3, d3, q3, 1, h3 + 1, lambda i: 1.0, in_y, min(8, h3), whole_y=1, period=64)

    def begin3(i):
        return [(v3, i, q3[i] * b3[i])]

    loop(1, h3 + 1, begin3, h3)
    join_halves(v3, h3)

    def sweep3(i):
        here, total = neighbours(v3, wx3, wy3, wz3, i)
        return [(w3, i, 0.2 * here + q3[i] * (b3[i] + total))]

    loop(1, h3 + 1, sweep3, h3)
    join_halves(w3, h3)

    def restrict3(j):
        i = 2 * j + 1
        both = defect(w3, b3, wx3, wy3, wz3, d3, i) + defect(w3, b3, wx3, wy3, wz3, d3, i + 1)
        return [(thin3, j, both), (thin3, h4 + j, c3[i] + c3[i + 1])]

    loop(0, h4, restrict3, min(4, h4))
    rows = jnp.concatenate(
        [thin3[i, pl.ds(0, Y4, stride=2), :] + thin3[i, pl.ds(1, Y4, stride=2), :] for i in range(2 * h4)], axis=0
    )
    both = split_dot(rows, halves_matrix(0)).reshape(2 * h4, Y4, LANES)
    g4[...] = 0.5 * both[:h4]
    c4[1 : h4 + 1] = 0.125 * both[h4:]
    join_halves(c4, h4)
    in_y = jnp.logical_and(iota((Y4, LANES), 0) < count_y, iota((Y4, LANES), 1) % 64 < 32).astype(F32)
    make_faces(c4, wx4, wy4, wz4, d4, q4, 1, h4 + 1, lambda i: 1.0, in_y, h4, whole_y=1, period=64)

    along_x = [wx4[i] for i in range(h4 + 1)]
    along_y, along_z = [wy4[1 + i] for i in range(h4)], [wz4[1 + i] for i in range(h4)]
    scale = [q4[1 + i] for i in range(h4)]
    start = [scale[i] * g4[i] for i in range(h4)]
    first = iota((Y4, LANES), 1) < 64

    def bottom(step, v):
        before = jnp.where(first, 0.0, pltpu.roll(v[-1], 64, 1))
        after = jnp.where(first, pltpu.roll(v[0], 64, 1), 0.0)
        padded = (before, *v, after)
        out = []
        for i, here in enumerate(v):
            total = along_x[i + 1] * padded[i + 2] + along_x[i] * padded[i]
            total += along_y[i] * up_of(here, 0) + down_of(along_y[i] * here, 0)
            total += along_z[i] * up_of(here, 1) + down_of(along_z[i] * here, 1)
            out.append((0.2 * here + start[i]) + scale[i] * total)
        return tuple(out)

    final = lax.fori_loop(0, BOTTOM - 1, bottom, tuple(start))

    wide = split_dot(jnp.concatenate(final, axis=0), halves_matrix(1)).reshape(h4, Y4, LANES)
    for i in range(h4):
        thin4[i, pl.ds(0, Y4, stride=2), :] = wide[i]
        thin4[i, pl.ds(1, Y4, stride=2), :] = wide[i]
    for i in range(h4):
        extra = thin4[i]
        v3[1 + 2 * i] = w3[1 + 2 * i] + extra
        v3[2 + 2 * i] = w3[2 + 2 * i] + extra
    join_halves(v3, h3)
    loop(1, h3 + 1, sweep3, h3)
    join_halves(w3, h3)

    def sweep3_again(i):
        here, total = neighbours(w3, wx3, wy3, wz3, i)
        return [(v3, i, 0.2 * here + q3[i] * (b3[i] + total))]

    loop(1, h3 + 1, sweep3_again, h3)


def up_kernel(
    count_x, count_y,
    all_ref, *rest,
):
    far, rest = rest[:FAR_COUNT], rest[FAR_COUNT:]
    solution_far, residual_far = rest[:2]
    near, rest = rest[2 : 2 + FAR_COUNT], rest[2 + FAR_COUNT :]
    grids, rest = rest[:19], rest[19:]
    v2, w2, b2, v1, b1, c1, wx1, wy1, wz1, d1, q1, w1, spread1 = rest[:13]
    v0, w0, spread0, solution_ref, residual_ref, sems = rest[13:]
    (wx2, wy2, wz2, q2, own2, low_ref, high_ref, below_ref, above_ref,
     g1_mid, g1_below, g1_above, c1_ref, low0, high0, below0, above0, v1_ref, v_own,
     wx0, wy0, wz0, q0, b0, d0, g_ref) = near
    copies = start_copies(far, near, sems, 0)
    v3 = grids[0]
    solve_coarse(count_x, count_y, all_ref, *grids)
    wait_copies(copies[:19])
    place_x, place_y = lax.axis_index("gx"), lax.axis_index("gy")
    n3, h3 = 2 * count_x, count_x
    sides = ends("gx", count_x) + ends("gy", count_y)
    first, last, low_y, high_y = sides

    fill_c1(c1, c1_ref, low0, high0, below0, above0, *sides)
    fill_g1(w1, g1_mid, g1_below, g1_above, low_y, high_y)
    in_y = inside((Y1, Z1), 0, place_y * 8 - OY1, 8 * count_y).astype(F32)
    make_faces(
        c1, wx1, wy1, wz1, d1, q1, 5, X1 - 5, lambda i: flag(place_x * 8 - OX1 + i, 8 * count_x), in_y, 7
    )

    def begin1(i):
        return [(b1, i, q1[i] * w1[i])]

    loop(5, X1 - 5, begin1, 2)

    slabs = []
    for j in range(6):
        at = 2 * place_x - 2 + j
        cells = v3[1 + jnp.clip(at - jnp.where(at < h3, 0, h3), 0, h3 - 1)]
        slabs.append(cells * flag(at, h3) + pltpu.roll(cells, 64, 1) * flag(at - h3, h3))
    wide = split_dot(jnp.concatenate(slabs, axis=0), copy_matrix(LANES, LANES))
    target, origin = iota((Y2, Y3), 0), iota((Y2, Y3), 1)
    rows = jnp.logical_and(origin == 2 * place_y - 2 + target // 2, target < 12).astype(F32).astype(BF16)
    half = iota((8, Z2), 0) < 4
    wide = jnp.concatenate([wide[Y3 * j : Y3 * j + Y3] for j in range(6)], axis=1)
    wide = split_dot_left(rows, wide)
    for j in range(6):
        extra = lanes(wide, j)
        for k in range(2):
            i = 2 * j + k
            at = slice(LANES * (i % 4), LANES * (i % 4) + LANES)
            mid = own2[:, at] if i // 4 == 1 else low_ref[6, :, at] * first if i < 4 else high_ref[6, :, at] * last
            below = below_ref[11 + i // 4, :, at] * low_y
            above = above_ref[11 + i // 4, :, at] * high_y
            v2[i, 0:8] = jnp.where(half, below, pltpu.roll(mid, 4, 0)) + extra[0:8]
            v2[i, 8:16] = jnp.where(half, above, 0.0) + extra[8:16]
            b2[i, 0:8] = jnp.where(half, pltpu.roll(below, 4, 0), mid)
            b2[i, 8:16] = jnp.where(half, pltpu.roll(above, 4, 0), 0.0)
    for i in range(1, X2 - 1):
        b2[i] = q2[i] * b2[i]
    sweep(v2, w2, b2, wx2, wy2, wz2, q2, 1, X2 - 1, 10)
    sweep(w2, v2, b2, wx2, wy2, wz2, q2, 2, X2 - 2, 8)

    spread1[...] = jnp.zeros(spread1.shape, F32)
    for j in range(8):
        double_rows(spread1, j, v2[2 + j, 2:10], 4)
    for j in range(8):
        extra = doubled(spread1, j)
        extra = jnp.concatenate([extra[0], extra[0]], axis=1)
        for k in range(2):
            i = 4 + 2 * j + k
            v1[i] = v1_ref[i - 4] + extra
    sweep(v1, w1, b1, wx1, wy1, wz1, q1, 5, X1 - 5, 7)
    sweep(w1, v1, b1, wx1, wy1, wz1, q1, 6, X1 - 6, 6)

    half = iota((8, Z0), 0) < 4
    wait_copies(copies[19:])
    for j in range(12):
        double_rows(spread0, j, v1[6 + j, 6:18], 0)
    for j in range(12):
        extra = doubled(spread0, j)
        extra = jnp.concatenate([extra[k // 2] for k in range(Z0 // LANES)], axis=1)
        for k in range(2):
            i = 2 * j - 1 + k
            if i < 0 or i >= X0:
                continue
            if i < 3:
                own = [low_ref[2 * i + side] * first for side in range(2)]
            elif i < 19:
                own = [v_own[i - 3, 8 * side : 8 * side + 8, :] for side in range(2)]
            else:
                own = [high_ref[2 * (i - 19) + side] * last for side in range(2)]
            below, above = below_ref[i // 2] * low_y, above_ref[i // 2] * high_y
            if i % 2:
                below = pltpu.roll(below, 4, 0)
            else:
                above = pltpu.roll(above, 4, 0)
            head, tail = pltpu.roll(own[0], 4, 0), pltpu.roll(own[1], 4, 0)
            v0[i, 0:8] = jnp.where(half, below, head) + extra[0:8]
            v0[i, 8:16] = jnp.where(half, head, tail) + extra[8:16]
            v0[i, 16:24] = jnp.where(half, tail, above) + extra[16:24]
    sweep(v0, w0, b0, wx0, wy0, wz0, q0, 1, X0 - 1, 4)
    sweep(w0, v0, b0, wx0, wy0, wz0, q0, 2, X0 - 2, 3)

    pick = collect_matrix(Z0)
    rows = jnp.concatenate([pltpu.roll(v0[i + OX0], Y0 - OY0, 0)[0:16] for i in range(16)], axis=0)
    solution_ref[...] = split_dot(rows, pick).reshape(16, 16, Z0)
    copies = start_copies((solution_ref,), (solution_far,), sems, FAR_COUNT)

    def finish(i):
        here, total = neighbours(v0, wx0, wy0, wz0, i + OX0)
        return [(residual_ref, i, pltpu.roll(total - d0[i + OX0] * here, Y0 - OY0, 0)[0:16])]

    loop(0, 16, finish, 4)
    for part in range(2):
        here = pl.ds(8 * part, 8)
        rows = residual_ref[here].reshape(128, Z0)
        residual_ref[here] = g_ref[here] + split_dot(rows, pick).reshape(8, 16, Z0)
        copies += start_copies((residual_ref.at[here],), (residual_far.at[here],), sems, FAR_COUNT + 1 + part)
    wait_copies(copies)


def up(count_x, count_y, everything, *operands):
    frame0, frame1, frame2 = (X0, Y0, Z0), (X1, Y1, Z1), (X2, Y2, Z2)
    frame3, frame4 = (count_x + 2, Y3, LANES), (count_x // 2 + 2, Y4, LANES)
    return call(
        functools.partial(up_kernel, count_x, count_y),
        [struct(16, 16, Z0), struct(16, 16, Z0)],
        [vmem(*operand.shape) for operand in operands]
        + [vmem(*frame3)] * 9 + [vmem(count_x, Y3, LANES)]
        + [vmem(*frame4)] * 6 + [vmem(count_x // 2, Y4, LANES), vmem(*frame4), vmem(count_x // 2, Y3, LANES)]
        + [vmem(*frame2)] * 3 + [vmem(*frame1)] * 9 + [vmem(8, 1, Y1, LANES)]
        + [vmem(*frame0)] * 2 + [vmem(12, Z1 // LANES, Y0, LANES)] + [vmem(16, 16, Z0)] * 2
        + [pltpu.SemaphoreType.DMA((FAR_COUNT + 3,))],
        60,
        in_specs=[WHOLE] + [FAR] * FAR_COUNT,
        out_specs=[FAR] * 2,
    )(everything, *operands)


def to_next(cells, axis):
    count = lax.axis_size(axis)
    return lax.ppermute(cells, axis, [(i, (i + 1) % count) for i in range(count)])


def to_previous(cells, axis):
    count = lax.axis_size(axis)
    return lax.ppermute(cells, axis, [((i + 1) % count, i) for i in range(count)])


def shards(right_side, coefficient):
    count_x, count_y = lax.axis_size("gx"), lax.axis_size("gy")
    place_x = lax.axis_index("gx")

    def with_sides(low, cells, high):
        low = jnp.where(place_x > 0, low, 0.0)
        high = jnp.where(place_x < count_x - 1, high, 0.0)
        return jnp.concatenate([low, cells, high], axis=0)

    to_right, to_left, c1 = begin(coefficient, right_side)
    low, high = to_next(to_right, "gx"), to_previous(to_left, "gx")
    c_own, g_own, pick = deal(coefficient, right_side)
    top, bottom, low, high = edges_y(count_x, pick, c_own, g_own, c1, low, high)
    below, above = to_next(top, "gy"), to_previous(bottom, "gy")
    g1, v_own = down0(count_x, count_y, c_own, g_own, low, high, below, above)

    g1_low, g1_high = to_next(g1[2:8], "gx"), to_previous(g1[0:6], "gx")
    levels = prepare(count_x, count_y, c1, low, high, below, above)
    wx2, wy2, wz2, q2 = levels[5], levels[6], levels[7], levels[9]
    g1_mid = with_sides(g1_low, g1, g1_high)
    g1_below, g1_above = to_next(g1_mid, "gy"), to_previous(g1_mid, "gy")
    v1, own2, send3 = down1(count_x, count_y, g1_mid, g1_below, g1_above, *levels)

    everything = lax.all_to_all(send3, ("gx", "gy"), split_axis=0, concat_axis=0, tiled=True)
    to_right, to_left = iterate_sides(v_own, own2)
    low2, high2 = to_next(to_right, "gx"), to_previous(to_left, "gx")
    top, bottom = iterate_edges(count_x, v_own, own2, low2, high2)
    below2, above2 = to_next(top, "gy"), to_previous(bottom, "gy")
    c_own, send3 = lax.optimization_barrier((c_own, send3))
    weights = weights0(count_x, count_y, c_own, g_own, low, high, below, above)
    wx0, wy0, wz0, d0, q0, b0 = weights
    return tuple(
        up(
            count_x, count_y, everything, wx2, wy2, wz2, q2, own2, low2, high2, below2, above2,
            g1_mid, g1_below, g1_above, c1, low, high, below, above, v1, v_own,
            wx0, wy0, wz0, q0, b0, d0, right_side,
        )
    )


def solution(mesh):
    specs = (P("gx", "gy", None), P("gx", "gy", None))
    return jax.shard_map(shards, mesh=mesh, in_specs=specs, out_specs=specs, check_vma=False)
```

```python
import functools

import jax
import jax.numpy as jnp
from jax import lax
from jax.experimental import pallas as pl
from jax.experimental.pallas import tpu as pltpu
from jax.sharding import PartitionSpec as P

F32 = jnp.float32
BF16 = jnp.bfloat16
OMEGA = 0.8
BOTTOM = 16
MIB = 1024 * 1024

X0, Y0, Z0, OX0, OY0 = 22, 24, 512, 3, 4
X1, Y1, Z1, OX1, OY1 = 24, 24, 256, 8, 8
X2, Y2, Z2, OX2, OY2 = 12, 16, 128, 4, 4
Y3, Y4, LANES = 16, 8, 128
C_TILES, CG_TILES = 11, 16


def iota(shape, dim):
    return lax.broadcasted_iota(jnp.int32, shape, dim)


def up_of(cells, dim):
    if dim == 0 or cells.shape[1] == LANES:
        return pltpu.roll(cells, cells.shape[dim] - 1, dim)
    return jnp.concatenate([cells[:, LANES:], pltpu.roll(cells[:, :LANES], LANES - 1, 1)], axis=1)


def down_of(cells, dim):
    if dim == 0 or cells.shape[1] == LANES:
        return pltpu.roll(cells, 1, dim)
    return jnp.concatenate([pltpu.roll(cells[:, -LANES:], 1, 1), cells[:, :-LANES]], axis=1)


def cell_of(position, count):
    pieces = count // LANES
    return pieces * (position % LANES) + position // LANES


def deal_matrix(count):
    hit = iota((count, count), 0) == cell_of(iota((count, count), 1), count)
    return hit.astype(F32).astype(BF16)


def collect_matrix(count):
    hit = cell_of(iota((count, count), 0), count) == iota((count, count), 1)
    return hit.astype(F32).astype(BF16)


def pair_sums(cells):
    pieces = [lanes(cells, k) for k in range(cells.shape[1] // LANES)]
    sums = [even + odd for even, odd in zip(pieces[::2], pieces[1::2])]
    return jnp.concatenate(sums, axis=1) if len(sums) > 1 else sums[0]


def split_dot(cells, pick):
    high = cells.astype(BF16)
    rest = cells - high.astype(F32)
    mid = rest.astype(BF16)
    low = (rest - mid.astype(F32)).astype(BF16)
    count = cells.shape[0]
    all_pieces = jnp.dot(jnp.concatenate([high, mid, low], axis=0), pick, preferred_element_type=F32)
    return all_pieces[:count] + (all_pieces[count : 2 * count] + all_pieces[2 * count :])


def split_dot_left(pick, cells):
    high = cells.astype(BF16)
    rest = cells - high.astype(F32)
    mid = rest.astype(BF16)
    low = (rest - mid.astype(F32)).astype(BF16)
    dot = functools.partial(jnp.dot, preferred_element_type=F32)
    return dot(pick, high) + (dot(pick, mid) + dot(pick, low))


def pair_sum_matrix(fine, coarse, offset=0):
    hit = (iota((fine, coarse), 0) // 2) + offset == iota((fine, coarse), 1)
    return hit.astype(F32).astype(BF16)


def pair_deal_matrix(fine, coarse):
    hit = iota((fine, coarse), 0) // 2 == cell_of(iota((fine, coarse), 1), coarse)
    return hit.astype(F32).astype(BF16)


def copy_matrix(coarse, fine):
    hit = iota((coarse, fine), 0) == iota((coarse, fine), 1) // 2
    return hit.astype(F32).astype(BF16)


def inside(shape, dim, start, count):
    place = iota(shape, dim) + start
    return jnp.logical_and(place >= 0, place < count)


def flag(start, count):
    return jnp.where(jnp.logical_and(start >= 0, start < count), 1.0, 0.0).astype(F32)


def loop(first, last, body, width=1):
    def run(i, count):
        stores = [store for j in range(count) for store in body(i + j)]
        for ref, at, value in stores:
            ref[at] = value

    count = (last - first) // width

    def step(t, carry):
        run(first + t * width, width)
        return carry

    if count == 1:
        run(first, width)
    else:
        lax.fori_loop(0, count, step, 0)
    if (last - first) % width:
        run(first + count * width, (last - first) % width)


def inverse(total):
    total = jnp.maximum(total, 1e-30)
    guess = pl.reciprocal(total, approx=True)
    guess = guess * (2.0 - total * guess)
    return guess * (2.0 - total * guess)


def make_faces(c, wx, wy, wz, d, q, first, last, in_x, in_y, width, whole_y=0, period=0):
    rows, cells = c.shape[1], c.shape[2]
    period = period or cells
    end_z = iota((rows, cells), 1) % period == period - 1
    start_z = iota((rows, cells), 1) % period == 0
    row = iota((rows, cells), 0)
    wx[first - 1] = 0.5 * (c[first - 1] + c[first])

    def body(i):
        here = c[i]
        after = c[i + 1]
        before = c[i - 1]
        y_up, y_down = up_of(here, 0), down_of(here, 0)
        if whole_y:
            y_up = jnp.where(row == rows - 1, 0.0, y_up)
            y_down = jnp.where(row == 0, 0.0, y_down)
        z_up = jnp.where(end_z, 0.0, up_of(here, 1))
        z_down = jnp.where(start_z, 0.0, down_of(here, 1))
        side = 0.5 * (here + y_up)
        side = jnp.where(row == rows - 1, 0.0, side) if whole_y else side
        total = 3.0 * here + 0.5 * ((after + before) + (y_up + y_down) + (z_up + z_down))
        return [
            (wx, i, 0.5 * (here + after)),
            (wy, i, side),
            (wz, i, jnp.where(end_z, 0.0, 0.5 * (here + z_up))),
            (d, i, total),
            (q, i, (in_y * (OMEGA * in_x(i))) * inverse(total)),
        ]

    loop(first, last, body, width)


def neighbours(v, wx, wy, wz, i):
    here = v[i]
    side_y, side_z = wy[i], wz[i]
    along_x = wx[i] * v[i + 1] + wx[i - 1] * v[i - 1]
    along_y = side_y * up_of(here, 0) + down_of(side_y * here, 0)
    along_z = side_z * up_of(here, 1) + down_of(side_z * here, 1)
    return here, along_x + along_y + along_z


def sweep(v, out, b, wx, wy, wz, q, first, last, width):
    def body(i):
        here, total = neighbours(v, wx, wy, wz, i)
        return [(out, i, (0.2 * here + b[i]) + q[i] * total)]

    loop(first, last, body, width)


def defect(v, source, wx, wy, wz, d, i):
    here, total = neighbours(v, wx, wy, wz, i)
    return (source[i] - d[i] * here) + total


def lanes(cells, k):
    return cells[:, LANES * k : LANES * k + LANES]


def keep(scratch, j, cells):
    for k in range(cells.shape[1] // LANES):
        scratch[j, k] = lanes(cells, k)


def halve_rows(scratch, j, start, count):
    parts = [
        scratch[j, k, pl.ds(start, count, stride=2), :] + scratch[j, k, pl.ds(start + 1, count, stride=2), :]
        for k in range(scratch.shape[1])
    ]
    return jnp.concatenate(parts, axis=1)


def double_rows(scratch, j, cells, start):
    for k in range(scratch.shape[1]):
        for odd in range(2):
            scratch[j, k, pl.ds(start + odd, cells.shape[0], stride=2), :] = lanes(cells, k)


def doubled(scratch, j):
    return [scratch[j, k] for k in range(scratch.shape[1])]


def call(kernel, out_shape, scratch, limit, in_specs=None, out_specs=None, flops=1000000, bytes_accessed=1000000):
    extra = {}
    if in_specs is not None:
        extra["in_specs"] = in_specs
    if out_specs is not None:
        extra["out_specs"] = out_specs
    return pl.pallas_call(
        kernel,
        out_shape=out_shape,
        scratch_shapes=scratch,
        compiler_params=pltpu.CompilerParams(vmem_limit_bytes=limit * MIB),
        cost_estimate=pl.CostEstimate(flops=flops, bytes_accessed=bytes_accessed, transcendentals=0),
        **extra,
    )


def struct(*shape):
    return jax.ShapeDtypeStruct(shape, F32)


def vmem(*shape):
    return pltpu.VMEM(shape, F32)


WHOLE = pl.BlockSpec(memory_space=pltpu.VMEM)
FAR = pl.BlockSpec(memory_space=pl.ANY)
FAR_COUNT = 26


def start_copies(sources, targets, sems, first):
    copies = [
        pltpu.make_async_copy(source, target, sems.at[first + k])
        for k, (source, target) in enumerate(zip(sources, targets))
    ]
    for copy in copies:
        copy.start()
    return copies


def wait_copies(copies):
    for copy in copies:
        copy.wait()


def place_of(i):
    row, cell = 8 * ((i // 2) % 2), Z1 * (i % 2)
    return 5 + i // 4, slice(row, row + 8), slice(cell, cell + Z1)


def begin_kernel(c_ref, g_ref, next_ref, previous_ref, c1_ref, pairs):
    for i in range(8):
        keep(pairs, i, c_ref[2 * i] + c_ref[2 * i + 1])
    for i in range(3):
        next_ref[i] = c_ref[13 + i]
        previous_ref[i] = c_ref[i]
    for i in range(2):
        next_ref[3 + i] = g_ref[14 + i]
        previous_ref[3 + i] = g_ref[i]
    rows = jnp.concatenate([halve_rows(pairs, i, 0, 8) for i in range(8)], axis=0)
    small = 0.125 * split_dot(rows, pair_deal_matrix(Z0, Z1))
    for i in range(8):
        block = small[8 * i : 8 * i + 8]
        c1_ref[i] = block
        next_ref[place_of(i)] = block
        previous_ref[place_of(i)] = block


def begin(coefficient, right_side):
    return call(
        begin_kernel, [struct(7, 16, Z0), struct(7, 16, Z0), struct(8, 8, Z1)], [vmem(8, Z0 // LANES, 16, LANES)], 8
    )(coefficient, right_side)


def deal_kernel(c_ref, g_ref, c_out, g_out, pick_out):
    pick = deal_matrix(Z0)
    pick_out[...] = pick
    for ref, out in ((c_ref, c_out), (g_ref, g_out)):
        out[...] = split_dot(ref[...].reshape(256, Z0), pick).reshape(16, 16, Z0)


def deal(coefficient, right_side):
    pick = jax.ShapeDtypeStruct((Z0, Z0), BF16)
    return call(deal_kernel, [struct(16, 16, Z0), struct(16, 16, Z0), pick], [], 8)(coefficient, right_side)


def edge_kernel(
    count_x, pick_ref, c_ref, g_ref, c1_ref, low_raw, high_raw, top_ref, bottom_ref, low_ref, high_ref
):
    pick = pick_ref[...]
    for raw, out in ((low_raw, low_ref), (high_raw, high_ref)):
        out[0:5] = split_dot(raw[0:5].reshape(80, Z0), pick).reshape(5, 16, Z0)
        out[5:7] = raw[5:7]
    place = lax.axis_index("gx")
    first = jnp.where(place > 0, 1.0, 0.0).astype(F32)
    last = jnp.where(place < count_x - 1, 1.0, 0.0).astype(F32)
    row = iota((8, Z0), 0)

    def c_part(i, half):
        rows = slice(8 * half, 8 * half + 8)
        if i < 3:
            return low_ref[i, rows, :] * first
        return c_ref[i - 3, rows, :] if i < 19 else high_ref[i - 19, rows, :] * last

    def g_part(i, half):
        rows = slice(8 * half, 8 * half + 8)
        if i < 3:
            return low_ref[i + 2, rows, :] * first
        return g_ref[i - 3, rows, :] if i < 19 else high_ref[i - 16, rows, :] * last

    for j in range(X0 // 2):
        top_ref[j] = jnp.where(row < 4, pltpu.roll(c_part(2 * j, 1), 4, 0), c_part(2 * j + 1, 1))
        bottom_ref[j] = jnp.where(row < 4, c_part(2 * j, 0), pltpu.roll(c_part(2 * j + 1, 0), 4, 0))
    for j in range(5):
        top, bottom = g_part(1 + 4 * j, 1), g_part(1 + 4 * j, 0)
        top = pltpu.roll(top, 2, 0)
        for k in range(1, 4):
            part = g_part(1 + 4 * j + k, 1)
            part = pltpu.roll(part, (2 * k + 2) % 8, 0) if k < 3 else part
            top = jnp.where(row // 2 == k, part, top)
            bottom = jnp.where(row // 2 == k, pltpu.roll(g_part(1 + 4 * j + k, 0), 2 * k, 0), bottom)
        top_ref[C_TILES + j] = top
        bottom_ref[C_TILES + j] = bottom
    for i in range(24):
        part = low_ref[place_of(i)] * first if i < 8 else c1_ref[i - 8] if i < 16 else high_ref[place_of(i - 16)] * last
        for ref in (top_ref, bottom_ref):
            ref[CG_TILES + i // 2, :, Z1 * (i % 2) : Z1 * (i % 2) + Z1] = part


def edges_y(count_x, *operands):
    return call(
        functools.partial(edge_kernel, count_x), [struct(CG_TILES + 12, 8, Z0)] * 2 + [struct(7, 16, Z0)] * 2, [], 8
    )(*operands)


def ends(axis, count):
    place = lax.axis_index(axis)
    low = jnp.where(place > 0, 1.0, 0.0).astype(F32)
    return low, jnp.where(place < count - 1, 1.0, 0.0).astype(F32)


def window0(low_ref, high_ref, below_ref, above_ref, c_ref, g_ref, first, last, low_y, high_y):
    row = iota((8, Z0), 0) < 4

    def put(own, below, above):
        head, tail = pltpu.roll(own[0:8], 4, 0), pltpu.roll(own[8:16], 4, 0)
        parts = [jnp.where(row, below, head), jnp.where(row, head, tail), jnp.where(row, tail, above)]
        return jnp.concatenate(parts, axis=0)

    def turn(cells, rows):
        return pltpu.roll(cells, rows % 8, 0) if rows % 8 else cells

    def c_slab(i, own):
        odd = i % 2
        below = turn(below_ref[i // 2], 4 * odd) * low_y
        return put(own, below, turn(above_ref[i // 2], 4 - 4 * odd) * high_y)

    def g_slab(i, own):
        tile, k = C_TILES + (i - 1) // 4, (i - 1) % 4
        below = turn(below_ref[tile], 2 - 2 * k) * low_y
        return put(own, below, turn(above_ref[tile], 4 - 2 * k) * high_y)

    def fill(c, g):
        for i in range(3):
            c[i] = c_slab(i, low_ref[i] * first)
            c[19 + i] = c_slab(19 + i, high_ref[i] * last)
        for i in range(3, 19):
            c[i] = c_slab(i, c_ref[i - 3])
        for i in (1, 2):
            g[i] = g_slab(i, low_ref[i + 2] * first)
            g[18 + i] = g_slab(18 + i, high_ref[i + 2] * last)
        for i in range(3, 19):
            g[i] = g_slab(i, g_ref[i - 3])

    return fill


def down0_kernel(
    count_x, count_y,
    c_ref, g_ref, low_ref, high_ref, below_ref, above_ref,
    g1_ref, v_own_ref, c, g, wx, wy, wz, d, q, b, v, pairs,
):
    place_x, place_y = lax.axis_index("gx"), lax.axis_index("gy")
    sides = ends("gx", count_x) + ends("gy", count_y)
    window0(low_ref, high_ref, below_ref, above_ref, c_ref, g_ref, *sides)(c, g)
    in_y = inside((Y0, Z0), 0, place_y * 16 - OY0, 16 * count_y).astype(F32)
    make_faces(
        c, wx, wy, wz, d, q, 1, X0 - 1, lambda i: flag(place_x * 16 - OX0 + i, 16 * count_x), in_y, 4
    )

    def begin(i):
        return [(b, i, q[i] * g[i])]

    loop(1, X0 - 1, begin, 5)
    sweep(b, v, b, wx, wy, wz, q, 2, X0 - 2, 6)

    def own_of(i):
        return [(v_own_ref, i, pltpu.roll(v[i + 3], Y0 - OY0, 0)[0:16])]

    loop(0, 16, own_of, 2)

    def restrict(j):
        i = 2 * j + OX0
        both = defect(v, g, wx, wy, wz, d, i) + defect(v, g, wx, wy, wz, d, i + 1)
        return [(pairs, (j, k), lanes(both, k)) for k in range(Z0 // LANES)]

    loop(0, 8, restrict, 4)
    rows = jnp.concatenate([halve_rows(pairs, i, 4, 8) for i in range(8)], axis=0)
    g1_ref[...] = (0.5 * pair_sums(rows)).reshape(8, 8, Z1)


def down0(count_x, count_y, *operands):
    frame = (X0, Y0, Z0)
    return call(
        functools.partial(down0_kernel, count_x, count_y),
        [struct(8, 8, Z1), struct(16, 16, Z0)],
        [vmem(*frame)] * 9 + [vmem(8, Z0 // LANES, Y0, LANES)],
        18,
    )(*operands)


def fill_c1(c1, c1_ref, low_ref, high_ref, below_ref, above_ref, first, last, low_y, high_y):
    for i in range(24):
        at = CG_TILES + i // 2, slice(0, 8), slice(Z1 * (i % 2), Z1 * (i % 2) + Z1)
        part = low_ref[place_of(i)] * first if i < 8 else c1_ref[i - 8] if i < 16 else high_ref[place_of(i - 16)] * last
        c1[i, 0:8, :] = below_ref[at] * low_y
        c1[i, 8:16, :] = part
        c1[i, 16:24, :] = above_ref[at] * high_y


def prepare_kernel(
    count_x, count_y, c1_ref, low_ref, high_ref, below_ref, above_ref,
    wx1, wy1, wz1, d1, q1, wx2, wy2, wz2, d2, q2, c3_ref, c1, c2, pairs,
):
    place_x, place_y = lax.axis_index("gx"), lax.axis_index("gy")
    sides = ends("gx", count_x) + ends("gy", count_y)
    fill_c1(c1, c1_ref, low_ref, high_ref, below_ref, above_ref, *sides)
    in_y = inside((Y1, Z1), 0, place_y * 8 - OY1, 8 * count_y).astype(F32)
    make_faces(
        c1, wx1, wy1, wz1, d1, q1, 2, X1 - 2, lambda i: flag(place_x * 8 - OX1 + i, 8 * count_x), in_y, 5
    )
    for i in range(12):
        keep(pairs, i, c1[2 * i] + c1[2 * i + 1])
    blank = jnp.zeros((4, Z1), F32)
    rows = []
    for i in range(12):
        rows.append(halve_rows(pairs, i, 0, 12))
        rows.append(blank)
    c2[...] = (0.125 * pair_sums(jnp.concatenate(rows, axis=0))).reshape(X2, Y2, Z2)
    in_y = inside((Y2, Z2), 0, place_y * 4 - OY2, 4 * count_y).astype(F32)
    make_faces(
        c2, wx2, wy2, wz2, d2, q2, 1, X2 - 1, lambda i: flag(place_x * 4 - OX2 + i, 4 * count_x), in_y, 10
    )
    rows = jnp.concatenate([c2[4] + c2[5], c2[6] + c2[7]], axis=0)
    thin = 0.125 * split_dot(rows, pair_sum_matrix(Z2, LANES, 64))
    row = iota((8, LANES), 0)
    c3 = jnp.zeros((8, LANES), F32)
    for i in range(2):
        for j in range(2):
            at = 16 * i + 4 + 2 * j
            both = thin[at : at + 1] + thin[at + 1 : at + 2]
            c3 = jnp.where(row == 2 * i + j, jnp.broadcast_to(both, (8, LANES)), c3)
    c3_ref[...] = c3


def prepare(count_x, count_y, *operands):
    frame1, frame2 = (X1, Y1, Z1), (X2, Y2, Z2)
    return call(
        functools.partial(prepare_kernel, count_x, count_y),
        [struct(*frame1)] * 5 + [struct(*frame2)] * 5 + [struct(8, LANES)],
        [vmem(*frame1), vmem(*frame2), vmem(12, Z1 // LANES, Y1, LANES)],
        8,
    )(*operands)


def fill_g1(g1, mid_ref, below_ref, above_ref, low_y, high_y):
    g1[2:22, 0:8, :] = below_ref[...] * low_y
    g1[2:22, 8:16, :] = mid_ref[...]
    g1[2:22, 16:24, :] = above_ref[...] * high_y


def down1_kernel(
    count_x, count_y, mid_ref, below_ref, above_ref,
    wx1, wy1, wz1, d1, q1, wx2, wy2, wz2, d2, q2, c3_ref,
    v_far, send2_ref, send3_ref, v1_ref, b1_ref, g1, g2, b2, v2, pairs, thin,
):
    place_y = lax.axis_index("gy")
    low_y = jnp.where(place_y > 0, 1.0, 0.0).astype(F32)
    high_y = jnp.where(place_y < count_y - 1, 1.0, 0.0).astype(F32)
    fill_g1(g1, mid_ref, below_ref, above_ref, low_y, high_y)

    def begin1(i):
        return [(b1_ref, i, q1[i] * g1[i])]

    loop(2, X1 - 2, begin1, 10)
    sweep(b1_ref, v1_ref, b1_ref, wx1, wy1, wz1, q1, 3, X1 - 3, 9)

    def restrict(j):
        i = 2 * j + 4
        after = defect(v1_ref, g1, wx1, wy1, wz1, d1, i + 1)
        both = defect(v1_ref, g1, wx1, wy1, wz1, d1, i) + after
        return [(pairs, (j, k), lanes(both, k)) for k in range(Z1 // LANES)]

    loop(0, 8, restrict, 4)
    rows = jnp.concatenate([halve_rows(pairs, i, 4, 8) for i in range(8)], axis=0)
    small = 0.5 * pair_sums(rows)
    g2[...] = jnp.zeros((X2, Y2, Z2), F32)
    for i in range(8):
        g2[2 + i, 2:10, :] = small[8 * i : 8 * i + 8]
    for i in range(2, X2 - 2):
        b2[i] = q2[i] * g2[i]
    sweep(b2, v2, b2, wx2, wy2, wz2, q2, 3, X2 - 3, 6)
    row = iota((8, Z2), 0) < 4
    for i in range(4):
        both = jnp.where(row, pltpu.roll(v2[4 + i, 0:8, :], 4, 0), g2[4 + i, 0:8, :])
        send2_ref[:, LANES * i : LANES * i + LANES] = both
    halves = [
        defect(v2, g2, wx2, wy2, wz2, d2, 4 + 2 * i) + defect(v2, g2, wx2, wy2, wz2, d2, 5 + 2 * i)
        for i in range(2)
    ]
    thin[...] = 0.5 * split_dot(jnp.concatenate(halves, axis=0), pair_sum_matrix(Z2, LANES))
    row = iota((8, LANES), 0)
    source = jnp.zeros((8, LANES), F32)
    for i in range(2):
        for j in range(2):
            at = 16 * i + 4 + 2 * j
            both = thin[at : at + 1, :] + thin[at + 1 : at + 2, :]
            source = jnp.where(row == 2 * i + j, jnp.broadcast_to(both, (8, LANES)), source)
    source = source + c3_ref[...]
    double = jnp.where(row < 4, source, pltpu.roll(source, 4, 0))
    for i in range(count_x * count_y // 2):
        send3_ref[8 * i : 8 * i + 8, :] = double
    v_far[...] = v1_ref[4:20]


def down1(count_x, count_y, *operands):
    frame1, frame2 = (X1, Y1, Z1), (X2, Y2, Z2)
    return call(
        functools.partial(down1_kernel, count_x, count_y),
        [struct(16, Y1, Z1), struct(8, Z0)]
        + [struct(4 * count_x * count_y, LANES)],
        [vmem(*frame1)] * 3 + [vmem(*frame2)] * 3 + [vmem(8, Z1 // LANES, Y1, LANES), vmem(32, LANES)],
        8,
    )(*operands)


def iterate_side_kernel(own_ref, own2_ref, next_ref, previous_ref):
    for i in range(3):
        for half in range(2):
            next_ref[2 * i + half] = own_ref[13 + i, 8 * half : 8 * half + 8, :]
            previous_ref[2 * i + half] = own_ref[i, 8 * half : 8 * half + 8, :]
    next_ref[6] = own2_ref[...]
    previous_ref[6] = own2_ref[...]


def iterate_sides(*operands):
    return call(iterate_side_kernel, [struct(7, 8, Z0), struct(7, 8, Z0)], [], 8)(*operands)


def iterate_edge_kernel(count_x, own_ref, own2_ref, low_ref, high_ref, top_ref, bottom_ref):
    place = lax.axis_index("gx")
    first = jnp.where(place > 0, 1.0, 0.0).astype(F32)
    last = jnp.where(place < count_x - 1, 1.0, 0.0).astype(F32)
    row = iota((8, Z0), 0) < 4

    def slab(i, half):
        if i < 3:
            return low_ref[2 * i + half] * first
        if i < 19:
            return own_ref[i - 3, 8 * half : 8 * half + 8, :]
        return high_ref[2 * (i - 19) + half] * last

    for j in range(X0 // 2):
        top_ref[j] = jnp.where(row, pltpu.roll(slab(2 * j, 1), 4, 0), slab(2 * j + 1, 1))
        bottom_ref[j] = jnp.where(row, slab(2 * j, 0), pltpu.roll(slab(2 * j + 1, 0), 4, 0))
    for ref in (top_ref, bottom_ref):
        ref[11] = low_ref[6] * first
        ref[12] = own2_ref[...]
        ref[13] = high_ref[6] * last


def iterate_edges(count_x, *operands):
    return call(
        functools.partial(iterate_edge_kernel, count_x), [struct(14, 8, Z0), struct(14, 8, Z0)], [], 8
    )(*operands)


def weights0_kernel(
    count_x, count_y, c_ref, g_ref, low0, high0, below0, above0, *rest,
):
    stored, (c, g, wx, wy, wz, d, q, b, sems) = rest[:6], rest[6:]
    place_x, place_y = lax.axis_index("gx"), lax.axis_index("gy")
    sides = ends("gx", count_x) + ends("gy", count_y)
    window0(low0, high0, below0, above0, c_ref, g_ref, *sides)(c, g)
    in_y = inside((Y0, Z0), 0, place_y * 16 - OY0, 16 * count_y).astype(F32)
    make_faces(
        c, wx, wy, wz, d, q, 1, X0 - 1, lambda i: flag(place_x * 16 - OX0 + i, 16 * count_x), in_y, 2
    )
    copies = start_copies((wx, wy, wz, d, q), stored[:5], sems, 0)

    def begin(i):
        return [(b, i, q[i] * g[i])]

    loop(1, X0 - 1, begin, 2)
    copies += start_copies((b,), stored[5:], sems, 5)
    wait_copies(copies)


def weights0(count_x, count_y, *operands):
    frame0 = (X0, Y0, Z0)
    return call(
        functools.partial(weights0_kernel, count_x, count_y),
        [struct(*frame0)] * 6,
        [vmem(*frame0)] * 8 + [pltpu.SemaphoreType.DMA((6,))],
        60,
        in_specs=[WHOLE] * 6,
        out_specs=[FAR] * 6,
        flops=20000000,
        bytes_accessed=20000000,
    )(*operands)


def join_halves(frame, count):
    first = iota(frame.shape[1:], 1) < 64
    frame[0] = jnp.where(first, 0.0, pltpu.roll(frame[count], 64, 1))
    frame[count + 1] = jnp.where(first, pltpu.roll(frame[1], 64, 1), 0.0)


def halves_matrix(of_fine):
    fine, coarse = iota((LANES, LANES), of_fine), iota((LANES, LANES), 1 - of_fine)
    hit = jnp.logical_and(fine // 64 == coarse // 64, (fine % 64) // 2 == coarse % 64)
    return hit.astype(F32).astype(BF16)


def solve_coarse(
    count_x, count_y, all_ref, v3,
    c3, wx3, wy3, wz3, d3, q3, b3, w3, thin3,
    c4, wx4, wy4, wz4, d4, q4, g4, v4, thin4,
):
    h3, h4 = count_x, count_x // 2

    if 2 * count_y < Y3:
        c3[...] = jnp.zeros(c3.shape, F32)
        b3[...] = jnp.zeros(b3.shape, F32)
    first = iota((count_y, LANES), 1) < 64
    for i in range(h3):
        for j in range(2):
            parts = []
            for x in (i, i + h3):
                base = (x // 2) * count_y * 4 + 2 * (x % 2)
                parts.append(all_ref[pl.ds(base + j, count_y, stride=4), :])
            rows = pl.ds(j, count_y, stride=2)
            b3[1 + i, rows, :] = jnp.where(first, parts[0], pltpu.roll(parts[1], 64, 1))
            c3[1 + i, rows, :] = jnp.where(first, pltpu.roll(parts[0], 64, 1), parts[1])
    join_halves(c3, h3)
    in_y = (iota((Y3, LANES), 0) < 2 * count_y).astype(F32)
    make_faces(c3, wx3, wy3, wz3, d3, q3, 1, h3 + 1, lambda i: 1.0, in_y, min(8, h3), whole_y=1, period=64)

    def begin3(i):
        return [(v3, i, q3[i] * b3[i])]

    loop(1, h3 + 1, begin3, h3)
    join_halves(v3, h3)

    def sweep3(i):
        here, total = neighbours(v3, wx3, wy3, wz3, i)
        return [(w3, i, 0.2 * here + q3[i] * (b3[i] + total))]

    loop(1, h3 + 1, sweep3, h3)
    join_halves(w3, h3)

    def restrict3(j):
        i = 2 * j + 1
        both = defect(w3, b3, wx3, wy3, wz3, d3, i) + defect(w3, b3, wx3, wy3, wz3, d3, i + 1)
        return [(thin3, j, both), (thin3, h4 + j, c3[i] + c3[i + 1])]

    loop(0, h4, restrict3, min(4, h4))
    rows = jnp.concatenate(
        [thin3[i, pl.ds(0, Y4, stride=2), :] + thin3[i, pl.ds(1, Y4, stride=2), :] for i in range(2 * h4)], axis=0
    )
    both = split_dot(rows, halves_matrix(0)).reshape(2 * h4, Y4, LANES)
    g4[...] = 0.5 * both[:h4]
    c4[1 : h4 + 1] = 0.125 * both[h4:]
    join_halves(c4, h4)
    in_y = jnp.logical_and(iota((Y4, LANES), 0) < count_y, iota((Y4, LANES), 1) % 64 < 32).astype(F32)
    make_faces(c4, wx4, wy4, wz4, d4, q4, 1, h4 + 1, lambda i: 1.0, in_y, h4, whole_y=1, period=64)

    along_x = [wx4[i] for i in range(h4 + 1)]
    along_y, along_z = [wy4[1 + i] for i in range(h4)], [wz4[1 + i] for i in range(h4)]
    scale = [q4[1 + i] for i in range(h4)]
    start = [scale[i] * g4[i] for i in range(h4)]
    first = iota((Y4, LANES), 1) < 64

    def bottom(step, v):
        before = jnp.where(first, 0.0, pltpu.roll(v[-1], 64, 1))
        after = jnp.where(first, pltpu.roll(v[0], 64, 1), 0.0)
        padded = (before, *v, after)
        out = []
        for i, here in enumerate(v):
            total = along_x[i + 1] * padded[i + 2] + along_x[i] * padded[i]
            total += along_y[i] * up_of(here, 0) + down_of(along_y[i] * here, 0)
            total += along_z[i] * up_of(here, 1) + down_of(along_z[i] * here, 1)
            out.append((0.2 * here + start[i]) + scale[i] * total)
        return tuple(out)

    final = lax.fori_loop(0, BOTTOM - 1, bottom, tuple(start))

    wide = split_dot(jnp.concatenate(final, axis=0), halves_matrix(1)).reshape(h4, Y4, LANES)
    for i in range(h4):
        thin4[i, pl.ds(0, Y4, stride=2), :] = wide[i]
        thin4[i, pl.ds(1, Y4, stride=2), :] = wide[i]
    for i in range(h4):
        extra = thin4[i]
        v3[1 + 2 * i] = w3[1 + 2 * i] + extra
        v3[2 + 2 * i] = w3[2 + 2 * i] + extra
    join_halves(v3, h3)
    loop(1, h3 + 1, sweep3, h3)
    join_halves(w3, h3)

    def sweep3_again(i):
        here, total = neighbours(w3, wx3, wy3, wz3, i)
        return [(v3, i, 0.2 * here + q3[i] * (b3[i] + total))]

    loop(1, h3 + 1, sweep3_again, h3)


def up_kernel(
    count_x, count_y,
    all_ref, *rest,
):
    far, rest = rest[:FAR_COUNT], rest[FAR_COUNT:]
    solution_far, residual_far = rest[:2]
    near, rest = rest[2 : 2 + FAR_COUNT], rest[2 + FAR_COUNT :]
    grids, rest = rest[:19], rest[19:]
    v2, w2, b2, v1, b1, c1, wx1, wy1, wz1, d1, q1, w1, spread1 = rest[:13]
    v0, w0, spread0, solution_ref, residual_ref, sems = rest[13:]
    (wx2, wy2, wz2, q2, own2, low_ref, high_ref, below_ref, above_ref,
     g1_mid, g1_below, g1_above, c1_ref, low0, high0, below0, above0, v1_ref, v_own,
     wx0, wy0, wz0, q0, b0, d0, g_ref) = near
    copies = start_copies(far, near, sems, 0)
    v3 = grids[0]
    solve_coarse(count_x, count_y, all_ref, *grids)
    wait_copies(copies[:19])
    place_x, place_y = lax.axis_index("gx"), lax.axis_index("gy")
    n3, h3 = 2 * count_x, count_x
    sides = ends("gx", count_x) + ends("gy", count_y)
    first, last, low_y, high_y = sides

    fill_c1(c1, c1_ref, low0, high0, below0, above0, *sides)
    fill_g1(w1, g1_mid, g1_below, g1_above, low_y, high_y)
    in_y = inside((Y1, Z1), 0, place_y * 8 - OY1, 8 * count_y).astype(F32)
    make_faces(
        c1, wx1, wy1, wz1, d1, q1, 5, X1 - 5, lambda i: flag(place_x * 8 - OX1 + i, 8 * count_x), in_y, 7
    )

    def begin1(i):
        return [(b1, i, q1[i] * w1[i])]

    loop(5, X1 - 5, begin1, 7)

    slabs = []
    for j in range(6):
        at = 2 * place_x - 2 + j
        cells = v3[1 + jnp.clip(at - jnp.where(at < h3, 0, h3), 0, h3 - 1)]
        slabs.append(cells * flag(at, h3) + pltpu.roll(cells, 64, 1) * flag(at - h3, h3))
    wide = split_dot(jnp.concatenate(slabs, axis=0), copy_matrix(LANES, LANES))
    target, origin = iota((Y2, Y3), 0), iota((Y2, Y3), 1)
    rows = jnp.logical_and(origin == 2 * place_y - 2 + target // 2, target < 12).astype(F32).astype(BF16)
    half = iota((8, Z2), 0) < 4
    wide = jnp.concatenate([wide[Y3 * j : Y3 * j + Y3] for j in range(6)], axis=1)
    wide = split_dot_left(rows, wide)
    for j in range(6):
        extra = lanes(wide, j)
        for k in range(2):
            i = 2 * j + k
            at = slice(LANES * (i % 4), LANES * (i % 4) + LANES)
            mid = own2[:, at] if i // 4 == 1 else low_ref[6, :, at] * first if i < 4 else high_ref[6, :, at] * last
            below = below_ref[11 + i // 4, :, at] * low_y
            above = above_ref[11 + i // 4, :, at] * high_y
            v2[i, 0:8] = jnp.where(half, below, pltpu.roll(mid, 4, 0)) + extra[0:8]
            v2[i, 8:16] = jnp.where(half, above, 0.0) + extra[8:16]
            b2[i, 0:8] = jnp.where(half, pltpu.roll(below, 4, 0), mid)
            b2[i, 8:16] = jnp.where(half, pltpu.roll(above, 4, 0), 0.0)
    for i in range(1, X2 - 1):
        b2[i] = q2[i] * b2[i]
    sweep(v2, w2, b2, wx2, wy2, wz2, q2, 1, X2 - 1, 10)
    sweep(w2, v2, b2, wx2, wy2, wz2, q2, 2, X2 - 2, 8)

    spread1[...] = jnp.zeros(spread1.shape, F32)
    for j in range(8):
        double_rows(spread1, j, v2[2 + j, 2:10], 4)
    for j in range(8):
        extra = doubled(spread1, j)
        extra = jnp.concatenate([extra[0], extra[0]], axis=1)
        for k in range(2):
            i = 4 + 2 * j + k
            v1[i] = v1_ref[i - 4] + extra
    sweep(v1, w1, b1, wx1, wy1, wz1, q1, 5, X1 - 5, 7)
    sweep(w1, v1, b1, wx1, wy1, wz1, q1, 6, X1 - 6, 6)

    half = iota((8, Z0), 0) < 4
    wait_copies(copies[19:])
    for j in range(12):
        double_rows(spread0, j, v1[6 + j, 6:18], 0)
    for j in range(12):
        extra = doubled(spread0, j)
        extra = jnp.concatenate([extra[k // 2] for k in range(Z0 // LANES)], axis=1)
        for k in range(2):
            i = 2 * j - 1 + k
            if i < 0 or i >= X0:
                continue
            if i < 3:
                own = [low_ref[2 * i + side] * first for side in range(2)]
            elif i < 19:
                own = [v_own[i - 3, 8 * side : 8 * side + 8, :] for side in range(2)]
            else:
                own = [high_ref[2 * (i - 19) + side] * last for side in range(2)]
            below, above = below_ref[i // 2] * low_y, above_ref[i // 2] * high_y
            if i % 2:
                below = pltpu.roll(below, 4, 0)
            else:
                above = pltpu.roll(above, 4, 0)
            head, tail = pltpu.roll(own[0], 4, 0), pltpu.roll(own[1], 4, 0)
            v0[i, 0:8] = jnp.where(half, below, head) + extra[0:8]
            v0[i, 8:16] = jnp.where(half, head, tail) + extra[8:16]
            v0[i, 16:24] = jnp.where(half, tail, above) + extra[16:24]
    sweep(v0, w0, b0, wx0, wy0, wz0, q0, 1, X0 - 1, 5)
    sweep(w0, v0, b0, wx0, wy0, wz0, q0, 2, X0 - 2, 6)

    pick = collect_matrix(Z0)
    rows = jnp.concatenate([pltpu.roll(v0[i + OX0], Y0 - OY0, 0)[0:16] for i in range(16)], axis=0)
    solution_ref[...] = split_dot(rows, pick).reshape(16, 16, Z0)
    copies = start_copies((solution_ref,), (solution_far,), sems, FAR_COUNT)

    def finish(i):
        here, total = neighbours(v0, wx0, wy0, wz0, i + OX0)
        return [(residual_ref, i, pltpu.roll(total - d0[i + OX0] * here, Y0 - OY0, 0)[0:16])]

    loop(0, 16, finish, 8)
    for part in range(2):
        here = pl.ds(8 * part, 8)
        rows = residual_ref[here].reshape(128, Z0)
        residual_ref[here] = g_ref[here] + split_dot(rows, pick).reshape(8, 16, Z0)
        copies += start_copies((residual_ref.at[here],), (residual_far.at[here],), sems, FAR_COUNT + 1 + part)
    wait_copies(copies)


def up(count_x, count_y, everything, *operands):
    frame0, frame1, frame2 = (X0, Y0, Z0), (X1, Y1, Z1), (X2, Y2, Z2)
    frame3, frame4 = (count_x + 2, Y3, LANES), (count_x // 2 + 2, Y4, LANES)
    return call(
        functools.partial(up_kernel, count_x, count_y),
        [struct(16, 16, Z0), struct(16, 16, Z0)],
        [vmem(*operand.shape) for operand in operands]
        + [vmem(*frame3)] * 9 + [vmem(count_x, Y3, LANES)]
        + [vmem(*frame4)] * 6 + [vmem(count_x // 2, Y4, LANES), vmem(*frame4), vmem(count_x // 2, Y3, LANES)]
        + [vmem(*frame2)] * 3 + [vmem(*frame1)] * 9 + [vmem(8, 1, Y1, LANES)]
        + [vmem(*frame0)] * 2 + [vmem(12, Z1 // LANES, Y0, LANES)] + [vmem(16, 16, Z0)] * 2
        + [pltpu.SemaphoreType.DMA((FAR_COUNT + 3,))],
        60,
        in_specs=[WHOLE] + [FAR] * FAR_COUNT,
        out_specs=[FAR] * 2,
    )(everything, *operands)


def to_next(cells, axis):
    count = lax.axis_size(axis)
    return lax.ppermute(cells, axis, [(i, (i + 1) % count) for i in range(count)])


def to_previous(cells, axis):
    count = lax.axis_size(axis)
    return lax.ppermute(cells, axis, [((i + 1) % count, i) for i in range(count)])


def shards(right_side, coefficient):
    count_x, count_y = lax.axis_size("gx"), lax.axis_size("gy")
    place_x = lax.axis_index("gx")

    def with_sides(low, cells, high):
        low = jnp.where(place_x > 0, low, 0.0)
        high = jnp.where(place_x < count_x - 1, high, 0.0)
        return jnp.concatenate([low, cells, high], axis=0)

    to_right, to_left, c1 = begin(coefficient, right_side)
    low, high = to_next(to_right, "gx"), to_previous(to_left, "gx")
    c_own, g_own, pick = deal(coefficient, right_side)
    top, bottom, low, high = edges_y(count_x, pick, c_own, g_own, c1, low, high)
    below, above = to_next(top, "gy"), to_previous(bottom, "gy")
    g1, v_own = down0(count_x, count_y, c_own, g_own, low, high, below, above)

    g1_low, g1_high = to_next(g1[2:8], "gx"), to_previous(g1[0:6], "gx")
    levels = prepare(count_x, count_y, c1, low, high, below, above)
    wx2, wy2, wz2, q2 = levels[5], levels[6], levels[7], levels[9]
    g1_mid = with_sides(g1_low, g1, g1_high)
    g1_below, g1_above = to_next(g1_mid, "gy"), to_previous(g1_mid, "gy")
    v1, own2, send3 = down1(count_x, count_y, g1_mid, g1_below, g1_above, *levels)

    everything = lax.all_to_all(send3, ("gx", "gy"), split_axis=0, concat_axis=0, tiled=True)
    to_right, to_left = iterate_sides(v_own, own2)
    low2, high2 = to_next(to_right, "gx"), to_previous(to_left, "gx")
    top, bottom = iterate_edges(count_x, v_own, own2, low2, high2)
    below2, above2 = to_next(top, "gy"), to_previous(bottom, "gy")
    c_own, send3 = lax.optimization_barrier((c_own, send3))
    weights = weights0(count_x, count_y, c_own, g_own, low, high, below, above)
    wx0, wy0, wz0, d0, q0, b0 = weights
    return tuple(
        up(
            count_x, count_y, everything, wx2, wy2, wz2, q2, own2, low2, high2, below2, above2,
            g1_mid, g1_below, g1_above, c1, low, high, below, above, v1, v_own,
            wx0, wy0, wz0, q0, b0, d0, right_side,
        )
    )


def solution(mesh):
    specs = (P("gx", "gy", None), P("gx", "gy", None))
    return jax.shard_map(shards, mesh=mesh, in_specs=specs, out_specs=specs, check_vma=False)
```
